32 devices in a mesh: batch: 4 (over y, x), tensor: 8 (over z, core).
Axes of the slice: x: 2, y: 2, z: 4, core: 2. Of those that a mesh axis runs over, the one named last changes fastest.
Arguments:
- tokens: bfloat16 [8, 1024, 2048], P('batch', 'tensor'), may hold values from -6 to 6
- cotangent: bfloat16 [8, 1024, 2048], P('batch', 'tensor'), may hold values from -6 to 6
- segment_ids: int32 [8, 1024], P('batch'), may hold values from 0 to 3, as said below
- prefix_lengths: int32 [8, 4], P('batch'), may hold values from 1 to 1021, as said below
- rotary_positions: int32 [8, 1024], P('batch'), may hold values from 0 to 1023, as said below
- residual_scale: float32 [1], replicated, may hold values from 1.2 to 2
- qkv_weight: bfloat16 [2048, 3, 2048], P(None, None, 'tensor'), may hold values from -0.125 to 0.125
- qkv_bias: float32 [3, 2048], P(None, 'tensor'), may hold values from -0.625 to 0.625
- out_weight: bfloat16 [2048, 2048], P('tensor'), may hold values from -1 to 1
- out_bias: float32 [2048], replicated, may hold values from -1.25 to 1.25
- norm_gain: float32 [2048], replicated, may hold values from 0.5 to 1.5
- norm_shift: float32 [2048], replicated, may hold values from -1.25 to 1.25
- gate_weight: bfloat16 [2048, 5504], P(None, 'tensor'), may hold values from -0.125 to 0.125
- gate_bias: float32 [5504], P('tensor'), may hold values from -1.75 to 1.75
- up_weight: bfloat16 [2048, 5504], P(None, 'tensor'), may hold values from -0.125 to 0.125
- up_bias: float32 [5504], P('tensor'), may hold values from -1.75 to 1.75
- down_weight: bfloat16 [5504, 2048], P('tensor'), may hold values from -0.078125 to 0.078125
- down_bias: float32 [2048], replicated, may hold values from -1.25 to 1.25
- final_gain: float32 [2048], replicated, may hold values from 0.5 to 1.5
- final_shift: float32 [2048], replicated, may hold values from -1.25 to 1.25
Outputs:
- block_output: bfloat16 [8, 1024, 2048], P('batch', 'tensor')
- tokens_grad: float32 [8, 1024, 2048], P('batch', 'tensor')
- qkv_weight_grad: float32 [2048, 3, 2048], P(None, None, 'tensor')
- qkv_bias_grad: float32 [3, 2048], P(None, 'tensor')
- out_weight_grad: float32 [2048, 2048], P('tensor')
- out_bias_grad: float32 [2048], replicated
- norm_gain_grad: float32 [2048], replicated
- norm_shift_grad: float32 [2048], replicated
- gate_weight_grad: float32 [2048, 5504], P(None, 'tensor')
- gate_bias_grad: float32 [5504], P('tensor')
- up_weight_grad: float32 [2048, 5504], P(None, 'tensor')
- up_bias_grad: float32 [5504], P('tensor')
- down_weight_grad: float32 [5504, 2048], P('tensor')
- down_bias_grad: float32 [2048], replicated
- final_gain_grad: float32 [2048], replicated
- final_shift_grad: float32 [2048], replicated
The draws below stay inside these ranges and needn't reach their ends.
Inputs may be any that keep to these rules, and one draw needn't show every extreme that they name: `segment_ids`: along each pack the ids never fall, and each of 0 to 3 appears. prefix_lengths[p, s] lies between 1 and the number of positions of segment s in pack p. `rotary_positions`: within a segment the positions rise by one from each position to the next.
All inputs are finite; a program needn't handle non-finite values.
Results may differ from the reference program's by a relative error of at most 0.019.
Values may be sent and summed in bfloat16 or wider, within the bound.
No kernel may reach another device: no remote copies, remote signals or barrier semaphores. Data moves between devices by JAX's collectives and lax.ppermute only.
A program may use at most 256 MiB of HBM per device.

```python
import math
import jax
import jax.numpy as jnp
from jax import lax

D = 2048
HEADS = 16
FF_LIVE = 5461
FF = 5504
LEN = 1024
SEGS = 4
HEAD_DIM = 128
PACKS = 8
SHORT_MAX = 32


def pack_layout(key):
    key = jax.random.fold_in(key, 101)
    long_key, short_key, pick_key = jax.random.split(key, 3)
    long_slot = jax.random.randint(long_key, (PACKS, 1), 0, SEGS)
    shorts = jax.random.randint(short_key, (PACKS, SEGS), 1, SHORT_MAX + 1)
    chosen_pack = jax.random.randint(pick_key, (), 0, PACKS)
    forced_row = jnp.arange(PACKS, dtype=jnp.int32)[:, None] == chosen_pack
    shorts = jnp.where(forced_row, 1, shorts)
    seg_slots = jnp.arange(SEGS, dtype=jnp.int32)[None, :]
    is_long = seg_slots == long_slot
    short_total = jnp.sum(jnp.where(is_long, 0, shorts), axis=1, keepdims=True)
    lengths = jnp.where(is_long, LEN - short_total, shorts)
    seg_ends = jnp.cumsum(lengths, axis=1)
    ordinal = jnp.arange(LEN, dtype=jnp.int32)[None, :, None]
    segment = jnp.sum((ordinal >= seg_ends[:, None, :]).astype(jnp.int32), axis=2)
    return (lengths, segment, is_long, seg_slots, long_slot, forced_row)


def draw_segment_ids(key, part):
    lengths, segment, is_long, seg_slots, long_slot, forced_row = pack_layout(key)
    return segment.astype(jnp.int32)


def draw_prefix_lengths(key, part):
    lengths, segment, is_long, seg_slots, long_slot, forced_row = pack_layout(key)
    key = jax.random.fold_in(key, 7)
    raw_values = jax.random.randint(key, (PACKS, SEGS), 0, 1 << 20)
    drawn = 1 + raw_values % lengths
    return jnp.where(is_long & forced_row, lengths, drawn).astype(jnp.int32)


def draw_rotary_positions(key, part):
    lengths, segment, is_long, seg_slots, long_slot, forced_row = pack_layout(key)
    key = jax.random.fold_in(key, 11)
    begins = jax.random.randint(key, (PACKS, SEGS), 0, LEN - SHORT_MAX + 1)
    follow = seg_slots == (long_slot + 1) % SEGS
    begins = jnp.where(is_long, LEN - lengths, jnp.where(follow, 0, begins))
    starts = jnp.cumsum(lengths, axis=1) - lengths
    member = segment[:, :, None] == seg_slots[:, None, :]
    offset = jnp.arange(LEN, dtype=jnp.int32)[None, :] - jnp.sum(jnp.where(member, starts[:, None, :], 0), axis=2)
    return (offset + jnp.sum(jnp.where(member, begins[:, None, :], 0), axis=2)).astype(jnp.int32)


def steps_of(key, shape, pieces, low, top_value):
    def one(axis_at, shards_of):
        heights = jax.random.uniform(jax.random.fold_in(jax.random.fold_in(key, 6), axis_at), (shards_of,), jnp.float32, low / len(pieces), top_value / len(pieces))
        return jnp.repeat(jnp.exp(heights), shape[axis_at] // shards_of).reshape((-1,) + (1,) * (len(shape) - axis_at - 1))

    factor_of = one(*pieces[0])
    for cut in pieces[1:]:
        factor_of = factor_of * one(*cut)
    return factor_of


def bell_draw(stream_key, dims, scale, limit, pieces=(), kind=jnp.bfloat16):
    gain = steps_of(stream_key, dims, pieces, -0.22, 0.18) if pieces else 1.0
    values = jax.random.normal(stream_key, dims, jnp.float32) * scale * gain
    return jnp.minimum(jnp.maximum(values, -limit), limit).astype(kind)


def setup_inputs(seed: int = 0) -> dict:
    streams_of = jax.random.split(jax.random.key(seed), 21)
    tokens = bell_draw(streams_of[0], (PACKS, LEN, D), 1.0, 6.0, ((0, 4), (1, 8)))
    cotangent = bell_draw(streams_of[1], (PACKS, LEN, D), 1.0, 6.0, ((0, 4), (1, 8)))
    segment_ids = draw_segment_ids(jax.random.fold_in(streams_of[20], 71), 0)
    prefix_lengths = draw_prefix_lengths(jax.random.fold_in(streams_of[20], 71), 0)
    rotary_positions = draw_rotary_positions(jax.random.fold_in(streams_of[20], 71), 0)
    residual_scale = jnp.clip(jax.random.uniform(streams_of[5], (1,), jnp.float32, 1.2, 2.0), 1.2, 2.0)
    qkv_weight = bell_draw(streams_of[6], (D, 3, D), D ** -0.5, 0.125, ((2, 8),))
    qkv_bias = bell_draw(streams_of[7], (3, D), 0.1, 0.625, ((1, 8),), jnp.float32)
    out_weight = bell_draw(streams_of[8], (D, D), (D // 64) ** -0.5, 1.0, ((0, 8),))
    out_bias = bell_draw(streams_of[9], (D,), 0.2, 1.25, (), jnp.float32)
    norm_gain = jnp.clip(1.0 + 0.1 * jax.random.normal(streams_of[10], (D,), jnp.float32), 0.5, 1.5)
    norm_shift = bell_draw(streams_of[11], (D,), 0.2, 1.25, (), jnp.float32)
    gate_weight = bell_draw(streams_of[12], (D, FF), D ** -0.5, 0.125, ((1, 8),))
    gate_bias = bell_draw(streams_of[13], (FF,), 0.3, 1.75, ((0, 8),), jnp.float32)
    up_weight = bell_draw(streams_of[14], (D, FF), D ** -0.5, 0.125, ((1, 8),))
    up_bias = bell_draw(streams_of[15], (FF,), 0.3, 1.75, ((0, 8),), jnp.float32)
    down_weight = bell_draw(streams_of[16], (FF, D), FF ** -0.5, 0.078125, ((0, 8),))
    down_bias = bell_draw(streams_of[17], (D,), 0.2, 1.25, (), jnp.float32)
    final_gain = jnp.clip(1.0 + 0.1 * jax.random.normal(streams_of[18], (D,), jnp.float32), 0.5, 1.5)
    final_shift = bell_draw(streams_of[19], (D,), 0.2, 1.25, (), jnp.float32)
    return {"tokens": tokens, "cotangent": cotangent, "segment_ids": segment_ids, "prefix_lengths": prefix_lengths, "rotary_positions": rotary_positions, "residual_scale": residual_scale, "qkv_weight": qkv_weight, "qkv_bias": qkv_bias, "out_weight": out_weight, "out_bias": out_bias, "norm_gain": norm_gain, "norm_shift": norm_shift, "gate_weight": gate_weight, "gate_bias": gate_bias, "up_weight": up_weight, "up_bias": up_bias, "down_weight": down_weight, "down_bias": down_bias, "final_gain": final_gain, "final_shift": final_shift}


EPSILON = 1e-05
NEG_FILL = -1e+30
ROPE_BASE = 10000.0
GELU_ROOT = math.sqrt(2.0 / math.pi)
GELU_CUBIC = 0.044715

@jax.custom_vjp
def low(v):
    return lax.optimization_barrier(v.astype(jnp.bfloat16)).astype(jnp.float32)

@jax.custom_vjp
def low_back(v):
    return v

def low_keep(v):
    return (low(v), None)

def low_pass(kept, grad):
    return (grad,)

def back_keep(v):
    return (v, None)

def back_low(kept, grad):
    return (low(grad),)
low.defvjp(low_keep, low_pass)
low_back.defvjp(back_keep, back_low)

def highest(left_side, right_side):
    return jnp.dot(left_side, right_side, precision=lax.Precision.HIGHEST, preferred_element_type=jnp.float32)

def gelu_value(values):
    return 0.5 * values * (1.0 + jnp.tanh(GELU_ROOT * (values + GELU_CUBIC * values * values * values)))

def layer_norm(values, gain_vector, shift_vector):
    average = lax.optimization_barrier(jnp.mean(values, axis=-1, keepdims=True))
    centred = values - average
    spread = lax.optimization_barrier(jnp.mean(centred * centred, axis=-1, keepdims=True))
    return centred * lax.rsqrt(spread + EPSILON) * gain_vector + shift_vector

def rotary_tables(positions):
    half_dim = HEAD_DIM // 2
    frequency = jnp.exp(jnp.arange(half_dim, dtype=jnp.float32) * (-2.0 * math.log(ROPE_BASE) / HEAD_DIM))
    angles = positions.astype(jnp.float32)[:, None] * frequency[None, :]
    angles = jnp.concatenate([angles, angles], axis=-1)
    return (jnp.cos(angles), jnp.sin(angles))

def rotate_heads(values, cosine, sine_table):
    half_dim = values.shape[-1] // 2
    turned = jnp.concatenate([-values[..., half_dim:], values[..., :half_dim]], axis=-1)
    return values * cosine + turned * sine_table

def attend_mask(segment, prefix):
    seg_slots = jnp.arange(SEGS, dtype=jnp.int32)
    member = (segment[:, None] == seg_slots[None, :]).astype(jnp.int32)
    counts = lax.optimization_barrier(jnp.sum(member, axis=0))
    starts = jnp.cumsum(counts) - counts
    ordinal = jnp.arange(segment.shape[0], dtype=jnp.int32)
    offset = ordinal - lax.optimization_barrier(jnp.sum(member * starts[None, :], axis=1))
    in_prefix = offset < lax.optimization_barrier(jnp.sum(member * prefix[None, :], axis=1))
    same_doc = segment[:, None] == segment[None, :]
    return same_doc & (in_prefix[None, :] | (ordinal[None, :] <= ordinal[:, None]))

def head_attention(query_rows, key_rows, value_rows, allowed):
    scores = low_back(highest(query_rows, key_rows.T) * (1.0 / math.sqrt(HEAD_DIM)))
    scores = jnp.where(allowed, scores, NEG_FILL)
    row_top = lax.optimization_barrier(jnp.max(scores, axis=-1, keepdims=True))
    shifted = jnp.exp(scores - row_top)
    attention_probs = low(shifted / lax.optimization_barrier(jnp.sum(shifted, axis=-1, keepdims=True)))
    return highest(attention_probs, value_rows)

def layer_forward(tokens_in, weights, scale_value, allowed, cosine, sine_table, live_cols):
    qkv_w, qkv_b, out_w, out_b, norm_g, norm_s, gate_w, gate_b, up_w, up_b, down_w, down_b, final_g, final_s = weights
    projected = low_back(highest(tokens_in, qkv_w.reshape(D, 3 * D))).reshape(LEN, 3, HEADS, HEAD_DIM)
    projected = projected + qkv_b.reshape(1, 3, HEADS, HEAD_DIM)
    cos_heads = cosine[:, None, :]
    sin_heads = sine_table[:, None, :]
    queries = low(rotate_heads(projected[:, 0], cos_heads, sin_heads))
    keys_rot = low(rotate_heads(projected[:, 1], cos_heads, sin_heads))
    values_in = low(projected[:, 2])

    def one_head(triple):
        return head_attention(triple[0], triple[1], triple[2], allowed)
    contexts = lax.map(jax.checkpoint(one_head), (jnp.moveaxis(queries, 1, 0), jnp.moveaxis(keys_rot, 1, 0), jnp.moveaxis(values_in, 1, 0)))
    context = low(low_back(jnp.moveaxis(contexts, 0, 1).reshape(LEN, D)))
    attended = low_back(highest(context, out_w)) + out_b
    normed = layer_norm(scale_value * tokens_in + attended, norm_g, norm_s)
    hidden = low(normed)
    gate_pre = low_back(highest(hidden, gate_w * live_cols[None, :])) + gate_b * live_cols
    up_pre = low_back(highest(hidden, up_w * live_cols[None, :])) + up_b * live_cols
    activated = low(gelu_value(gate_pre) * up_pre)
    branch = low_back(highest(activated, down_w * live_cols[:, None])) + down_b
    return layer_norm(scale_value * normed + branch, final_g, final_s)

def reference(tokens, cotangent, segment_ids, prefix_lengths, rotary_positions, residual_scale, qkv_weight, qkv_bias, out_weight, out_bias, norm_gain, norm_shift, gate_weight, gate_bias, up_weight, up_bias, down_weight, down_bias, final_gain, final_shift):
    live_cols = (jnp.arange(FF, dtype=jnp.int32) < FF_LIVE).astype(jnp.float32)
    params = (qkv_weight.astype(jnp.float32), qkv_bias, out_weight.astype(jnp.float32), out_bias, norm_gain, norm_shift, gate_weight.astype(jnp.float32), gate_bias, up_weight.astype(jnp.float32), up_bias, down_weight.astype(jnp.float32), down_bias, final_gain, final_shift)
    scale_value = residual_scale[0]

    def per_pack(totals, pack_items):
        pack_tokens, pack_cot, pack_segments, pack_prefix, pack_positions = pack_items
        allowed = attend_mask(pack_segments, pack_prefix)
        cosine, sine_table = rotary_tables(pack_positions)

        def forward(tokens_in, weights):
            return layer_forward(tokens_in, weights, scale_value, allowed, cosine, sine_table, live_cols)
        result, pullback = jax.vjp(forward, pack_tokens.astype(jnp.float32), params)
        input_grad, weight_grads = pullback(pack_cot.astype(jnp.float32))
        totals = jax.tree.map(lambda running, addend: running + addend, totals, weight_grads)
        return (totals, (result.astype(jnp.bfloat16), input_grad))
    start_totals = jax.tree.map(jnp.zeros_like, params)
    totals, outputs = lax.scan(per_pack, start_totals, (tokens, cotangent, segment_ids, prefix_lengths, rotary_positions))
    return (outputs[0], outputs[1], totals[0], totals[1], totals[2], totals[3], totals[4], totals[5], totals[6], totals[7], totals[8], totals[9], totals[10], totals[11], totals[12], totals[13])
```

```python
import functools
import math

import jax
import jax.numpy as jnp
from jax import lax
from jax.experimental import pallas as pl
from jax.experimental.pallas import tpu as pltpu
from jax.sharding import PartitionSpec as P

FF_LIVE = 5461
SEGS = 4
HEAD_DIM = 128

EPSILON = 1e-05
NEG_FILL = -1e30
ROPE_BASE = 10000.0
GELU_ROOT = math.sqrt(2.0 / math.pi)
GELU_CUBIC = 0.044715
FACTOR = 1.0 / math.sqrt(HEAD_DIM)
QUERY_TILE = 256
ROW_TILE = 256
VMEM_LIMIT = 56 * 1024 * 1024
BF16 = jnp.bfloat16
F32 = jnp.float32


def dot_nn(a, b):
    return lax.dot_general(a, b, (((1,), (0,)), ((), ())), preferred_element_type=F32)


def dot_nt(a, b):
    return lax.dot_general(a, b, (((1,), (1,)), ((), ())), preferred_element_type=F32)


def dot_tn(a, b):
    return lax.dot_general(a, b, (((0,), (0,)), ((), ())), preferred_element_type=F32)


def attend_forward_kernel(
    x_ref, w_ref, b_ref, cos_ref, sin_ref, lo_ref, hi_ref, qkv_ref, ctx_ref, lse_ref
):
    step = pl.program_id(0)
    heads = ctx_ref.shape[1] // HEAD_DIM
    tile = x_ref.shape[0]
    rows = pl.ds(pl.multiple_of(step * tile, tile), tile)
    x = x_ref[...]
    cosine = cos_ref[rows, :]
    sine = sin_ref[rows, :]
    for part in range(3):
        projected = dot_nn(x, w_ref[part]) + b_ref[part]
        for head in range(heads):
            value = projected[:, head * HEAD_DIM : (head + 1) * HEAD_DIM]
            if part < 2:
                value = value * cosine + pltpu.roll(value, HEAD_DIM // 2, 1) * sine
            qkv_ref[part * heads + head, rows, :] = value.astype(BF16)

    @pl.when(step == pl.num_programs(0) - 1)
    def _():
        length = qkv_ref.shape[1]
        for head in range(heads):
            keys = qkv_ref[heads + head]
            values_t = qkv_ref[2 * heads + head].T

            def one_tile(index, carry):
                first = pl.multiple_of(index * QUERY_TILE, QUERY_TILE)
                queries = qkv_ref[head, pl.ds(first, QUERY_TILE), :]
                scores = dot_nt(keys, queries)
                place = lax.broadcasted_iota(jnp.int32, (length, QUERY_TILE), 0)
                seen = (place >= lo_ref[index]) & (place <= hi_ref[index])
                scores = jnp.where(seen, scores, NEG_FILL)
                top = jnp.max(scores, axis=0, keepdims=True)
                shifted = jnp.exp((scores - top) * FACTOR)
                total = jnp.sum(shifted, axis=0, keepdims=True)
                probs = (shifted * (1.0 / total)).astype(BF16)
                context_t = dot_nn(values_t, probs)
                ctx_ref[pl.ds(first, QUERY_TILE), head * HEAD_DIM : (head + 1) * HEAD_DIM] = (
                    context_t.T.astype(BF16)
                )
                lse_ref[head, index] = top * FACTOR + jnp.log(total)
                return carry

            lax.fori_loop(0, length // QUERY_TILE, one_tile, 0)


def attend_forward(x, w, b, cosine, sine, lo, hi):
    length, width = x.shape
    head_width = w.shape[2]
    heads = head_width // HEAD_DIM
    tiles = length // QUERY_TILE
    whole = lambda *shape: pl.BlockSpec(shape, lambda i: (0,) * len(shape))
    return pl.pallas_call(
        attend_forward_kernel,
        grid=(length // ROW_TILE,),
        in_specs=[
            pl.BlockSpec((ROW_TILE, width), lambda i: (i, 0)),
            whole(3, width, head_width),
            whole(3, 1, head_width),
            whole(length, HEAD_DIM),
            whole(length, HEAD_DIM),
            whole(tiles, 1, QUERY_TILE),
            whole(tiles, 1, QUERY_TILE),
        ],
        out_specs=[
            whole(3 * heads, length, HEAD_DIM),
            whole(length, head_width),
            whole(heads, tiles, 1, QUERY_TILE),
        ],
        out_shape=[
            jax.ShapeDtypeStruct((3 * heads, length, HEAD_DIM), BF16),
            jax.ShapeDtypeStruct((length, head_width), BF16),
            jax.ShapeDtypeStruct((heads, tiles, 1, QUERY_TILE), F32),
        ],
        compiler_params=pltpu.CompilerParams(vmem_limit_bytes=VMEM_LIMIT),
        cost_estimate=pl.CostEstimate(
            flops=2 * length * width * 3 * head_width + 8 * heads * length * length * HEAD_DIM,
            bytes_accessed=2 * (length * width + 3 * width * head_width),
            transcendentals=heads * length * length,
        ),
        name="attend_forward",
    )(x, w, b, cosine, sine, lo, hi)


def attend_backward_kernel(
    qkv_ref,
    grad_ref,
    lse_ref,
    lo_ref,
    hi_ref,
    cos_ref,
    sin_ref,
    w_ref,
    low_ref,
    bias_ref,
    x_grad_ref,
    key_total,
    value_total,
):
    step = pl.program_id(0)
    length = qkv_ref.shape[1]
    heads = qkv_ref.shape[0] // 3
    tile = x_grad_ref.shape[0]

    def rope_back(grad, cosine, sine):
        return grad * cosine - pltpu.roll(grad, HEAD_DIM // 2, 1) * sine

    @pl.when(step == 0)
    def _():
        for head in range(heads):
            lanes = slice(head * HEAD_DIM, (head + 1) * HEAD_DIM)
            keys = qkv_ref[heads + head]
            keys_t = keys.T
            values = qkv_ref[2 * heads + head]
            key_total[...] = jnp.zeros_like(key_total)
            value_total[...] = jnp.zeros_like(value_total)

            def one_tile(index, query_bias):
                first = pl.multiple_of(index * QUERY_TILE, QUERY_TILE)
                rows = pl.ds(first, QUERY_TILE)
                queries = qkv_ref[head, rows, :]
                grads = grad_ref[rows, lanes]
                scores = dot_nt(keys, queries)
                place = lax.broadcasted_iota(jnp.int32, (length, QUERY_TILE), 0)
                seen = (place >= lo_ref[index]) & (place <= hi_ref[index])
                scores = jnp.where(seen, scores * FACTOR, NEG_FILL)
                probs = jnp.exp(scores - lse_ref[head, index])
                probs_grad = dot_nt(values, grads)
                delta = jnp.sum(probs * probs_grad, axis=0, keepdims=True)
                score_grad = (probs * (probs_grad - delta)).astype(BF16)
                query_grad = dot_nn(keys_t, score_grad).T * FACTOR
                key_total[...] += dot_nn(score_grad, queries)
                value_total[...] += dot_nn(probs.astype(BF16), grads)
                query_grad = rope_back(query_grad, cos_ref[rows, :], sin_ref[rows, :])
                low_ref[0, rows, lanes] = query_grad.astype(BF16)
                return query_bias + jnp.sum(query_grad, axis=0, keepdims=True)

            query_bias = lax.fori_loop(
                0, length // QUERY_TILE, one_tile, jnp.zeros((1, HEAD_DIM), F32)
            )
            key_grad = rope_back(key_total[...] * FACTOR, cos_ref[...], sin_ref[...])
            value_grad = value_total[...]
            low_ref[1, :, lanes] = key_grad.astype(BF16)
            low_ref[2, :, lanes] = value_grad.astype(BF16)
            bias_ref[0, :, lanes] = query_bias
            bias_ref[1, :, lanes] = jnp.sum(key_grad, axis=0, keepdims=True)
            bias_ref[2, :, lanes] = jnp.sum(value_grad, axis=0, keepdims=True)

    rows = pl.ds(pl.multiple_of(step * tile, tile), tile)
    total = dot_nt(low_ref[0, rows, :], w_ref[0])
    total += dot_nt(low_ref[1, rows, :], w_ref[1])
    total += dot_nt(low_ref[2, rows, :], w_ref[2])
    x_grad_ref[...] = total.astype(BF16)


def attend_backward(qkv, grad, lse, lo, hi, cosine, sine, w):
    width, head_width = w.shape[1:]
    length = grad.shape[0]
    heads = head_width // HEAD_DIM
    tiles = length // QUERY_TILE
    whole = lambda *shape: pl.BlockSpec(shape, lambda i: (0,) * len(shape))
    return pl.pallas_call(
        attend_backward_kernel,
        grid=(length // ROW_TILE,),
        in_specs=[
            whole(3 * heads, length, HEAD_DIM),
            whole(length, head_width),
            whole(heads, tiles, 1, QUERY_TILE),
            whole(tiles, 1, QUERY_TILE),
            whole(tiles, 1, QUERY_TILE),
            whole(length, HEAD_DIM),
            whole(length, HEAD_DIM),
            whole(3, width, head_width),
        ],
        out_specs=[
            whole(3, length, head_width),
            whole(3, 1, head_width),
            pl.BlockSpec((ROW_TILE, width), lambda i: (i, 0)),
        ],
        out_shape=[
            jax.ShapeDtypeStruct((3, length, head_width), BF16),
            jax.ShapeDtypeStruct((3, 1, head_width), F32),
            jax.ShapeDtypeStruct((length, width), BF16),
        ],
        scratch_shapes=[
            pltpu.VMEM((length, HEAD_DIM), F32),
            pltpu.VMEM((length, HEAD_DIM), F32),
        ],
        compiler_params=pltpu.CompilerParams(vmem_limit_bytes=VMEM_LIMIT),
        cost_estimate=pl.CostEstimate(
            flops=2 * length * width * 3 * head_width + 20 * heads * length * length * HEAD_DIM,
            bytes_accessed=2 * (length * width + 3 * width * head_width),
            transcendentals=heads * length * length,
        ),
        name="attend_backward",
    )(qkv, grad, lse, lo, hi, cosine, sine, w)


def glu_forward_kernel(
    live_ref, h_ref, wg_ref, wu_ref, wd_ref, bg_ref, bu_ref, act_ref, gelu_ref, slope_ref, out_ref
):
    hidden = h_ref[...]
    gate = dot_nt(wg_ref[...], hidden) + bg_ref[...]
    up = dot_nt(wu_ref[...], hidden) + bu_ref[...]
    squared = gate * gate
    tangent = jnp.tanh(GELU_ROOT * gate * (1.0 + GELU_CUBIC * squared))
    half = 0.5 * (1.0 + tangent)
    gelu = gate * half
    slope = half + 0.5 * gate * (1.0 - tangent * tangent) * GELU_ROOT * (
        1.0 + 3.0 * GELU_CUBIC * squared
    )
    column = lax.broadcasted_iota(jnp.int32, gate.shape, 0)
    activated = jnp.where(column < live_ref[0], gelu * up, 0.0).astype(BF16)
    act_ref[...] = activated
    gelu_ref[...] = gelu.astype(BF16)
    slope_ref[...] = (up * slope).astype(BF16)
    out_ref[...] = dot_tn(activated, wd_ref[...]).astype(BF16)


def glu_forward(live, hidden, wg, wu, wd, bg, bu):
    length, width = hidden.shape
    columns = wg.shape[0]
    whole = lambda *shape: pl.BlockSpec(shape, lambda i: (0,) * len(shape))
    tall = pl.BlockSpec((columns, ROW_TILE), lambda i: (0, i))
    wide = pl.BlockSpec((ROW_TILE, width), lambda i: (i, 0))
    return pl.pallas_call(
        glu_forward_kernel,
        grid=(length // ROW_TILE,),
        in_specs=[pl.BlockSpec(memory_space=pltpu.SMEM), wide]
        + [whole(columns, width)] * 3
        + [whole(columns, 1)] * 2,
        out_specs=[tall, tall, tall, wide],
        out_shape=[jax.ShapeDtypeStruct((columns, length), BF16)] * 3
        + [jax.ShapeDtypeStruct((length, width), BF16)],
        compiler_params=pltpu.CompilerParams(vmem_limit_bytes=VMEM_LIMIT),
        cost_estimate=pl.CostEstimate(
            flops=6 * length * width * columns,
            bytes_accessed=2 * (2 * length * width + 3 * columns * (width + length)),
            transcendentals=length * columns,
        ),
        name="glu_forward",
    )(live, hidden, wg, wu, wd, bg, bu)


def glu_backward_kernel(
    live_ref,
    g_ref,
    wg_ref,
    wu_ref,
    wd_ref,
    gelu_ref,
    slope_ref,
    gate_ref,
    up_ref,
    gate_bias_ref,
    up_bias_ref,
    out_ref,
):
    @pl.when(pl.program_id(0) == 0)
    def _():
        gate_bias_ref[...] = jnp.zeros_like(gate_bias_ref)
        up_bias_ref[...] = jnp.zeros_like(up_bias_ref)

    grad = dot_nt(wd_ref[...], g_ref[...])
    column = lax.broadcasted_iota(jnp.int32, grad.shape, 0)
    grad = jnp.where(column < live_ref[0], grad, 0.0)
    gate_grad = grad * slope_ref[...].astype(F32)
    up_grad = grad * gelu_ref[...].astype(F32)
    gate_bias_ref[...] += jnp.sum(gate_grad, axis=1, keepdims=True)
    up_bias_ref[...] += jnp.sum(up_grad, axis=1, keepdims=True)
    gate_low = gate_grad.astype(BF16)
    up_low = up_grad.astype(BF16)
    gate_ref[...] = gate_low
    up_ref[...] = up_low
    out_ref[...] = (dot_tn(gate_low, wg_ref[...]) + dot_tn(up_low, wu_ref[...])).astype(BF16)


def glu_backward(live, grad, wg, wu, wd, gelu, slope):
    length, width = grad.shape
    columns = wg.shape[0]
    whole = lambda *shape: pl.BlockSpec(shape, lambda i: (0,) * len(shape))
    tall = pl.BlockSpec((columns, ROW_TILE), lambda i: (0, i))
    wide = pl.BlockSpec((ROW_TILE, width), lambda i: (i, 0))
    return pl.pallas_call(
        glu_backward_kernel,
        grid=(length // ROW_TILE,),
        in_specs=[pl.BlockSpec(memory_space=pltpu.SMEM), wide]
        + [whole(columns, width)] * 3
        + [tall, tall],
        out_specs=[tall, tall, whole(columns, 1), whole(columns, 1), wide],
        out_shape=[jax.ShapeDtypeStruct((columns, length), BF16)] * 2
        + [jax.ShapeDtypeStruct((columns, 1), F32)] * 2
        + [jax.ShapeDtypeStruct((length, width), BF16)],
        compiler_params=pltpu.CompilerParams(vmem_limit_bytes=VMEM_LIMIT),
        cost_estimate=pl.CostEstimate(
            flops=6 * length * width * columns,
            bytes_accessed=2 * (2 * length * width + 3 * columns * (width + length)),
            transcendentals=0,
        ),
        name="glu_backward",
    )(live, grad, wg, wu, wd, gelu, slope)


def weight_grad_kernel(packs, outs, *refs):
    lefts = refs[: packs * outs]
    rights = refs[packs * outs : packs * (outs + 1)]
    for out in range(outs):
        total = dot_nn(lefts[out][...], rights[0][...])
        for pack in range(1, packs):
            total += dot_nn(lefts[pack * outs + out][...], rights[pack][...])
        refs[packs * (outs + 1)][out] = total.astype(BF16)


def weight_grad(lefts, rights):
    packs = len(rights)
    outs = len(lefts[0])
    length, width = rights[0].shape
    columns = lefts[0][0].shape[0]
    tile = 512
    return pl.pallas_call(
        functools.partial(weight_grad_kernel, packs, outs),
        grid=(width // tile,),
        in_specs=[pl.BlockSpec((columns, length), lambda i: (0, 0))] * (packs * outs)
        + [pl.BlockSpec((length, tile), lambda i: (0, i))] * packs,
        out_specs=pl.BlockSpec((outs, columns, tile), lambda i: (0, 0, i)),
        out_shape=jax.ShapeDtypeStruct((outs, columns, width), BF16),
        compiler_params=pltpu.CompilerParams(vmem_limit_bytes=VMEM_LIMIT),
        cost_estimate=pl.CostEstimate(
            flops=2 * packs * outs * length * width * columns,
            bytes_accessed=2 * packs * length * (width + outs * columns)
            + 2 * outs * columns * width,
            transcendentals=0,
        ),
        name="weight_grad",
    )(*[left for pack in lefts for left in pack], *rights)


def add_low(a, b):
    return (a.astype(F32) + b.astype(F32)).astype(BF16)


def swap_bit(x, axis_name, bit):
    size = lax.axis_size(axis_name)
    return lax.ppermute(x, axis_name, [(i, i ^ (1 << bit)) for i in range(size)])


def scatter_bits(x, rank, bits, dim, axis_name="batch"):
    for bit in bits:
        half = x.shape[dim] // 2
        mine = (rank >> bit) & 1
        send = lax.dynamic_slice_in_dim(x, (1 - mine) * half, half, dim)
        keep = lax.dynamic_slice_in_dim(x, mine * half, half, dim)
        x = add_low(keep, swap_bit(send, axis_name, bit))
    return x


def gather_bits(x, rank, bits, dim, axis_name="batch"):
    for bit in reversed(bits):
        other = swap_bit(x, axis_name, bit)
        mine = ((rank >> bit) & 1) == 1
        x = jnp.concatenate([jnp.where(mine, other, x), jnp.where(mine, x, other)], axis=dim)
    return x


def bit_orders(size):
    count = size.bit_length() - 1
    return [[(start + k) % count for k in range(count)] for start in range(min(count, 2))]


def sum_over_batch(x, rank, size, dim):
    if size & (size - 1):
        return lax.psum(x, "batch")
    orders = bit_orders(size)
    if not orders:
        return x
    unit = 128 * size if dim == x.ndim - 1 else 16 * size
    width = x.shape[dim]
    cuts = [unit * round(width * k / len(orders) / unit) for k in range(len(orders))] + [width]
    parts = []
    for order, first, last in zip(orders, cuts[:-1], cuts[1:]):
        piece = lax.slice_in_dim(x, first, last, axis=dim)
        piece = scatter_bits(piece, rank, order, dim)
        parts.append(gather_bits(piece, rank, order, dim))
    return jnp.concatenate(parts, axis=dim)


def ring_gather(x, rank, axis_size, shift):
    up = down = x
    ups, downs = [], []
    for _ in range(axis_size - 1):
        up, down = shift(up, 1), shift(down, -1)
        ups.append(up)
        downs.append(down)
    whole = jnp.zeros((axis_size,) + x.shape, x.dtype)
    whole = lax.dynamic_update_index_in_dim(whole, x, rank, 0)
    for away in range(1, axis_size):
        block = jnp.where(rank >= away, ups[away - 1], downs[axis_size - away - 1])
        whole = lax.dynamic_update_index_in_dim(
            whole, block, lax.rem(rank - away + axis_size, axis_size), 0
        )
    return whole


def line_scatter(x, rank, axis_size, shift):
    total = lax.dynamic_index_in_dim(x, rank, 0, keepdims=False).astype(F32)
    for away in range(1, axis_size):
        for step in (away, -away):
            target = jnp.clip(rank + step, 0, axis_size - 1)
            block = lax.dynamic_index_in_dim(x, target, 0, keepdims=False)
            total = total + shift(block, step).astype(F32)
    return total.astype(BF16)


def sum_all(x, axis_name):
    size = lax.axis_size(axis_name)
    if size & (size - 1):
        return lax.psum(x, axis_name)
    for bit in range(size.bit_length() - 1):
        x = x + swap_bit(x, axis_name, bit)
    return x


def norm_forward(values, gain_vector, shift_vector):
    average = jnp.mean(values, axis=-1, keepdims=True)
    centred = values - average
    spread = jnp.mean(centred * centred, axis=-1, keepdims=True)
    inverse = lax.rsqrt(spread + EPSILON)
    normal = centred * inverse
    return (normal * gain_vector + shift_vector, normal, inverse)


def norm_backward(grad_rows, gain_vector, normal, inverse):
    scaled = grad_rows * gain_vector
    return inverse * (
        scaled
        - jnp.mean(scaled, axis=-1, keepdims=True)
        - normal * jnp.mean(scaled * normal, axis=-1, keepdims=True)
    )


def rotary_tables(positions):
    half_dim = HEAD_DIM // 2
    frequency = jnp.exp(
        jnp.arange(half_dim, dtype=F32) * (-2.0 * math.log(ROPE_BASE) / HEAD_DIM)
    )
    angles = positions.astype(F32)[..., None] * frequency
    cosine, sine = jnp.cos(angles), jnp.sin(angles)
    return (
        jnp.concatenate([cosine, cosine], axis=-1),
        jnp.concatenate([-sine, sine], axis=-1),
    )


def visible_range(segment, prefix):
    member = (segment[:, None] == jnp.arange(SEGS, dtype=jnp.int32)[None, :]).astype(jnp.int32)
    counts = jnp.sum(member, axis=0)
    starts = jnp.cumsum(counts) - counts
    ordinal = jnp.arange(segment.shape[0], dtype=jnp.int32)
    first = jnp.sum(member * starts[None, :], axis=1)
    seen = jnp.sum(member * jnp.minimum(prefix, counts)[None, :], axis=1)
    last = jnp.maximum(ordinal, first + seen - 1)
    tiled = (segment.shape[0] // QUERY_TILE, 1, QUERY_TILE)
    return first.reshape(tiled), last.reshape(tiled)


def per_device(
    batch_size,
    tensor_size,
    tokens,
    cotangent,
    segment_ids,
    prefix_lengths,
    rotary_positions,
    residual_scale,
    qkv_weight,
    qkv_bias,
    out_weight,
    out_bias,
    norm_gain,
    norm_shift,
    gate_weight,
    gate_bias,
    up_weight,
    up_bias,
    down_weight,
    down_bias,
    final_gain,
    final_shift,
):
    packs, local_rows, width = tokens.shape
    head_width = qkv_weight.shape[2]
    columns = down_weight.shape[0]
    pack_range = range(packs)
    batch_rank = lax.axis_index("batch")
    tensor_rank = lax.axis_index("tensor")
    chips = tensor_size // 2
    chip_rank = tensor_rank // 2
    core = lax.rem(tensor_rank, 2)
    orders = bit_orders(batch_size)
    scale_value = residual_scale[0]

    def shift(x, step):
        moves = [
            (chip * 2 + side, (chip + step) * 2 + side)
            for chip in range(chips)
            for side in range(2)
            if 0 <= chip + step < chips
        ]
        return lax.ppermute(x, "tensor", moves)

    gate_rows = gate_weight.T
    up_rows = up_weight.T
    qkv_slabs = jnp.transpose(qkv_weight, (1, 0, 2))
    qkv_bias_rows = qkv_bias[:, None, :]
    gate_bias_column = gate_bias[:, None]
    up_bias_column = up_bias[:, None]
    live = (FF_LIVE - tensor_rank * columns).astype(jnp.int32)[None]

    half = width // 2
    part = half // len(orders)

    def own_piece(x, side):
        pieces = []
        for index, order in enumerate(orders):
            piece = lax.dynamic_slice_in_dim(x, side * half + index * part, part, 1)
            for bit in order:
                size = piece.shape[1] // 2
                piece = lax.dynamic_slice_in_dim(piece, ((batch_rank >> bit) & 1) * size, size, 1)
            pieces.append(piece)
        return jnp.concatenate(pieces, axis=1)

    def join_pieces(x):
        size = x.shape[1] // len(orders)
        return jnp.concatenate(
            [
                gather_bits(x[:, index * size : (index + 1) * size], batch_rank, order, 1)
                for index, order in enumerate(orders)
            ],
            axis=1,
        )

    def by_core(mine, other, axis):
        first = core == 0
        return jnp.concatenate(
            [jnp.where(first, mine, other), jnp.where(first, other, mine)], axis=axis
        )

    chunk = by_core(
        own_piece(out_weight, core), swap_bit(own_piece(out_weight, 1 - core), "tensor", 0), 0
    )
    chunk = ring_gather(chunk, chip_rank, chips, shift).reshape(-1, chunk.shape[1])
    out_half = join_pieces(chunk)
    whole_out = by_core(out_half, swap_bit(out_half, "tensor", 0), 1)

    tables = [rotary_tables(rotary_positions[p]) for p in pack_range]
    ranges = [visible_range(segment_ids[p], prefix_lengths[p]) for p in pack_range]
    whole_tokens = [lax.all_gather(tokens[p], "tensor", axis=0, tiled=True) for p in pack_range]
    qkvs, log_sums, context_rows = [], [], []
    for p in pack_range:
        qkv, context, log_sum = attend_forward(
            whole_tokens[p], qkv_slabs, qkv_bias_rows, *tables[p], *ranges[p]
        )
        qkvs.append(qkv)
        log_sums.append(log_sum)
        context_rows.append(
            lax.all_to_all(context, "tensor", split_axis=0, concat_axis=1, tiled=True)
        )
    normed, normal_one, inverse_one, hidden = [], [], [], []
    for p in pack_range:
        attended = dot_nn(context_rows[p], whole_out) + out_bias
        value, normal, inverse = norm_forward(
            scale_value * tokens[p].astype(F32) + attended, norm_gain, norm_shift
        )
        normed.append(value)
        normal_one.append(normal)
        inverse_one.append(inverse)
        hidden.append(lax.all_gather(value.astype(BF16), "tensor", axis=0, tiled=True))
    activated, gelus, slopes, branches = [], [], [], []
    for p in pack_range:
        act, gelu, slope, branch = glu_forward(
            live, hidden[p], gate_rows, up_rows, down_weight, gate_bias_column, up_bias_column
        )
        activated.append(act)
        gelus.append(gelu)
        slopes.append(slope)
        branches.append(lax.psum_scatter(branch, "tensor", scatter_dimension=0, tiled=True))
    outputs, grads_two, branch_grads = [], [], []
    final_gain_part = final_shift_part = down_bias_part = 0.0
    for p in pack_range:
        rows, normal_two, inverse_two = norm_forward(
            scale_value * normed[p] + (branches[p].astype(F32) + down_bias),
            final_gain,
            final_shift,
        )
        outputs.append(rows.astype(BF16))
        grad_final = cotangent[p].astype(F32)
        final_gain_part += jnp.sum(grad_final * normal_two, axis=0)
        final_shift_part += jnp.sum(grad_final, axis=0)
        grad_two = norm_backward(grad_final, final_gain, normal_two, inverse_two)
        down_bias_part += jnp.sum(grad_two, axis=0)
        grads_two.append(grad_two)
        branch_grads.append(lax.all_gather(grad_two.astype(BF16), "tensor", axis=0, tiled=True))

    gate_lows, up_lows, normed_sums = [], [], []
    gate_bias_part = up_bias_part = 0.0
    for p in pack_range:
        gate_low, up_low, gate_sum, up_sum, normed_part = glu_backward(
            live, branch_grads[p], gate_rows, up_rows, down_weight, gelus[p], slopes[p]
        )
        gate_lows.append(gate_low)
        up_lows.append(up_low)
        gate_bias_part += gate_sum
        up_bias_part += up_sum
        normed_sums.append(lax.psum_scatter(normed_part, "tensor", scatter_dimension=0, tiled=True))
    down_part = weight_grad([[act] for act in activated], branch_grads)
    down_grad = sum_over_batch(down_part[0], batch_rank, batch_size, 1).astype(F32)
    glu_part = weight_grad(list(zip(gate_lows, up_lows)), hidden)
    glu_grad = sum_over_batch(glu_part, batch_rank, batch_size, 2).astype(F32)

    grads_one, context_grads, attended_lows = [], [], []
    norm_gain_part = norm_shift_part = out_bias_part = 0.0
    for p in pack_range:
        normed_grad = normed_sums[p].astype(F32) + scale_value * grads_two[p]
        norm_gain_part += jnp.sum(normed_grad * normal_one[p], axis=0)
        norm_shift_part += jnp.sum(normed_grad, axis=0)
        grad_one = norm_backward(normed_grad, norm_gain, normal_one[p], inverse_one[p])
        out_bias_part += jnp.sum(grad_one, axis=0)
        attended_low = grad_one.astype(BF16)
        grads_one.append(grad_one)
        attended_lows.append(attended_low)
        context_grads.append(
            lax.all_to_all(
                dot_nt(attended_low, whole_out).astype(BF16),
                "tensor",
                split_axis=1,
                concat_axis=0,
                tiled=True,
            )
        )
    input_grads, lows = [], []
    qkv_bias_part = 0.0
    for p in pack_range:
        low, bias_sum, input_part = attend_backward(
            qkvs[p], context_grads[p], log_sums[p], *ranges[p], *tables[p], qkv_slabs
        )
        lows.append(low)
        qkv_bias_part += bias_sum
        input_sum = lax.psum_scatter(input_part, "tensor", scatter_dimension=0, tiled=True)
        input_grads.append(input_sum.astype(F32) + scale_value * grads_one[p])

    out_part = sum(dot_tn(context_rows[p], attended_lows[p]) for p in pack_range).astype(BF16)
    out_sum = add_low(
        lax.dynamic_slice_in_dim(out_part, core * half, half, 1),
        swap_bit(lax.dynamic_slice_in_dim(out_part, (1 - core) * half, half, 1), "tensor", 0),
    )
    out_sum = jnp.concatenate(
        [
            scatter_bits(out_sum[:, index * part : (index + 1) * part], batch_rank, order, 1)
            for index, order in enumerate(orders)
        ],
        axis=1,
    )
    out_sum = line_scatter(
        out_sum.reshape(chips, -1, out_sum.shape[1]), chip_rank, chips, shift
    )
    own_rows = out_sum.shape[0] // 2
    mine = lax.dynamic_slice_in_dim(out_sum, core * own_rows, own_rows, 0)
    other = swap_bit(
        lax.dynamic_slice_in_dim(out_sum, (1 - core) * own_rows, own_rows, 0), "tensor", 0
    )
    out_grad = jnp.concatenate(
        [
            join_pieces(jnp.where(core == 0, mine, other)),
            join_pieces(jnp.where(core == 0, other, mine)),
        ],
        axis=1,
    ).astype(F32)

    qkv_part = sum(
        lax.dot_general(
            whole_tokens[p], lows[p], (((0,), (1,)), ((), ())), preferred_element_type=F32
        )
        for p in pack_range
    )
    qkv_part = jnp.transpose(qkv_part, (1, 0, 2)).astype(BF16)
    qkv_grad = sum_over_batch(qkv_part, batch_rank, batch_size, 1).astype(F32)

    shared = jnp.stack(
        [
            out_bias_part,
            norm_gain_part,
            norm_shift_part,
            down_bias_part,
            final_gain_part,
            final_shift_part,
        ]
    )
    shared = sum_all(sum_all(shared, "tensor"), "batch")
    glu_bias = sum_all(jnp.concatenate([gate_bias_part[:, 0], up_bias_part[:, 0]]), "batch")
    qkv_bias_grad = sum_all(qkv_bias_part[:, 0, :], "batch")
    return (
        jnp.stack(outputs),
        jnp.stack(input_grads),
        jnp.transpose(qkv_grad, (1, 0, 2)),
        qkv_bias_grad,
        out_grad,
        shared[0],
        shared[1],
        shared[2],
        glu_grad[0].T,
        glu_bias[:columns],
        glu_grad[1].T,
        glu_bias[columns:],
        down_grad,
        shared[3],
        shared[4],
        shared[5],
    )


def solution(mesh):
    return jax.shard_map(
        functools.partial(per_device, mesh.shape["batch"], mesh.shape["tensor"]),
        mesh=mesh,
        in_specs=(
            P("batch", "tensor", None),
            P("batch", "tensor", None),
            P("batch", None),
            P("batch", None),
            P("batch", None),
            P(),
            P(None, None, "tensor"),
            P(None, "tensor"),
            P("tensor", None),
            P(),
            P(),
            P(),
            P(None, "tensor"),
            P("tensor"),
            P(None, "tensor"),
            P("tensor"),
            P("tensor", None),
            P(),
            P(),
            P(),
        ),
        out_specs=(
            P("batch", "tensor", None),
            P("batch", "tensor", None),
            P(None, None, "tensor"),
            P(None, "tensor"),
            P("tensor", None),
            P(),
            P(),
            P(),
            P(None, "tensor"),
            P("tensor"),
            P(None, "tensor"),
            P("tensor"),
            P("tensor", None),
            P(),
            P(),
            P(),
        ),
        check_vma=False,
    )
```

```python
import functools
import math

import jax
import jax.numpy as jnp
from jax import lax
from jax.experimental import pallas as pl
from jax.experimental.pallas import tpu as pltpu
from jax.sharding import PartitionSpec as P

FF_LIVE = 5461
SEGS = 4
HEAD_DIM = 128

EPSILON = 1e-05
NEG_FILL = -1e30
ROPE_BASE = 10000.0
GELU_ROOT = math.sqrt(2.0 / math.pi)
GELU_CUBIC = 0.044715
FACTOR = 1.0 / math.sqrt(HEAD_DIM)
QUERY_TILE = 256
ROW_TILE = 256
VMEM_LIMIT = 56 * 1024 * 1024
LONG = pl.CostEstimate(flops=200_000_000_000, bytes_accessed=1024, transcendentals=0)
BF16 = jnp.bfloat16
F32 = jnp.float32


def dot_nn(a, b):
    return lax.dot_general(a, b, (((1,), (0,)), ((), ())), preferred_element_type=F32)


def dot_nt(a, b):
    return lax.dot_general(a, b, (((1,), (1,)), ((), ())), preferred_element_type=F32)


def dot_tn(a, b):
    return lax.dot_general(a, b, (((0,), (0,)), ((), ())), preferred_element_type=F32)


def attend_forward_kernel(
    x_ref, w_ref, b_ref, cos_ref, sin_ref, lo_ref, hi_ref, qkv_ref, ctx_ref, lse_ref
):
    step = pl.program_id(0)
    heads = ctx_ref.shape[1] // HEAD_DIM
    tile = x_ref.shape[0]
    rows = pl.ds(pl.multiple_of(step * tile, tile), tile)
    x = x_ref[...]
    cosine = cos_ref[rows, :]
    sine = sin_ref[rows, :]
    for part in range(3):
        projected = dot_nn(x, w_ref[part]) + b_ref[part]
        for head in range(heads):
            value = projected[:, head * HEAD_DIM : (head + 1) * HEAD_DIM]
            if part < 2:
                value = value * cosine + pltpu.roll(value, HEAD_DIM // 2, 1) * sine
            qkv_ref[part * heads + head, rows, :] = value.astype(BF16)

    @pl.when(step == pl.num_programs(0) - 1)
    def _():
        length = qkv_ref.shape[1]
        for head in range(heads):
            keys = qkv_ref[heads + head]
            values_t = qkv_ref[2 * heads + head].T

            def one_tile(index, carry):
                first = pl.multiple_of(index * QUERY_TILE, QUERY_TILE)
                queries = qkv_ref[head, pl.ds(first, QUERY_TILE), :]
                scores = dot_nt(keys, queries)
                place = lax.broadcasted_iota(jnp.int32, (length, QUERY_TILE), 0)
                seen = (place >= lo_ref[index]) & (place <= hi_ref[index])
                scores = jnp.where(seen, scores, NEG_FILL)
                top = jnp.max(scores, axis=0, keepdims=True)
                shifted = jnp.exp((scores - top) * FACTOR)
                total = jnp.sum(shifted, axis=0, keepdims=True)
                probs = (shifted * (1.0 / total)).astype(BF16)
                context_t = dot_nn(values_t, probs)
                ctx_ref[pl.ds(first, QUERY_TILE), head * HEAD_DIM : (head + 1) * HEAD_DIM] = (
                    context_t.T.astype(BF16)
                )
                lse_ref[head, index] = top * FACTOR + jnp.log(total)
                return carry

            lax.fori_loop(0, length // QUERY_TILE, one_tile, 0)


def attend_forward(x, w, b, cosine, sine, lo, hi):
    length, width = x.shape
    head_width = w.shape[2]
    heads = head_width // HEAD_DIM
    tiles = length // QUERY_TILE
    whole = lambda *shape: pl.BlockSpec(shape, lambda i: (0,) * len(shape))
    return pl.pallas_call(
        attend_forward_kernel,
        grid=(length // ROW_TILE,),
        in_specs=[
            pl.BlockSpec((ROW_TILE, width), lambda i: (i, 0)),
            whole(3, width, head_width),
            whole(3, 1, head_width),
            whole(length, HEAD_DIM),
            whole(length, HEAD_DIM),
            whole(tiles, 1, QUERY_TILE),
            whole(tiles, 1, QUERY_TILE),
        ],
        out_specs=[
            whole(3 * heads, length, HEAD_DIM),
            whole(length, head_width),
            whole(heads, tiles, 1, QUERY_TILE),
        ],
        out_shape=[
            jax.ShapeDtypeStruct((3 * heads, length, HEAD_DIM), BF16),
            jax.ShapeDtypeStruct((length, head_width), BF16),
            jax.ShapeDtypeStruct((heads, tiles, 1, QUERY_TILE), F32),
        ],
        compiler_params=pltpu.CompilerParams(vmem_limit_bytes=VMEM_LIMIT),
        cost_estimate=LONG,
        name="attend_forward",
    )(x, w, b, cosine, sine, lo, hi)


def attend_backward_kernel(
    qkv_ref,
    grad_ref,
    lse_ref,
    lo_ref,
    hi_ref,
    cos_ref,
    sin_ref,
    w_ref,
    low_ref,
    bias_ref,
    x_grad_ref,
    key_total,
    value_total,
):
    step = pl.program_id(0)
    length = qkv_ref.shape[1]
    heads = qkv_ref.shape[0] // 3
    tile = x_grad_ref.shape[0]

    def rope_back(grad, cosine, sine):
        return grad * cosine - pltpu.roll(grad, HEAD_DIM // 2, 1) * sine

    @pl.when(step == 0)
    def _():
        for head in range(heads):
            lanes = slice(head * HEAD_DIM, (head + 1) * HEAD_DIM)
            keys = qkv_ref[heads + head]
            keys_t = keys.T
            values = qkv_ref[2 * heads + head]
            key_total[...] = jnp.zeros_like(key_total)
            value_total[...] = jnp.zeros_like(value_total)

            def one_tile(index, query_bias):
                first = pl.multiple_of(index * QUERY_TILE, QUERY_TILE)
                rows = pl.ds(first, QUERY_TILE)
                queries = qkv_ref[head, rows, :]
                grads = grad_ref[rows, lanes]
                scores = dot_nt(keys, queries)
                place = lax.broadcasted_iota(jnp.int32, (length, QUERY_TILE), 0)
                seen = (place >= lo_ref[index]) & (place <= hi_ref[index])
                scores = jnp.where(seen, scores * FACTOR, NEG_FILL)
                probs = jnp.exp(scores - lse_ref[head, index])
                probs_grad = dot_nt(values, grads)
                delta = jnp.sum(probs * probs_grad, axis=0, keepdims=True)
                score_grad = (probs * (probs_grad - delta)).astype(BF16)
                query_grad = dot_nn(keys_t, score_grad).T * FACTOR
                key_total[...] += dot_nn(score_grad, queries)
                value_total[...] += dot_nn(probs.astype(BF16), grads)
                query_grad = rope_back(query_grad, cos_ref[rows, :], sin_ref[rows, :])
                low_ref[0, rows, lanes] = query_grad.astype(BF16)
                return query_bias + jnp.sum(query_grad, axis=0, keepdims=True)

            query_bias = lax.fori_loop(
                0, length // QUERY_TILE, one_tile, jnp.zeros((1, HEAD_DIM), F32)
            )
            key_grad = rope_back(key_total[...] * FACTOR, cos_ref[...], sin_ref[...])
            value_grad = value_total[...]
            low_ref[1, :, lanes] = key_grad.astype(BF16)
            low_ref[2, :, lanes] = value_grad.astype(BF16)
            bias_ref[0, :, lanes] = query_bias
            bias_ref[1, :, lanes] = jnp.sum(key_grad, axis=0, keepdims=True)
            bias_ref[2, :, lanes] = jnp.sum(value_grad, axis=0, keepdims=True)

    rows = pl.ds(pl.multiple_of(step * tile, tile), tile)
    total = dot_nt(low_ref[0, rows, :], w_ref[0])
    total += dot_nt(low_ref[1, rows, :], w_ref[1])
    total += dot_nt(low_ref[2, rows, :], w_ref[2])
    x_grad_ref[...] = total.astype(BF16)


def attend_backward(qkv, grad, lse, lo, hi, cosine, sine, w):
    width, head_width = w.shape[1:]
    length = grad.shape[0]
    heads = head_width // HEAD_DIM
    tiles = length // QUERY_TILE
    whole = lambda *shape: pl.BlockSpec(shape, lambda i: (0,) * len(shape))
    return pl.pallas_call(
        attend_backward_kernel,
        grid=(length // ROW_TILE,),
        in_specs=[
            whole(3 * heads, length, HEAD_DIM),
            whole(length, head_width),
            whole(heads, tiles, 1, QUERY_TILE),
            whole(tiles, 1, QUERY_TILE),
            whole(tiles, 1, QUERY_TILE),
            whole(length, HEAD_DIM),
            whole(length, HEAD_DIM),
            whole(3, width, head_width),
        ],
        out_specs=[
            whole(3, length, head_width),
            whole(3, 1, head_width),
            pl.BlockSpec((ROW_TILE, width), lambda i: (i, 0)),
        ],
        out_shape=[
            jax.ShapeDtypeStruct((3, length, head_width), BF16),
            jax.ShapeDtypeStruct((3, 1, head_width), F32),
            jax.ShapeDtypeStruct((length, width), BF16),
        ],
        scratch_shapes=[
            pltpu.VMEM((length, HEAD_DIM), F32),
            pltpu.VMEM((length, HEAD_DIM), F32),
        ],
        compiler_params=pltpu.CompilerParams(vmem_limit_bytes=VMEM_LIMIT),
        cost_estimate=LONG,
        name="attend_backward",
    )(qkv, grad, lse, lo, hi, cosine, sine, w)


def glu_forward_kernel(
    live_ref, h_ref, wg_ref, wu_ref, wd_ref, bg_ref, bu_ref, act_ref, gelu_ref, slope_ref, out_ref
):
    hidden = h_ref[...]
    gate = dot_nt(wg_ref[...], hidden) + bg_ref[...]
    up = dot_nt(wu_ref[...], hidden) + bu_ref[...]
    squared = gate * gate
    tangent = jnp.tanh(GELU_ROOT * gate * (1.0 + GELU_CUBIC * squared))
    half = 0.5 * (1.0 + tangent)
    gelu = gate * half
    slope = half + 0.5 * gate * (1.0 - tangent * tangent) * GELU_ROOT * (
        1.0 + 3.0 * GELU_CUBIC * squared
    )
    column = lax.broadcasted_iota(jnp.int32, gate.shape, 0)
    activated = jnp.where(column < live_ref[0], gelu * up, 0.0).astype(BF16)
    act_ref[...] = activated
    gelu_ref[...] = gelu.astype(BF16)
    slope_ref[...] = (up * slope).astype(BF16)
    out_ref[...] = dot_tn(activated, wd_ref[...]).astype(BF16)


def glu_forward(live, hidden, wg, wu, wd, bg, bu):
    length, width = hidden.shape
    columns = wg.shape[0]
    whole = lambda *shape: pl.BlockSpec(shape, lambda i: (0,) * len(shape))
    tall = pl.BlockSpec((columns, ROW_TILE), lambda i: (0, i))
    wide = pl.BlockSpec((ROW_TILE, width), lambda i: (i, 0))
    return pl.pallas_call(
        glu_forward_kernel,
        grid=(length // ROW_TILE,),
        in_specs=[pl.BlockSpec(memory_space=pltpu.SMEM), wide]
        + [whole(columns, width)] * 3
        + [whole(columns, 1)] * 2,
        out_specs=[tall, tall, tall, wide],
        out_shape=[jax.ShapeDtypeStruct((columns, length), BF16)] * 3
        + [jax.ShapeDtypeStruct((length, width), BF16)],
        compiler_params=pltpu.CompilerParams(vmem_limit_bytes=VMEM_LIMIT),
        cost_estimate=LONG,
        name="glu_forward",
    )(live, hidden, wg, wu, wd, bg, bu)


def glu_backward_kernel(
    live_ref,
    g_ref,
    wg_ref,
    wu_ref,
    wd_ref,
    gelu_ref,
    slope_ref,
    gate_ref,
    up_ref,
    gate_bias_ref,
    up_bias_ref,
    out_ref,
    gate_sum,
    up_sum,
):
    @pl.when(pl.program_id(0) == 0)
    def _():
        gate_sum[...] = jnp.zeros_like(gate_sum)
        up_sum[...] = jnp.zeros_like(up_sum)

    grad = dot_nt(wd_ref[...], g_ref[...])
    column = lax.broadcasted_iota(jnp.int32, grad.shape, 0)
    grad = jnp.where(column < live_ref[0], grad, 0.0)
    gate_grad = grad * slope_ref[...].astype(F32)
    up_grad = grad * gelu_ref[...].astype(F32)
    for first in range(0, grad.shape[1], 128):
        gate_sum[...] += gate_grad[:, first : first + 128]
        up_sum[...] += up_grad[:, first : first + 128]

    @pl.when(pl.program_id(0) == pl.num_programs(0) - 1)
    def _():
        gate_bias_ref[...] = jnp.sum(gate_sum[...], axis=1, keepdims=True)
        up_bias_ref[...] = jnp.sum(up_sum[...], axis=1, keepdims=True)

    gate_low = gate_grad.astype(BF16)
    up_low = up_grad.astype(BF16)
    gate_ref[...] = gate_low
    up_ref[...] = up_low
    out_ref[...] = (dot_tn(gate_low, wg_ref[...]) + dot_tn(up_low, wu_ref[...])).astype(BF16)


def glu_backward(live, grad, wg, wu, wd, gelu, slope):
    length, width = grad.shape
    columns = wg.shape[0]
    whole = lambda *shape: pl.BlockSpec(shape, lambda i: (0,) * len(shape))
    tall = pl.BlockSpec((columns, ROW_TILE), lambda i: (0, i))
    wide = pl.BlockSpec((ROW_TILE, width), lambda i: (i, 0))
    return pl.pallas_call(
        glu_backward_kernel,
        grid=(length // ROW_TILE,),
        in_specs=[pl.BlockSpec(memory_space=pltpu.SMEM), wide]
        + [whole(columns, width)] * 3
        + [tall, tall],
        out_specs=[tall, tall, whole(columns, 1), whole(columns, 1), wide],
        out_shape=[jax.ShapeDtypeStruct((columns, length), BF16)] * 2
        + [jax.ShapeDtypeStruct((columns, 1), F32)] * 2
        + [jax.ShapeDtypeStruct((length, width), BF16)],
        scratch_shapes=[pltpu.VMEM((columns, 128), F32)] * 2,
        compiler_params=pltpu.CompilerParams(vmem_limit_bytes=VMEM_LIMIT),
        cost_estimate=LONG,
        name="glu_backward",
    )(live, grad, wg, wu, wd, gelu, slope)


def weight_grad_kernel(packs, outs, blocks_ref, *refs):
    lefts = refs[: packs * outs]
    rights = refs[packs * outs : packs * (outs + 1)]
    results = refs[packs * (outs + 1) :]
    for index, result in enumerate(results):

        @pl.when(pl.program_id(0) == index)
        def _():
            for out in range(outs):
                total = dot_nn(lefts[out][...], rights[0][...])
                for pack in range(1, packs):
                    total += dot_nn(lefts[pack * outs + out][...], rights[pack][...])
                result[out] = total.astype(BF16)


def weight_grad(lefts, rights, blocks):
    packs = len(rights)
    outs = len(lefts[0])
    length, width = rights[0].shape
    columns = lefts[0][0].shape[0]
    count = blocks.shape[0]
    tile = width // count
    return pl.pallas_call(
        functools.partial(weight_grad_kernel, packs, outs),
        grid_spec=pltpu.PrefetchScalarGridSpec(
            num_scalar_prefetch=1,
            grid=(count,),
            in_specs=[pl.BlockSpec((columns, length), lambda i, at: (0, 0))] * (packs * outs)
            + [pl.BlockSpec((length, tile), lambda i, at: (0, at[i]))] * packs,
            out_specs=[pl.BlockSpec((outs, columns, tile), lambda i, at: (0, 0, 0))] * count,
        ),
        out_shape=[jax.ShapeDtypeStruct((outs, columns, tile), BF16)] * count,
        compiler_params=pltpu.CompilerParams(vmem_limit_bytes=VMEM_LIMIT),
        cost_estimate=LONG,
        name="weight_grad",
    )(blocks, *[left for pack in lefts for left in pack], *rights)


def slab_grad_kernel(packs, blocks_ref, *refs):
    results = refs[2 * packs :]
    for index, result in enumerate(results):

        @pl.when(pl.program_id(0) == index)
        def _():
            for part in range(3):
                total = dot_tn(refs[0][...], refs[packs][part])
                for pack in range(1, packs):
                    total += dot_tn(refs[pack][...], refs[packs + pack][part])
                result[part] = total.astype(BF16)


def slab_grad(lefts, rights, blocks):
    packs = len(rights)
    length, width = lefts[0].shape
    columns = rights[0].shape[2]
    count = blocks.shape[0]
    tile = width // count
    return pl.pallas_call(
        functools.partial(slab_grad_kernel, packs),
        grid_spec=pltpu.PrefetchScalarGridSpec(
            num_scalar_prefetch=1,
            grid=(count,),
            in_specs=[pl.BlockSpec((length, tile), lambda i, at: (0, at[i]))] * packs
            + [pl.BlockSpec((3, length, columns), lambda i, at: (0, 0, 0))] * packs,
            out_specs=[pl.BlockSpec((3, tile, columns), lambda i, at: (0, 0, 0))] * count,
        ),
        out_shape=[jax.ShapeDtypeStruct((3, tile, columns), BF16)] * count,
        compiler_params=pltpu.CompilerParams(vmem_limit_bytes=VMEM_LIMIT),
        cost_estimate=LONG,
        name="slab_grad",
    )(blocks, *lefts, *rights)


def row_grad_kernel(blocks_ref, left_ref, right_ref, *results):
    depth = left_ref.shape[1]
    for index, result in enumerate(results):

        @pl.when(pl.program_id(0) == index)
        def _():
            for first in range(0, depth, 512):
                result[first : first + 512, :] = dot_tn(
                    left_ref[:, first : first + 512], right_ref[...]
                ).astype(BF16)


def row_grad(left, right, blocks):
    rows, depth = left.shape
    count = blocks.shape[0]
    tile = right.shape[1] // count
    return pl.pallas_call(
        row_grad_kernel,
        grid_spec=pltpu.PrefetchScalarGridSpec(
            num_scalar_prefetch=1,
            grid=(count,),
            in_specs=[
                pl.BlockSpec((rows, depth), lambda i, at: (0, 0)),
                pl.BlockSpec((rows, tile), lambda i, at: (0, at[i])),
            ],
            out_specs=[pl.BlockSpec((depth, tile), lambda i, at: (0, 0))] * count,
        ),
        out_shape=[jax.ShapeDtypeStruct((depth, tile), BF16)] * count,
        compiler_params=pltpu.CompilerParams(vmem_limit_bytes=VMEM_LIMIT),
        cost_estimate=LONG,
        name="row_grad",
    )(blocks, left, right)


def add_low(a, b):
    return (a.astype(F32) + b.astype(F32)).astype(BF16)


def after(x, *earlier):
    return lax.optimization_barrier((x, *earlier))[0]


def swap_bit(x, axis_name, bit):
    size = lax.axis_size(axis_name)
    return lax.ppermute(x, axis_name, [(i, i ^ (1 << bit)) for i in range(size)])


class Flow:
    def __init__(self, chain):
        self.chain = chain
        self.result = None
        self.moving = None

    def step(self, *earlier):
        try:
            if self.moving is None:
                sends = next(self.chain)
                if earlier:
                    sends = [(after(x, *earlier), move) for x, move in sends]
            else:
                got = [after(x, *earlier) for x in self.moving] if earlier else self.moving
                sends = self.chain.send(got)
            self.sent = sends[0][0]
            self.moving = [move(x) for x, move in sends]
        except StopIteration as end:
            self.moving = None
            self.result = end.value
        return self

    def finish(self, *earlier):
        while self.result is None:
            self.step(*earlier)
            earlier = ()
        return self.result


def by_bit(bit, axis_name="batch"):
    return lambda x: swap_bit(x, axis_name, bit)


def halving_blocks(rank, orders):
    bits = [(rank >> order[0]) & 1 for order in orders]
    sends = [2 * index + 1 - bit for index, bit in enumerate(bits)]
    keeps = [2 * index + bit for index, bit in enumerate(bits)]
    return jnp.stack(sends + keeps).astype(jnp.int32)


def scatter_stages(parts, rank, orders, dim, blocks=None):
    if blocks is not None:
        count = len(orders)
        got = yield [
            (block, by_bit(order[0])) for block, order in zip(blocks[:count], orders)
        ]
        parts = [add_low(keep, other) for keep, other in zip(blocks[count:], got)]
    for place in range(blocks is not None, len(orders[0])):
        keeps, sends = [], []
        for part, order in zip(parts, orders):
            half = part.shape[dim] // 2
            mine = (rank >> order[place]) & 1
            send = lax.dynamic_slice_in_dim(part, (1 - mine) * half, half, dim)
            keeps.append(lax.dynamic_slice_in_dim(part, mine * half, half, dim))
            sends.append((send, by_bit(order[place])))
        parts = [add_low(keep, got) for keep, got in zip(keeps, (yield sends))]
    return parts


def gather_stages(parts, rank, orders, dim):
    for place in reversed(range(len(orders[0]))):
        sends = [(part, by_bit(order[place])) for part, order in zip(parts, orders)]
        others = yield sends
        joined = []
        for part, other, order in zip(parts, others, orders):
            mine = ((rank >> order[place]) & 1) == 1
            joined.append(
                jnp.concatenate(
                    [jnp.where(mine, other, part), jnp.where(mine, part, other)], axis=dim
                )
            )
        parts = joined
    return parts


def bit_orders(size):
    count = size.bit_length() - 1
    return [[(start + k) % count for k in range(count)] for start in range(min(count, 2))]


def cut(x, count, dim):
    size = x.shape[dim] // count
    return [lax.slice_in_dim(x, k * size, (k + 1) * size, axis=dim) for k in range(count)]


def sum_stages(blocks, rank, orders, dim):
    parts = yield from scatter_stages(None, rank, orders, dim, blocks)
    parts = yield from gather_stages(parts, rank, orders, dim)
    return jnp.concatenate(parts, axis=dim).astype(F32)


def line_scatter_stages(x, rank, size, shift):
    sends = []
    for away in range(1, size):
        for step in (away, -away):
            target = jnp.clip(rank + step, 0, size - 1)
            block = lax.dynamic_index_in_dim(x, target, 0, keepdims=False)
            sends.append((block, functools.partial(shift, step=step)))
    total = lax.dynamic_index_in_dim(x, rank, 0, keepdims=False).astype(F32)
    for block in (yield sends):
        total = total + block.astype(F32)
    return total.astype(BF16)


def small_stages(everywhere, over_batch, batch_bits, tensor_bits):
    for bit in range(tensor_bits):
        (other,) = yield [(everywhere, by_bit(bit, "tensor"))]
        everywhere = everywhere + other
    values = [everywhere, *over_batch]
    for bit in range(batch_bits):
        others = yield [(value, by_bit(bit)) for value in values]
        values = [value + other for value, other in zip(values, others)]
    return values


def norm_forward(values, gain_vector, shift_vector):
    average = jnp.mean(values, axis=-1, keepdims=True)
    centred = values - average
    spread = jnp.mean(centred * centred, axis=-1, keepdims=True)
    inverse = lax.rsqrt(spread + EPSILON)
    normal = centred * inverse
    return (normal * gain_vector + shift_vector, normal, inverse)


def norm_backward(grad_rows, gain_vector, normal, inverse):
    scaled = grad_rows * gain_vector
    return inverse * (
        scaled
        - jnp.mean(scaled, axis=-1, keepdims=True)
        - normal * jnp.mean(scaled * normal, axis=-1, keepdims=True)
    )


def rotary_tables(positions):
    half_dim = HEAD_DIM // 2
    frequency = jnp.exp(
        jnp.arange(half_dim, dtype=F32) * (-2.0 * math.log(ROPE_BASE) / HEAD_DIM)
    )
    angles = positions.astype(F32)[..., None] * frequency
    cosine, sine = jnp.cos(angles), jnp.sin(angles)
    return (
        jnp.concatenate([cosine, cosine], axis=-1),
        jnp.concatenate([-sine, sine], axis=-1),
    )


def visible_range(segment, prefix):
    member = (segment[:, None] == jnp.arange(SEGS, dtype=jnp.int32)[None, :]).astype(jnp.int32)
    counts = jnp.sum(member, axis=0)
    starts = jnp.cumsum(counts) - counts
    ordinal = jnp.arange(segment.shape[0], dtype=jnp.int32)
    first = jnp.sum(member * starts[None, :], axis=1)
    seen = jnp.sum(member * jnp.minimum(prefix, counts)[None, :], axis=1)
    last = jnp.maximum(ordinal, first + seen - 1)
    tiled = (segment.shape[0] // QUERY_TILE, 1, QUERY_TILE)
    return first.reshape(tiled), last.reshape(tiled)


def per_device(
    batch_size,
    tensor_size,
    tokens,
    cotangent,
    segment_ids,
    prefix_lengths,
    rotary_positions,
    residual_scale,
    qkv_weight,
    qkv_bias,
    out_weight,
    out_bias,
    norm_gain,
    norm_shift,
    gate_weight,
    gate_bias,
    up_weight,
    up_bias,
    down_weight,
    down_bias,
    final_gain,
    final_shift,
):
    packs, local_rows, width = tokens.shape
    columns = down_weight.shape[0]
    batch_rank = lax.axis_index("batch")
    tensor_rank = lax.axis_index("tensor")
    chips = tensor_size // 2
    chip_rank = tensor_rank // 2
    core = lax.rem(tensor_rank, 2)
    first_core = core == 0
    orders = bit_orders(batch_size)
    scale_value = residual_scale[0]
    across = by_bit(0, "tensor")

    def shift(x, step):
        moves = [
            (chip * 2 + side, (chip + step) * 2 + side)
            for chip in range(chips)
            for side in range(2)
            if 0 <= chip + step < chips
        ]
        return lax.ppermute(x, "tensor", moves)

    def by_core(mine, other, axis):
        return jnp.concatenate(
            [jnp.where(first_core, mine, other), jnp.where(first_core, other, mine)], axis=axis
        )

    def gather_rows(x):
        return lax.all_gather(x, "tensor", axis=0, tiled=True)

    def scatter_rows(x):
        return lax.psum_scatter(x, "tensor", scatter_dimension=0, tiled=True)

    gate_rows = gate_weight.T
    up_rows = up_weight.T
    qkv_slabs = jnp.transpose(qkv_weight, (1, 0, 2))
    qkv_bias_rows = qkv_bias[:, None, :]
    gate_bias_column = gate_bias[:, None]
    up_bias_column = up_bias[:, None]
    live = (FF_LIVE - tensor_rank * columns).astype(jnp.int32)[None]
    half = width // 2

    def own_piece(x, side):
        pieces = []
        for index, order in enumerate(orders):
            part = half // len(orders)
            piece = lax.dynamic_slice_in_dim(x, side * half + index * part, part, 1)
            for bit in order:
                size = piece.shape[1] // 2
                piece = lax.dynamic_slice_in_dim(piece, ((batch_rank >> bit) & 1) * size, size, 1)
            pieces.append(piece)
        return jnp.concatenate(pieces, axis=1)

    def out_gather_stages(piece):
        side = piece.shape[1] // 2
        piece = lax.dynamic_slice_in_dim(piece, core * side, side, 1)
        parts = yield from gather_stages(cut(piece, len(orders), 1), batch_rank, orders, 1)
        mine = jnp.concatenate(parts, axis=1)
        (other,) = yield [(mine, across)]
        return by_core(mine, other, 1)

    def out_scatter_stages(send, keep):
        (other,) = yield [(send, across)]
        total = add_low(keep, other)
        parts = yield from scatter_stages(cut(total, len(orders), 1), batch_rank, orders, 1)
        total = jnp.concatenate(parts, axis=1)
        total = yield from line_scatter_stages(
            total.reshape(chips, -1, total.shape[1]), chip_rank, chips, shift
        )
        rows = total.shape[0] // 2
        mine = lax.dynamic_slice_in_dim(total, core * rows, rows, 0)
        (other,) = yield [
            (lax.dynamic_slice_in_dim(total, (1 - core) * rows, rows, 0), across)
        ]
        sides = [jnp.where(first_core, mine, other), jnp.where(first_core, other, mine)]
        parts = [part for side in sides for part in cut(side, len(orders), 1)]
        parts = yield from gather_stages(parts, batch_rank, orders * 2, 1)
        return jnp.concatenate(parts, axis=1).astype(F32)

    tables = [rotary_tables(rotary_positions[p]) for p in range(packs)]
    ranges = [visible_range(segment_ids[p], prefix_lengths[p]) for p in range(packs)]

    out_piece = gather_rows(
        jnp.concatenate([own_piece(out_weight, 0), own_piece(out_weight, 1)], axis=1)
    )
    whole_tokens = []
    last = out_piece
    for p in range(packs):
        whole_tokens.append(gather_rows(tokens[p]))
    out_flow = Flow(out_gather_stages(out_piece))
    for _ in range(len(orders[0])):
        out_flow.step()
    last = out_flow.sent

    qkvs, log_sums, context_rows = [], [], []
    normed, normal_one, inverse_one, hidden = [], [], [], []
    for p in range(packs):
        qkv, context, log_sum = attend_forward(
            after(whole_tokens[p], last), qkv_slabs, qkv_bias_rows, *tables[p], *ranges[p]
        )
        qkvs.append(qkv)
        log_sums.append(log_sum)
        context_rows.append(
            lax.all_to_all(context, "tensor", split_axis=0, concat_axis=1, tiled=True)
        )
        if p == 0:
            out_flow.step(context)
            whole_out = out_flow.finish()
        attended = dot_nn(context_rows[p], whole_out) + out_bias
        value, normal, inverse = norm_forward(
            scale_value * tokens[p].astype(F32) + attended, norm_gain, norm_shift
        )
        normed.append(value)
        normal_one.append(normal)
        inverse_one.append(inverse)
        last = value.astype(BF16)
        hidden.append(gather_rows(last))

    activated, gelus, slopes, branches = [], [], [], []
    for p in range(packs):
        act, gelu, slope, branch = glu_forward(
            live, after(hidden[p], last), gate_rows, up_rows, down_weight,
            gate_bias_column, up_bias_column,
        )
        activated.append(act)
        gelus.append(gelu)
        slopes.append(slope)
        branches.append(scatter_rows(branch))
        last = act

    outputs, grads_two = [], []
    final_gain_part = final_shift_part = down_bias_part = 0.0
    branch_grads = []
    for p in range(packs):
        rows, normal_two, inverse_two = norm_forward(
            scale_value * normed[p] + (after(branches[p], last).astype(F32) + down_bias),
            final_gain,
            final_shift,
        )
        outputs.append(rows.astype(BF16))
        grad_final = cotangent[p].astype(F32)
        final_gain_part += jnp.sum(grad_final * normal_two, axis=0)
        final_shift_part += jnp.sum(grad_final, axis=0)
        grad_two = norm_backward(grad_final, final_gain, normal_two, inverse_two)
        down_bias_part += jnp.sum(grad_two, axis=0)
        grads_two.append(grad_two)
        last = grad_two.astype(BF16)
        branch_grads.append(gather_rows(last))

    blocks = halving_blocks(batch_rank, orders)
    gate_lows, up_lows, normed_sums = [], [], []
    gate_bias_part = up_bias_part = 0.0
    for p in range(packs):
        if p == packs - 1:
            down_blocks = weight_grad(
                [[after(act, last)] for act in activated], branch_grads, blocks
            )
            down_flow = Flow(
                sum_stages([block[0] for block in down_blocks], batch_rank, orders, 1)
            ).step()
            last = down_flow.sent
        gate_low, up_low, gate_sum, up_sum, normed_part = glu_backward(
            live, after(branch_grads[p], last), gate_rows, up_rows, down_weight,
            gelus[p], slopes[p],
        )
        gate_lows.append(gate_low)
        up_lows.append(up_low)
        gate_bias_part += gate_sum
        up_bias_part += up_sum
        normed_sums.append(scatter_rows(normed_part))
        last = gate_low
    last = down_flow.step(last).sent
    glu_blocks = weight_grad(
        [[after(gate, last), up] for gate, up in zip(gate_lows, up_lows)], hidden, blocks
    )
    glu_flow = Flow(sum_stages(glu_blocks, batch_rank, orders, 2)).step()
    down_flow.step(glu_flow.sent)
    last = down_flow.sent

    grads_one, attended_lows, lows, input_grads = [], [], [], []
    norm_gain_part = norm_shift_part = out_bias_part = 0.0
    qkv_bias_part = 0.0
    for p in range(packs):
        normed_grad = (
            after(normed_sums[p], last).astype(F32) + scale_value * grads_two[p]
        )
        norm_gain_part += jnp.sum(normed_grad * normal_one[p], axis=0)
        norm_shift_part += jnp.sum(normed_grad, axis=0)
        grad_one = norm_backward(normed_grad, norm_gain, normal_one[p], inverse_one[p])
        out_bias_part += jnp.sum(grad_one, axis=0)
        attended_low = grad_one.astype(BF16)
        grads_one.append(grad_one)
        attended_lows.append(attended_low)
        context_grad = dot_nt(attended_low, whole_out).astype(BF16)
        last = context_grad
        context_grad = lax.all_to_all(
            context_grad, "tensor", split_axis=1, concat_axis=0, tiled=True
        )
        if p == packs - 1:
            glu_flow.step(last)
            send, keep = row_grad(
                after(jnp.concatenate(context_rows, axis=0), glu_flow.sent),
                jnp.concatenate(attended_lows, axis=0),
                jnp.stack([1 - core, core]).astype(jnp.int32),
            )
            out_flow = Flow(out_scatter_stages(send, keep)).step()
            last = out_flow.sent
            shared = jnp.stack(
                [
                    out_bias_part,
                    norm_gain_part,
                    norm_shift_part,
                    down_bias_part,
                    final_gain_part,
                    final_shift_part,
                ]
            )
        else:
            last = down_flow.step(last).sent
        low, bias_sum, input_part = attend_backward(
            qkvs[p], after(context_grad, last), log_sums[p], *ranges[p], *tables[p], qkv_slabs
        )
        last = low
        lows.append(low)
        qkv_bias_part += bias_sum
        input_grads.append(
            scatter_rows(input_part).astype(F32) + scale_value * grads_one[p]
        )
        glu_flow.step(last)
        last = glu_flow.sent
        if p == packs - 1:
            last = out_flow.step(last).sent
    qkv_blocks = slab_grad(whole_tokens, [after(low, last) for low in lows], blocks)
    qkv_flow = Flow(sum_stages(qkv_blocks, batch_rank, orders, 1)).step()
    last = qkv_flow.sent
    glu_bias = jnp.concatenate([gate_bias_part[:, 0], up_bias_part[:, 0]])
    small_flow = Flow(
        small_stages(
            shared,
            (glu_bias, qkv_bias_part[:, 0, :]),
            batch_size.bit_length() - 1,
            tensor_size.bit_length() - 1,
        )
    )
    flows = [down_flow, glu_flow, out_flow, qkv_flow, small_flow]
    while any(flow.result is None for flow in flows):
        for flow in flows:
            if flow.result is None:
                flow.step(last)
                if flow.result is None:
                    last = flow.sent
    down_grad, glu_grad, out_grad, qkv_grad, (shared, glu_bias, qkv_bias_grad) = [
        flow.result for flow in flows
    ]
    return (
        jnp.stack(outputs),
        jnp.stack(input_grads),
        jnp.transpose(qkv_grad, (1, 0, 2)),
        qkv_bias_grad,
        out_grad,
        shared[0],
        shared[1],
        shared[2],
        glu_grad[0].T,
        glu_bias[:columns],
        glu_grad[1].T,
        glu_bias[columns:],
        down_grad,
        shared[3],
        shared[4],
        shared[5],
    )


def solution(mesh):
    return jax.shard_map(
        functools.partial(per_device, mesh.shape["batch"], mesh.shape["tensor"]),
        mesh=mesh,
        in_specs=(
            P("batch", "tensor", None),
            P("batch", "tensor", None),
            P("batch", None),
            P("batch", None),
            P("batch", None),
            P(),
            P(None, None, "tensor"),
            P(None, "tensor"),
            P("tensor", None),
            P(),
            P(),
            P(),
            P(None, "tensor"),
            P("tensor"),
            P(None, "tensor"),
            P("tensor"),
            P("tensor", None),
            P(),
            P(),
            P(),
        ),
        out_specs=(
            P("batch", "tensor", None),
            P("batch", "tensor", None),
            P(None, None, "tensor"),
            P(None, "tensor"),
            P("tensor", None),
            P(),
            P(),
            P(),
            P(None, "tensor"),
            P("tensor"),
            P(None, "tensor"),
            P("tensor"),
            P("tensor", None),
            P(),
            P(),
            P(),
        ),
        check_vma=False,
    )
```

```python
import functools
import math

import jax
import jax.numpy as jnp
from jax import lax
from jax.experimental import pallas as pl
from jax.experimental.pallas import tpu as pltpu
from jax.sharding import PartitionSpec as P

FF_LIVE = 5461
SEGS = 4
HEAD_DIM = 128

EPSILON = 1e-05
NEG_FILL = -1e30
ROPE_BASE = 10000.0
GELU_ROOT = math.sqrt(2.0 / math.pi)
GELU_CUBIC = 0.044715
FACTOR = 1.0 / math.sqrt(HEAD_DIM)
QUERY_TILE = 256
ROW_TILE = 256
VMEM_LIMIT = 56 * 1024 * 1024
LONG = pl.CostEstimate(flops=200_000_000_000, bytes_accessed=1024, transcendentals=0)
SHORT = pl.CostEstimate(flops=1024, bytes_accessed=1024, transcendentals=0)
BF16 = jnp.bfloat16
F32 = jnp.float32


def dot_nn(a, b):
    return lax.dot_general(a, b, (((1,), (0,)), ((), ())), preferred_element_type=F32)


def dot_nt(a, b):
    return lax.dot_general(a, b, (((1,), (1,)), ((), ())), preferred_element_type=F32)


def dot_tn(a, b):
    return lax.dot_general(a, b, (((0,), (0,)), ((), ())), preferred_element_type=F32)


def attend_forward_kernel(
    x_ref, w_ref, b_ref, cos_ref, sin_ref, lo_ref, hi_ref, qkv_ref, ctx_ref, lse_ref
):
    step = pl.program_id(0)
    heads = ctx_ref.shape[1] // HEAD_DIM
    tile = x_ref.shape[0]
    rows = pl.ds(pl.multiple_of(step * tile, tile), tile)
    x = x_ref[...]
    cosine = cos_ref[rows, :]
    sine = sin_ref[rows, :]
    for part in range(3):
        projected = dot_nn(x, w_ref[part]) + b_ref[part]
        for head in range(heads):
            value = projected[:, head * HEAD_DIM : (head + 1) * HEAD_DIM]
            if part < 2:
                value = value * cosine + pltpu.roll(value, HEAD_DIM // 2, 1) * sine
            qkv_ref[part * heads + head, rows, :] = value.astype(BF16)

    @pl.when(step == pl.num_programs(0) - 1)
    def _():
        length = qkv_ref.shape[1]
        for head in range(heads):
            keys = qkv_ref[heads + head]
            values_t = qkv_ref[2 * heads + head].T

            def one_tile(index, carry):
                first = pl.multiple_of(index * QUERY_TILE, QUERY_TILE)
                queries = qkv_ref[head, pl.ds(first, QUERY_TILE), :]
                scores = dot_nt(keys, queries)
                place = lax.broadcasted_iota(jnp.int32, (length, QUERY_TILE), 0)
                seen = (place >= lo_ref[index]) & (place <= hi_ref[index])
                scores = jnp.where(seen, scores, NEG_FILL)
                top = jnp.max(scores, axis=0, keepdims=True)
                shifted = jnp.exp((scores - top) * FACTOR)
                total = jnp.sum(shifted, axis=0, keepdims=True)
                probs = (shifted * (1.0 / total)).astype(BF16)
                context_t = dot_nn(values_t, probs)
                ctx_ref[pl.ds(first, QUERY_TILE), head * HEAD_DIM : (head + 1) * HEAD_DIM] = (
                    context_t.T.astype(BF16)
                )
                lse_ref[head, index] = top * FACTOR + jnp.log(total)
                return carry

            lax.fori_loop(0, length // QUERY_TILE, one_tile, 0)


def attend_forward(x, w, b, cosine, sine, lo, hi):
    length, width = x.shape
    head_width = w.shape[2]
    heads = head_width // HEAD_DIM
    tiles = length // QUERY_TILE
    whole = lambda *shape: pl.BlockSpec(shape, lambda i: (0,) * len(shape))
    return pl.pallas_call(
        attend_forward_kernel,
        grid=(length // ROW_TILE,),
        in_specs=[
            pl.BlockSpec((ROW_TILE, width), lambda i: (i, 0)),
            whole(3, width, head_width),
            whole(3, 1, head_width),
            whole(length, HEAD_DIM),
            whole(length, HEAD_DIM),
            whole(tiles, 1, QUERY_TILE),
            whole(tiles, 1, QUERY_TILE),
        ],
        out_specs=[
            whole(3 * heads, length, HEAD_DIM),
            whole(length, head_width),
            whole(heads, tiles, 1, QUERY_TILE),
        ],
        out_shape=[
            jax.ShapeDtypeStruct((3 * heads, length, HEAD_DIM), BF16),
            jax.ShapeDtypeStruct((length, head_width), BF16),
            jax.ShapeDtypeStruct((heads, tiles, 1, QUERY_TILE), F32),
        ],
        compiler_params=pltpu.CompilerParams(vmem_limit_bytes=VMEM_LIMIT),
        cost_estimate=LONG,
        name="attend_forward",
    )(x, w, b, cosine, sine, lo, hi)


def attend_backward_kernel(
    qkv_ref,
    grad_ref,
    lse_ref,
    lo_ref,
    hi_ref,
    cos_ref,
    sin_ref,
    w_ref,
    low_ref,
    bias_ref,
    x_grad_ref,
    key_total,
    value_total,
):
    step = pl.program_id(0)
    length = qkv_ref.shape[1]
    heads = qkv_ref.shape[0] // 3
    tile = x_grad_ref.shape[0]

    def rope_back(grad, cosine, sine):
        return grad * cosine - pltpu.roll(grad, HEAD_DIM // 2, 1) * sine

    @pl.when(step == 0)
    def _():
        for head in range(heads):
            lanes = slice(head * HEAD_DIM, (head + 1) * HEAD_DIM)
            keys = qkv_ref[heads + head]
            keys_t = keys.T
            values = qkv_ref[2 * heads + head]
            key_total[...] = jnp.zeros_like(key_total)
            value_total[...] = jnp.zeros_like(value_total)

            def one_tile(index, query_bias):
                first = pl.multiple_of(index * QUERY_TILE, QUERY_TILE)
                rows = pl.ds(first, QUERY_TILE)
                queries = qkv_ref[head, rows, :]
                grads = grad_ref[rows, lanes]
                scores = dot_nt(keys, queries)
                place = lax.broadcasted_iota(jnp.int32, (length, QUERY_TILE), 0)
                seen = (place >= lo_ref[index]) & (place <= hi_ref[index])
                scores = jnp.where(seen, scores * FACTOR, NEG_FILL)
                probs = jnp.exp(scores - lse_ref[head, index])
                probs_grad = dot_nt(values, grads)
                delta = jnp.sum(probs * probs_grad, axis=0, keepdims=True)
                score_grad = (probs * (probs_grad - delta)).astype(BF16)
                query_grad = dot_nn(keys_t, score_grad).T * FACTOR
                key_total[...] += dot_nn(score_grad, queries)
                value_total[...] += dot_nn(probs.astype(BF16), grads)
                query_grad = rope_back(query_grad, cos_ref[rows, :], sin_ref[rows, :])
                low_ref[0, rows, lanes] = query_grad.astype(BF16)
                return query_bias + jnp.sum(query_grad, axis=0, keepdims=True)

            query_bias = lax.fori_loop(
                0, length // QUERY_TILE, one_tile, jnp.zeros((1, HEAD_DIM), F32)
            )
            key_grad = rope_back(key_total[...] * FACTOR, cos_ref[...], sin_ref[...])
            value_grad = value_total[...]
            low_ref[1, :, lanes] = key_grad.astype(BF16)
            low_ref[2, :, lanes] = value_grad.astype(BF16)
            bias_ref[0, :, lanes] = query_bias
            bias_ref[1, :, lanes] = jnp.sum(key_grad, axis=0, keepdims=True)
            bias_ref[2, :, lanes] = jnp.sum(value_grad, axis=0, keepdims=True)

    rows = pl.ds(pl.multiple_of(step * tile, tile), tile)
    total = dot_nt(low_ref[0, rows, :], w_ref[0])
    total += dot_nt(low_ref[1, rows, :], w_ref[1])
    total += dot_nt(low_ref[2, rows, :], w_ref[2])
    x_grad_ref[...] = total.astype(BF16)


def attend_backward(qkv, grad, lse, lo, hi, cosine, sine, w, cost):
    width, head_width = w.shape[1:]
    length = grad.shape[0]
    heads = head_width // HEAD_DIM
    tiles = length // QUERY_TILE
    whole = lambda *shape: pl.BlockSpec(shape, lambda i: (0,) * len(shape))
    return pl.pallas_call(
        attend_backward_kernel,
        grid=(length // ROW_TILE,),
        in_specs=[
            whole(3 * heads, length, HEAD_DIM),
            whole(length, head_width),
            whole(heads, tiles, 1, QUERY_TILE),
            whole(tiles, 1, QUERY_TILE),
            whole(tiles, 1, QUERY_TILE),
            whole(length, HEAD_DIM),
            whole(length, HEAD_DIM),
            whole(3, width, head_width),
        ],
        out_specs=[
            whole(3, length, head_width),
            whole(3, 1, head_width),
            pl.BlockSpec((ROW_TILE, width), lambda i: (i, 0)),
        ],
        out_shape=[
            jax.ShapeDtypeStruct((3, length, head_width), BF16),
            jax.ShapeDtypeStruct((3, 1, head_width), F32),
            jax.ShapeDtypeStruct((length, width), BF16),
        ],
        scratch_shapes=[
            pltpu.VMEM((length, HEAD_DIM), F32),
            pltpu.VMEM((length, HEAD_DIM), F32),
        ],
        compiler_params=pltpu.CompilerParams(vmem_limit_bytes=VMEM_LIMIT),
        cost_estimate=cost,
        name="attend_backward",
    )(qkv, grad, lse, lo, hi, cosine, sine, w)


def glu_forward_kernel(
    live_ref, h_ref, wg_ref, wu_ref, wd_ref, bg_ref, bu_ref, act_ref, gelu_ref, slope_ref, out_ref
):
    hidden = h_ref[...]
    gate = dot_nt(wg_ref[...], hidden) + bg_ref[...]
    up = dot_nt(wu_ref[...], hidden) + bu_ref[...]
    squared = gate * gate
    tangent = jnp.tanh(GELU_ROOT * gate * (1.0 + GELU_CUBIC * squared))
    half = 0.5 * (1.0 + tangent)
    gelu = gate * half
    slope = half + 0.5 * gate * (1.0 - tangent * tangent) * GELU_ROOT * (
        1.0 + 3.0 * GELU_CUBIC * squared
    )
    column = lax.broadcasted_iota(jnp.int32, gate.shape, 0)
    activated = jnp.where(column < live_ref[0], gelu * up, 0.0).astype(BF16)
    act_ref[...] = activated
    gelu_ref[...] = gelu.astype(BF16)
    slope_ref[...] = (up * slope).astype(BF16)
    out_ref[...] = dot_tn(activated, wd_ref[...]).astype(BF16)


def glu_forward(live, hidden, wg, wu, wd, bg, bu):
    length, width = hidden.shape
    columns = wg.shape[0]
    whole = lambda *shape: pl.BlockSpec(shape, lambda i: (0,) * len(shape))
    tall = pl.BlockSpec((columns, ROW_TILE), lambda i: (0, i))
    wide = pl.BlockSpec((ROW_TILE, width), lambda i: (i, 0))
    return pl.pallas_call(
        glu_forward_kernel,
        grid=(length // ROW_TILE,),
        in_specs=[pl.BlockSpec(memory_space=pltpu.SMEM), wide]
        + [whole(columns, width)] * 3
        + [whole(columns, 1)] * 2,
        out_specs=[tall, tall, tall, wide],
        out_shape=[jax.ShapeDtypeStruct((columns, length), BF16)] * 3
        + [jax.ShapeDtypeStruct((length, width), BF16)],
        compiler_params=pltpu.CompilerParams(vmem_limit_bytes=VMEM_LIMIT),
        cost_estimate=LONG,
        name="glu_forward",
    )(live, hidden, wg, wu, wd, bg, bu)


def glu_backward_kernel(
    live_ref,
    g_ref,
    wg_ref,
    wu_ref,
    wd_ref,
    gelu_ref,
    slope_ref,
    gate_ref,
    up_ref,
    gate_bias_ref,
    up_bias_ref,
    out_ref,
    gate_sum,
    up_sum,
):
    @pl.when(pl.program_id(0) == 0)
    def _():
        gate_sum[...] = jnp.zeros_like(gate_sum)
        up_sum[...] = jnp.zeros_like(up_sum)

    grad = dot_nt(wd_ref[...], g_ref[...])
    column = lax.broadcasted_iota(jnp.int32, grad.shape, 0)
    grad = jnp.where(column < live_ref[0], grad, 0.0)
    gate_grad = grad * slope_ref[...].astype(F32)
    up_grad = grad * gelu_ref[...].astype(F32)
    for first in range(0, grad.shape[1], 128):
        gate_sum[...] += gate_grad[:, first : first + 128]
        up_sum[...] += up_grad[:, first : first + 128]

    @pl.when(pl.program_id(0) == pl.num_programs(0) - 1)
    def _():
        gate_bias_ref[...] = jnp.sum(gate_sum[...], axis=1, keepdims=True)
        up_bias_ref[...] = jnp.sum(up_sum[...], axis=1, keepdims=True)

    gate_low = gate_grad.astype(BF16)
    up_low = up_grad.astype(BF16)
    gate_ref[...] = gate_low
    up_ref[...] = up_low
    out_ref[...] = (dot_tn(gate_low, wg_ref[...]) + dot_tn(up_low, wu_ref[...])).astype(BF16)


def glu_backward(live, grad, wg, wu, wd, gelu, slope):
    length, width = grad.shape
    columns = wg.shape[0]
    whole = lambda *shape: pl.BlockSpec(shape, lambda i: (0,) * len(shape))
    tall = pl.BlockSpec((columns, ROW_TILE), lambda i: (0, i))
    wide = pl.BlockSpec((ROW_TILE, width), lambda i: (i, 0))
    return pl.pallas_call(
        glu_backward_kernel,
        grid=(length // ROW_TILE,),
        in_specs=[pl.BlockSpec(memory_space=pltpu.SMEM), wide]
        + [whole(columns, width)] * 3
        + [tall, tall],
        out_specs=[tall, tall, whole(columns, 1), whole(columns, 1), wide],
        out_shape=[jax.ShapeDtypeStruct((columns, length), BF16)] * 2
        + [jax.ShapeDtypeStruct((columns, 1), F32)] * 2
        + [jax.ShapeDtypeStruct((length, width), BF16)],
        scratch_shapes=[pltpu.VMEM((columns, 128), F32)] * 2,
        compiler_params=pltpu.CompilerParams(vmem_limit_bytes=VMEM_LIMIT),
        cost_estimate=LONG,
        name="glu_backward",
    )(live, grad, wg, wu, wd, gelu, slope)


def weight_grad_kernel(packs, outs, blocks_ref, *refs):
    lefts = refs[: packs * outs]
    rights = refs[packs * outs : packs * (outs + 1)]
    results = refs[packs * (outs + 1) :]
    for index, result in enumerate(results):

        @pl.when(pl.program_id(0) == index)
        def _():
            for out in range(outs):
                total = dot_nn(lefts[out][...], rights[0][...])
                for pack in range(1, packs):
                    total += dot_nn(lefts[pack * outs + out][...], rights[pack][...])
                result[out] = total.astype(BF16)


def weight_grad(lefts, rights, blocks):
    packs = len(rights)
    outs = len(lefts[0])
    length, width = rights[0].shape
    columns = lefts[0][0].shape[0]
    count = blocks.shape[0]
    tile = width // count
    return pl.pallas_call(
        functools.partial(weight_grad_kernel, packs, outs),
        grid_spec=pltpu.PrefetchScalarGridSpec(
            num_scalar_prefetch=1,
            grid=(count,),
            in_specs=[pl.BlockSpec((columns, length), lambda i, at: (0, 0))] * (packs * outs)
            + [pl.BlockSpec((length, tile), lambda i, at: (0, at[i]))] * packs,
            out_specs=[pl.BlockSpec((outs, columns, tile), lambda i, at: (0, 0, 0))] * count,
        ),
        out_shape=[jax.ShapeDtypeStruct((outs, columns, tile), BF16)] * count,
        compiler_params=pltpu.CompilerParams(vmem_limit_bytes=VMEM_LIMIT),
        cost_estimate=LONG,
        name="weight_grad",
    )(blocks, *[left for pack in lefts for left in pack], *rights)


def slab_grad_kernel(packs, blocks_ref, *refs):
    results = refs[2 * packs :]
    for index, result in enumerate(results):

        @pl.when(pl.program_id(0) == index)
        def _():
            for part in range(3):
                total = dot_tn(refs[0][...], refs[packs][part])
                for pack in range(1, packs):
                    total += dot_tn(refs[pack][...], refs[packs + pack][part])
                result[part] = total.astype(BF16)


def slab_grad(lefts, rights, blocks):
    packs = len(rights)
    length, width = lefts[0].shape
    columns = rights[0].shape[2]
    count = blocks.shape[0]
    tile = width // count
    return pl.pallas_call(
        functools.partial(slab_grad_kernel, packs),
        grid_spec=pltpu.PrefetchScalarGridSpec(
            num_scalar_prefetch=1,
            grid=(count,),
            in_specs=[pl.BlockSpec((length, tile), lambda i, at: (0, at[i]))] * packs
            + [pl.BlockSpec((3, length, columns), lambda i, at: (0, 0, 0))] * packs,
            out_specs=[pl.BlockSpec((3, tile, columns), lambda i, at: (0, 0, 0))] * count,
        ),
        out_shape=[jax.ShapeDtypeStruct((3, tile, columns), BF16)] * count,
        compiler_params=pltpu.CompilerParams(vmem_limit_bytes=VMEM_LIMIT),
        cost_estimate=SHORT,
        name="slab_grad",
    )(blocks, *lefts, *rights)


def row_grad_kernel(sides_ref, left_ref, right_ref, *results):
    columns = left_ref.shape[1]
    for index, result in enumerate(results):

        @pl.when(pl.program_id(0) == index)
        def _():
            rows = pl.ds(pl.multiple_of(pl.program_id(1) * columns, columns), columns)
            result[rows, :] = dot_tn(left_ref[...], right_ref[...]).astype(BF16)


def row_grad(left, right, sides, columns):
    rows, depth = left.shape
    width = right.shape[1]
    count = sides.shape[0]
    steps = depth // columns // count
    return pl.pallas_call(
        row_grad_kernel,
        grid_spec=pltpu.PrefetchScalarGridSpec(
            num_scalar_prefetch=1,
            grid=(count, steps),
            in_specs=[
                pl.BlockSpec((rows, columns), lambda i, j, at: (0, count * j + at[i])),
                pl.BlockSpec((rows, width), lambda i, j, at: (0, 0)),
            ],
            out_specs=[pl.BlockSpec((depth // count, width), lambda i, j, at: (0, 0))] * count,
        ),
        out_shape=[jax.ShapeDtypeStruct((depth // count, width), BF16)] * count,
        compiler_params=pltpu.CompilerParams(vmem_limit_bytes=VMEM_LIMIT),
        cost_estimate=SHORT,
        name="row_grad",
    )(sides, left, right)


def assemble_kernel(dim, sources_ref, *refs):
    pieces, result = refs[:-1], refs[-1]
    for index, piece in enumerate(pieces):

        @pl.when(sources_ref[pl.program_id(0)] == index)
        def _():
            result[...] = piece[...].astype(F32)


def assemble(pieces, sources, dim, cost):
    shape = pieces[0].shape
    count = len(pieces)
    whole = shape[:dim] + (shape[dim] * count,) + shape[dim + 1 :]
    zeros = (0,) * len(shape)
    place = lambda i, at: zeros[:dim] + (i,) + zeros[dim + 1 :]
    return pl.pallas_call(
        functools.partial(assemble_kernel, dim),
        grid_spec=pltpu.PrefetchScalarGridSpec(
            num_scalar_prefetch=1,
            grid=(count,),
            in_specs=[pl.BlockSpec(shape, lambda i, at: zeros)] * count,
            out_specs=pl.BlockSpec(shape, place),
        ),
        out_shape=jax.ShapeDtypeStruct(whole, F32),
        compiler_params=pltpu.CompilerParams(vmem_limit_bytes=VMEM_LIMIT),
        cost_estimate=cost,
        name="assemble",
    )(sources, *pieces)


def add_low(a, b):
    return (a.astype(F32) + b.astype(F32)).astype(BF16)


def after(x, *earlier):
    return lax.optimization_barrier((x, *jax.tree.leaves(earlier)))[0]


def all_after(xs, earlier):
    earlier = jax.tree.leaves(earlier)
    if not earlier:
        return list(xs)
    return list(lax.optimization_barrier((*xs, *earlier))[: len(xs)])


def swap_bit(x, axis_name, bit):
    size = lax.axis_size(axis_name)
    return lax.ppermute(x, axis_name, [(i, i ^ (1 << bit)) for i in range(size)])


class Flow:
    def __init__(self, chain):
        self.chain = chain
        self.result = None
        self.moving = None

    def step(self, *earlier):
        try:
            if self.moving is None:
                sends = next(self.chain)
                self.sent = all_after([x for x, _ in sends], earlier)
            else:
                sends = self.chain.send(all_after(self.moving, earlier))
                self.sent = [x for x, _ in sends]
            self.moving = [move(x) for x, (_, move) in zip(self.sent, sends)]
        except StopIteration as end:
            self.moving = None
            self.result = end.value
        return self

    def settle(self, *earlier):
        self.moving = all_after(self.moving, earlier)
        return self.moving

    def finish(self, *earlier):
        while self.result is None:
            self.step(*earlier)
            earlier = ()
        return self.result


def by_bit(bit, axis_name="batch"):
    return lambda x: swap_bit(x, axis_name, bit)


def halving_blocks(rank, orders):
    bits = [(rank >> order[0]) & 1 for order in orders]
    sends = [2 * index + 1 - bit for index, bit in enumerate(bits)]
    keeps = [2 * index + bit for index, bit in enumerate(bits)]
    return jnp.stack(sends + keeps).astype(jnp.int32)


def scatter_stages(parts, rank, orders, dim, blocks=None, axis_name="batch", first_bit=0):
    if blocks is not None:
        count = len(orders)
        got = yield [
            (block, by_bit(order[0])) for block, order in zip(blocks[:count], orders)
        ]
        parts = [add_low(keep, other) for keep, other in zip(blocks[count:], got)]
    for place in range(blocks is not None, len(orders[0])):
        keeps, sends = [], []
        for part, order in zip(parts, orders):
            half = part.shape[dim] // 2
            mine = (rank >> order[place]) & 1
            send = lax.dynamic_slice_in_dim(part, (1 - mine) * half, half, dim)
            keeps.append(lax.dynamic_slice_in_dim(part, mine * half, half, dim))
            sends.append((send, by_bit(order[place] + first_bit, axis_name)))
        parts = [add_low(keep, got) for keep, got in zip(keeps, (yield sends))]
    return parts


def gather_stages(parts, rank, orders, dim):
    for place in reversed(range(len(orders[0]))):
        sends = [(part, by_bit(order[place])) for part, order in zip(parts, orders)]
        others = yield sends
        joined = []
        for part, other, order in zip(parts, others, orders):
            mine = ((rank >> order[place]) & 1) == 1
            joined.append(
                jnp.concatenate(
                    [jnp.where(mine, other, part), jnp.where(mine, part, other)], axis=dim
                )
            )
        parts = joined
    return parts


def bit_orders(size):
    count = size.bit_length() - 1
    return [[(start + k) % count for k in range(count)] for start in range(min(count, 2))]


def cut(x, count, dim):
    size = x.shape[dim] // count
    return [lax.slice_in_dim(x, k * size, (k + 1) * size, axis=dim) for k in range(count)]


def sum_stages(blocks, rank, orders, dim, cost):
    parts = yield from scatter_stages(None, rank, orders, dim, blocks)
    parts = yield from gather_stages(parts, rank, [order[1:] for order in orders], dim)
    others = yield [(part, by_bit(order[0])) for part, order in zip(parts, orders)]
    sources = []
    for index, order in enumerate(orders):
        bit = (rank >> order[0]) & 1
        sources += [bit * len(orders) + index, (1 - bit) * len(orders) + index]
    return assemble(parts + others, jnp.stack(sources).astype(jnp.int32), dim, cost)


def to_peer(mask):
    def move(x):
        size = lax.axis_size("batch")
        return lax.ppermute(x, "batch", [(i, i ^ mask) for i in range(size)])

    return move


def peer_blocks(rank, size):
    return jnp.stack([rank ^ mask for mask in range(size)]).astype(jnp.int32)


def direct_gather_stages(piece, rank, size, dim):
    others = yield [(piece, to_peer(mask)) for mask in range(1, size)]
    return assemble([piece, *others], peer_blocks(rank, size), dim, LONG)


def direct_sum_stages(blocks, rank, size, dim):
    got = yield [(blocks[mask], to_peer(mask)) for mask in range(1, size)]
    total = blocks[0].astype(F32)
    for other in got:
        total = total + other.astype(F32)
    result = yield from direct_gather_stages(total.astype(BF16), rank, size, dim)
    return result


def small_stages(everywhere, over_batch, batch_bits, tensor_bits):
    for bit in range(tensor_bits):
        (other,) = yield [(everywhere, by_bit(bit, "tensor"))]
        everywhere = everywhere + other
    values = [everywhere, *over_batch]
    if callable(values[-1]):
        values = values[:-1] + [values[-1]()]
    for bit in range(batch_bits):
        others = yield [(value, by_bit(bit)) for value in values]
        values = [value + other for value, other in zip(values, others)]
    return values


def norm_forward(values, gain_vector, shift_vector):
    average = jnp.mean(values, axis=-1, keepdims=True)
    centred = values - average
    spread = jnp.mean(centred * centred, axis=-1, keepdims=True)
    inverse = lax.rsqrt(spread + EPSILON)
    normal = centred * inverse
    return (normal * gain_vector + shift_vector, normal, inverse)


def norm_backward(grad_rows, gain_vector, normal, inverse):
    scaled = grad_rows * gain_vector
    return inverse * (
        scaled
        - jnp.mean(scaled, axis=-1, keepdims=True)
        - normal * jnp.mean(scaled * normal, axis=-1, keepdims=True)
    )


def rotary_tables(positions):
    half_dim = HEAD_DIM // 2
    frequency = jnp.exp(
        jnp.arange(half_dim, dtype=F32) * (-2.0 * math.log(ROPE_BASE) / HEAD_DIM)
    )
    angles = positions.astype(F32)[..., None] * frequency
    cosine, sine = jnp.cos(angles), jnp.sin(angles)
    return (
        jnp.concatenate([cosine, cosine], axis=-1),
        jnp.concatenate([-sine, sine], axis=-1),
    )


def visible_range(segment, prefix):
    member = (segment[:, None] == jnp.arange(SEGS, dtype=jnp.int32)[None, :]).astype(jnp.int32)
    counts = jnp.sum(member, axis=0)
    starts = jnp.cumsum(counts) - counts
    ordinal = jnp.arange(segment.shape[0], dtype=jnp.int32)
    first = jnp.sum(member * starts[None, :], axis=1)
    seen = jnp.sum(member * jnp.minimum(prefix, counts)[None, :], axis=1)
    last = jnp.maximum(ordinal, first + seen - 1)
    tiled = (segment.shape[0] // QUERY_TILE, 1, QUERY_TILE)
    return first.reshape(tiled), last.reshape(tiled)


def per_device(
    batch_size,
    tensor_size,
    tokens,
    cotangent,
    segment_ids,
    prefix_lengths,
    rotary_positions,
    residual_scale,
    qkv_weight,
    qkv_bias,
    out_weight,
    out_bias,
    norm_gain,
    norm_shift,
    gate_weight,
    gate_bias,
    up_weight,
    up_bias,
    down_weight,
    down_bias,
    final_gain,
    final_shift,
):
    packs, local_rows, width = tokens.shape
    columns = down_weight.shape[0]
    batch_rank = lax.axis_index("batch")
    tensor_rank = lax.axis_index("tensor")
    chips = tensor_size // 2
    chip_rank = tensor_rank // 2
    core = lax.rem(tensor_rank, 2)
    first_core = core == 0
    orders = bit_orders(batch_size)
    scale_value = residual_scale[0]
    across = by_bit(0, "tensor")

    def by_core(mine, other, axis):
        return jnp.concatenate(
            [jnp.where(first_core, mine, other), jnp.where(first_core, other, mine)], axis=axis
        )

    def gather_rows(x):
        return lax.all_gather(x, "tensor", axis=0, tiled=True)

    def scatter_rows(x):
        return lax.psum_scatter(x, "tensor", scatter_dimension=0, tiled=True)

    gate_rows = gate_weight.T
    up_rows = up_weight.T
    qkv_slabs = jnp.transpose(qkv_weight, (1, 0, 2))
    qkv_bias_rows = qkv_bias[:, None, :]
    gate_bias_column = gate_bias[:, None]
    up_bias_column = up_bias[:, None]
    live = (FF_LIVE - tensor_rank * columns).astype(jnp.int32)[None]
    half = width // 2

    def own_piece(x, side):
        pieces = []
        for index, order in enumerate(orders):
            part = half // len(orders)
            piece = lax.dynamic_slice_in_dim(x, side * half + index * part, part, 1)
            for bit in order:
                size = piece.shape[1] // 2
                piece = lax.dynamic_slice_in_dim(piece, ((batch_rank >> bit) & 1) * size, size, 1)
            pieces.append(piece)
        return jnp.concatenate(pieces, axis=1)

    def out_gather_stages(piece):
        side = piece.shape[1] // 2
        piece = lax.dynamic_slice_in_dim(piece, core * side, side, 1)
        parts = yield from gather_stages(cut(piece, len(orders), 1), batch_rank, orders, 1)
        mine = jnp.concatenate(parts, axis=1)
        (other,) = yield [(mine, across)]
        return by_core(mine, other, 1)

    def out_scatter_stages(send, keep):
        (other,) = yield [(send, across)]
        total = add_low(keep, other)
        parts = yield from scatter_stages(
            cut(total, len(orders), 1), batch_rank, orders, 1
        )
        total = jnp.concatenate(parts, axis=1)
        chip_bits = list(reversed(range(chips.bit_length() - 1)))
        (total,) = yield from scatter_stages(
            [total], chip_rank, [chip_bits], 0, axis_name="tensor", first_bit=1
        )
        parts = yield from gather_stages(cut(total, len(orders), 1), batch_rank, orders, 1)
        return jnp.concatenate(parts, axis=1).astype(F32)

    tables = [rotary_tables(rotary_positions[p]) for p in range(packs)]
    ranges = [visible_range(segment_ids[p], prefix_lengths[p]) for p in range(packs)]

    out_piece = gather_rows(
        jnp.concatenate([own_piece(out_weight, 0), own_piece(out_weight, 1)], axis=1)
    )
    whole_tokens = []
    last = out_piece
    for p in range(packs):
        whole_tokens.append(gather_rows(tokens[p]))
    out_flow = Flow(out_gather_stages(out_piece))
    whole_out = out_flow.finish()
    last = whole_out

    qkvs, log_sums, context_rows = [], [], []
    normed, normal_one, inverse_one, hidden = [], [], [], []
    for p in range(packs):
        qkv, context, log_sum = attend_forward(
            after(whole_tokens[p], last), qkv_slabs, qkv_bias_rows, *tables[p], *ranges[p]
        )
        qkvs.append(qkv)
        log_sums.append(log_sum)
        context_rows.append(
            lax.all_to_all(context, "tensor", split_axis=0, concat_axis=1, tiled=True)
        )
        attended = dot_nn(context_rows[p], whole_out) + out_bias
        value, normal, inverse = norm_forward(
            scale_value * tokens[p].astype(F32) + attended, norm_gain, norm_shift
        )
        normed.append(value)
        normal_one.append(normal)
        inverse_one.append(inverse)
        last = value.astype(BF16)
        hidden.append(gather_rows(last))

    activated, gelus, slopes, branches = [], [], [], []
    for p in range(packs):
        act, gelu, slope, branch = glu_forward(
            live, after(hidden[p], last), gate_rows, up_rows, down_weight,
            gate_bias_column, up_bias_column,
        )
        activated.append(act)
        gelus.append(gelu)
        slopes.append(slope)
        branches.append(scatter_rows(branch))
        last = act

    outputs, grads_two = [], []
    final_gain_part = final_shift_part = down_bias_part = 0.0
    branch_grads = []
    for p in range(packs):
        rows, normal_two, inverse_two = norm_forward(
            scale_value * normed[p] + (after(branches[p], last).astype(F32) + down_bias),
            final_gain,
            final_shift,
        )
        outputs.append(rows.astype(BF16))
        grad_final = cotangent[p].astype(F32)
        final_gain_part += jnp.sum(grad_final * normal_two, axis=0)
        final_shift_part += jnp.sum(grad_final, axis=0)
        grad_two = norm_backward(grad_final, final_gain, normal_two, inverse_two)
        down_bias_part += jnp.sum(grad_two, axis=0)
        grads_two.append(grad_two)
        last = grad_two.astype(BF16)
        branch_grads.append(gather_rows(last))

    blocks = halving_blocks(batch_rank, orders)
    gate_lows, up_lows, normed_sums = [], [], []
    gate_bias_part = up_bias_part = 0.0
    for p in range(packs):
        if p == packs - 1:
            down_blocks = weight_grad(
                [[after(act, last)] for act in activated], branch_grads, blocks
            )
            down_flow = Flow(
                sum_stages([block[0] for block in down_blocks], batch_rank, orders, 1, LONG)
            ).step()
            last = down_flow.sent
        gate_low, up_low, gate_sum, up_sum, normed_part = glu_backward(
            live, after(branch_grads[p], last), gate_rows, up_rows, down_weight,
            gelus[p], slopes[p],
        )
        gate_lows.append(gate_low)
        up_lows.append(up_low)
        gate_bias_part += gate_sum
        up_bias_part += up_sum
        normed_sums.append(scatter_rows(normed_part))
        last = gate_low
    last = down_flow.step(last).sent
    glu_blocks = weight_grad(
        [[after(gate, last), up] for gate, up in zip(gate_lows, up_lows)], hidden, blocks
    )
    glu_flow = Flow(sum_stages(glu_blocks, batch_rank, orders, 2, SHORT)).step()
    down_flow.step(glu_flow.sent)
    last = down_flow.sent

    grads_one, attended_lows, lows, input_grads = [], [], [], []
    norm_gain_part = norm_shift_part = out_bias_part = 0.0
    qkv_bias_part = 0.0
    for p in range(packs):
        normed_grad = (
            after(normed_sums[p], last).astype(F32) + scale_value * grads_two[p]
        )
        norm_gain_part += jnp.sum(normed_grad * normal_one[p], axis=0)
        norm_shift_part += jnp.sum(normed_grad, axis=0)
        grad_one = norm_backward(normed_grad, norm_gain, normal_one[p], inverse_one[p])
        out_bias_part += jnp.sum(grad_one, axis=0)
        attended_low = grad_one.astype(BF16)
        grads_one.append(grad_one)
        attended_lows.append(attended_low)
        context_grad = dot_nt(attended_low, whole_out).astype(BF16)
        last = context_grad
        context_grad = lax.all_to_all(
            context_grad, "tensor", split_axis=1, concat_axis=0, tiled=True
        )
        if p == packs - 1:
            last = glu_flow.step(last).sent
            last = down_flow.step(last).result
            send, keep = row_grad(
                after(jnp.concatenate(context_rows, axis=0), last),
                jnp.concatenate(attended_lows, axis=0),
                jnp.stack([1 - core, core]).astype(jnp.int32),
                out_weight.shape[0],
            )
            out_flow = Flow(out_scatter_stages(send, keep)).step()
            last = send
            shared = jnp.stack(
                [
                    out_bias_part,
                    norm_gain_part,
                    norm_shift_part,
                    down_bias_part,
                    final_gain_part,
                    final_shift_part,
                ]
            )
            glu_bias = jnp.concatenate([gate_bias_part[:, 0], up_bias_part[:, 0]])
            small_flow = Flow(
                small_stages(
                    shared,
                    (glu_bias, lambda: qkv_bias_part[:, 0, :]),
                    batch_size.bit_length() - 1,
                    tensor_size.bit_length() - 1,
                )
            ).step(send)
        else:
            down_flow.step(last)
            last = glu_flow.step(down_flow.sent, context_grad).sent
        low, bias_sum, input_part = attend_backward(
            qkvs[p], after(context_grad, last), log_sums[p], *ranges[p], *tables[p], qkv_slabs,
            LONG if p < packs - 1 else SHORT,
        )
        last = low
        lows.append(low)
        qkv_bias_part += bias_sum
        input_grads.append(
            scatter_rows(input_part).astype(F32) + scale_value * grads_one[p]
        )
        if p == packs - 1:
            last = [out_flow.step(low).sent, small_flow.step(low).sent, glu_flow.settle(low)]
        else:
            last = glu_flow.step(last).sent
    qkv_blocks = slab_grad(
        whole_tokens, [after(low, last) for low in lows], peer_blocks(batch_rank, batch_size)
    )
    qkv_flow = Flow(direct_sum_stages(qkv_blocks, batch_rank, batch_size, 1)).step()
    last = qkv_flow.sent
    flows = [down_flow, glu_flow, small_flow, out_flow, qkv_flow]
    last = glu_flow.step(last).result
    while any(flow.result is None for flow in flows):
        for flow in (out_flow, small_flow, qkv_flow, glu_flow, down_flow):
            if flow.result is None:
                flow.step(last)
                if flow.result is None:
                    last = flow.sent
    down_grad, glu_grad, (shared, glu_bias, qkv_bias_grad), out_grad, qkv_grad = [
        flow.result for flow in flows
    ]
    return (
        jnp.stack(outputs),
        jnp.stack(input_grads),
        jnp.transpose(qkv_grad, (1, 0, 2)),
        qkv_bias_grad,
        out_grad,
        shared[0],
        shared[1],
        shared[2],
        glu_grad[0].T,
        glu_bias[:columns],
        glu_grad[1].T,
        glu_bias[columns:],
        down_grad,
        shared[3],
        shared[4],
        shared[5],
    )


def solution(mesh):
    return jax.shard_map(
        functools.partial(per_device, mesh.shape["batch"], mesh.shape["tensor"]),
        mesh=mesh,
        in_specs=(
            P("batch", "tensor", None),
            P("batch", "tensor", None),
            P("batch", None),
            P("batch", None),
            P("batch", None),
            P(),
            P(None, None, "tensor"),
            P(None, "tensor"),
            P("tensor", None),
            P(),
            P(),
            P(),
            P(None, "tensor"),
            P("tensor"),
            P(None, "tensor"),
            P("tensor"),
            P("tensor", None),
            P(),
            P(),
            P(),
        ),
        out_specs=(
            P("batch", "tensor", None),
            P("batch", "tensor", None),
            P(None, None, "tensor"),
            P(None, "tensor"),
            P("tensor", None),
            P(),
            P(),
            P(),
            P(None, "tensor"),
            P("tensor"),
            P(None, "tensor"),
            P("tensor"),
            P("tensor", None),
            P(),
            P(),
            P(),
        ),
        check_vma=False,
    )
```

```python
import functools
import math

import jax
import jax.numpy as jnp
from jax import lax
from jax.experimental import pallas as pl
from jax.experimental.pallas import tpu as pltpu
from jax.sharding import PartitionSpec as P

FF_LIVE = 5461
SEGS = 4
HEAD_DIM = 128

EPSILON = 1e-05
NEG_FILL = -1e30
ROPE_BASE = 10000.0
GELU_ROOT = math.sqrt(2.0 / math.pi)
GELU_CUBIC = 0.044715
FACTOR = 1.0 / math.sqrt(HEAD_DIM)
QUERY_TILE = 512
ROW_TILE = 256
VMEM_LIMIT = 56 * 1024 * 1024
LONG = pl.CostEstimate(flops=200_000_000_000, bytes_accessed=1024, transcendentals=0)
SHORT = pl.CostEstimate(flops=1024, bytes_accessed=1024, transcendentals=0)
BF16 = jnp.bfloat16
F32 = jnp.float32


def dot_nn(a, b):
    return lax.dot_general(a, b, (((1,), (0,)), ((), ())), preferred_element_type=F32)


def dot_nt(a, b):
    return lax.dot_general(a, b, (((1,), (1,)), ((), ())), preferred_element_type=F32)


def dot_tn(a, b):
    return lax.dot_general(a, b, (((0,), (0,)), ((), ())), preferred_element_type=F32)


def attend_forward_kernel(
    x_ref, w_ref, b_ref, cos_ref, sin_ref, lo_ref, hi_ref, qkv_ref, ctx_ref, lse_ref
):
    step = pl.program_id(0)
    heads = ctx_ref.shape[1] // HEAD_DIM
    tile = x_ref.shape[0]
    rows = pl.ds(pl.multiple_of(step * tile, tile), tile)
    x = x_ref[...]
    cosine = cos_ref[rows, :]
    sine = sin_ref[rows, :]
    for part in range(3):
        projected = dot_nn(x, w_ref[part]) + b_ref[part]
        for head in range(heads):
            value = projected[:, head * HEAD_DIM : (head + 1) * HEAD_DIM]
            if part < 2:
                value = value * cosine + pltpu.roll(value, HEAD_DIM // 2, 1) * sine
            qkv_ref[part * heads + head, rows, :] = value.astype(BF16)

    @pl.when(step == pl.num_programs(0) - 1)
    def _():
        length = qkv_ref.shape[1]
        for head in range(heads):
            keys = qkv_ref[heads + head]
            values_t = qkv_ref[2 * heads + head].T

            def one_tile(index, carry):
                first = pl.multiple_of(index * QUERY_TILE, QUERY_TILE)
                queries = qkv_ref[head, pl.ds(first, QUERY_TILE), :]
                scores = dot_nt(keys, queries)
                place = lax.broadcasted_iota(jnp.int32, (length, QUERY_TILE), 0)
                seen = (place >= lo_ref[index]) & (place <= hi_ref[index])
                scores = jnp.where(seen, scores, NEG_FILL)
                top = jnp.max(scores, axis=0, keepdims=True)
                shifted = jnp.exp((scores - top) * FACTOR)
                total = jnp.sum(shifted, axis=0, keepdims=True)
                probs = (shifted * (1.0 / total)).astype(BF16)
                context_t = dot_nn(values_t, probs)
                ctx_ref[pl.ds(first, QUERY_TILE), head * HEAD_DIM : (head + 1) * HEAD_DIM] = (
                    context_t.T.astype(BF16)
                )
                lse_ref[head, index] = top * FACTOR + jnp.log(total)
                return carry

            lax.fori_loop(0, length // QUERY_TILE, one_tile, 0, unroll=True)


def attend_forward(x, w, b, cosine, sine, lo, hi):
    length, width = x.shape
    head_width = w.shape[2]
    heads = head_width // HEAD_DIM
    tiles = length // QUERY_TILE
    whole = lambda *shape: pl.BlockSpec(shape, lambda i: (0,) * len(shape))
    return pl.pallas_call(
        attend_forward_kernel,
        grid=(length // ROW_TILE,),
        in_specs=[
            pl.BlockSpec((ROW_TILE, width), lambda i: (i, 0)),
            whole(3, width, head_width),
            whole(3, 1, head_width),
            whole(length, HEAD_DIM),
            whole(length, HEAD_DIM),
            whole(tiles, 1, QUERY_TILE),
            whole(tiles, 1, QUERY_TILE),
        ],
        out_specs=[
            whole(3 * heads, length, HEAD_DIM),
            whole(length, head_width),
            whole(heads, tiles, 1, QUERY_TILE),
        ],
        out_shape=[
            jax.ShapeDtypeStruct((3 * heads, length, HEAD_DIM), BF16),
            jax.ShapeDtypeStruct((length, head_width), BF16),
            jax.ShapeDtypeStruct((heads, tiles, 1, QUERY_TILE), F32),
        ],
        compiler_params=pltpu.CompilerParams(vmem_limit_bytes=VMEM_LIMIT),
        cost_estimate=LONG,
        name="attend_forward",
    )(x, w, b, cosine, sine, lo, hi)


def attend_backward_kernel(
    qkv_ref,
    grad_ref,
    lse_ref,
    lo_ref,
    hi_ref,
    cos_ref,
    sin_ref,
    w_ref,
    low_ref,
    bias_ref,
    x_grad_ref,
    key_total,
    value_total,
):
    step = pl.program_id(0)
    length = qkv_ref.shape[1]
    heads = qkv_ref.shape[0] // 3
    tile = x_grad_ref.shape[0]

    def rope_back(grad, cosine, sine):
        return grad * cosine - pltpu.roll(grad, HEAD_DIM // 2, 1) * sine

    @pl.when(step == 0)
    def _():
        for head in range(heads):
            lanes = slice(head * HEAD_DIM, (head + 1) * HEAD_DIM)
            keys = qkv_ref[heads + head]
            keys_t = keys.T
            values = qkv_ref[2 * heads + head]
            key_total[...] = jnp.zeros_like(key_total)
            value_total[...] = jnp.zeros_like(value_total)

            def one_tile(index, query_bias):
                first = pl.multiple_of(index * QUERY_TILE, QUERY_TILE)
                rows = pl.ds(first, QUERY_TILE)
                queries = qkv_ref[head, rows, :]
                grads = grad_ref[rows, lanes]
                scores = dot_nt(keys, queries)
                place = lax.broadcasted_iota(jnp.int32, (length, QUERY_TILE), 0)
                seen = (place >= lo_ref[index]) & (place <= hi_ref[index])
                scores = jnp.where(seen, scores * FACTOR, NEG_FILL)
                probs = jnp.exp(scores - lse_ref[head, index])
                probs_grad = dot_nt(values, grads)
                delta = jnp.sum(probs * probs_grad, axis=0, keepdims=True)
                score_grad = (probs * (probs_grad - delta)).astype(BF16)
                query_grad = dot_nn(keys_t, score_grad).T * FACTOR
                key_total[...] += dot_nn(score_grad, queries)
                value_total[...] += dot_nn(probs.astype(BF16), grads)
                query_grad = rope_back(query_grad, cos_ref[rows, :], sin_ref[rows, :])
                low_ref[0, rows, lanes] = query_grad.astype(BF16)
                return query_bias + jnp.sum(query_grad, axis=0, keepdims=True)

            query_bias = lax.fori_loop(
                0, length // QUERY_TILE, one_tile, jnp.zeros((1, HEAD_DIM), F32), unroll=True
            )
            key_grad = rope_back(key_total[...] * FACTOR, cos_ref[...], sin_ref[...])
            value_grad = value_total[...]
            low_ref[1, :, lanes] = key_grad.astype(BF16)
            low_ref[2, :, lanes] = value_grad.astype(BF16)
            bias_ref[0, :, lanes] = query_bias
            bias_ref[1, :, lanes] = jnp.sum(key_grad, axis=0, keepdims=True)
            bias_ref[2, :, lanes] = jnp.sum(value_grad, axis=0, keepdims=True)

    rows = pl.ds(pl.multiple_of(step * tile, tile), tile)
    total = dot_nt(low_ref[0, rows, :], w_ref[0])
    total += dot_nt(low_ref[1, rows, :], w_ref[1])
    total += dot_nt(low_ref[2, rows, :], w_ref[2])
    x_grad_ref[...] = total.astype(BF16)


def attend_backward(qkv, grad, lse, lo, hi, cosine, sine, w, cost):
    width, head_width = w.shape[1:]
    length = grad.shape[0]
    heads = head_width // HEAD_DIM
    tiles = length // QUERY_TILE
    whole = lambda *shape: pl.BlockSpec(shape, lambda i: (0,) * len(shape))
    return pl.pallas_call(
        attend_backward_kernel,
        grid=(length // ROW_TILE,),
        in_specs=[
            whole(3 * heads, length, HEAD_DIM),
            whole(length, head_width),
            whole(heads, tiles, 1, QUERY_TILE),
            whole(tiles, 1, QUERY_TILE),
            whole(tiles, 1, QUERY_TILE),
            whole(length, HEAD_DIM),
            whole(length, HEAD_DIM),
            whole(3, width, head_width),
        ],
        out_specs=[
            whole(3, length, head_width),
            whole(3, 1, head_width),
            pl.BlockSpec((ROW_TILE, width), lambda i: (i, 0)),
        ],
        out_shape=[
            jax.ShapeDtypeStruct((3, length, head_width), BF16),
            jax.ShapeDtypeStruct((3, 1, head_width), F32),
            jax.ShapeDtypeStruct((length, width), BF16),
        ],
        scratch_shapes=[
            pltpu.VMEM((length, HEAD_DIM), F32),
            pltpu.VMEM((length, HEAD_DIM), F32),
        ],
        compiler_params=pltpu.CompilerParams(vmem_limit_bytes=VMEM_LIMIT),
        cost_estimate=cost,
        name="attend_backward",
    )(qkv, grad, lse, lo, hi, cosine, sine, w)


def glu_forward_kernel(
    live_ref, h_ref, wg_ref, wu_ref, wd_ref, bg_ref, bu_ref, act_ref, gelu_ref, slope_ref, out_ref
):
    hidden = h_ref[...]
    gate = dot_nt(wg_ref[...], hidden) + bg_ref[...]
    up = dot_nt(wu_ref[...], hidden) + bu_ref[...]
    squared = gate * gate
    tangent = jnp.tanh(GELU_ROOT * gate * (1.0 + GELU_CUBIC * squared))
    half = 0.5 * (1.0 + tangent)
    gelu = gate * half
    slope = half + 0.5 * gate * (1.0 - tangent * tangent) * GELU_ROOT * (
        1.0 + 3.0 * GELU_CUBIC * squared
    )
    column = lax.broadcasted_iota(jnp.int32, gate.shape, 0)
    activated = jnp.where(column < live_ref[0], gelu * up, 0.0).astype(BF16)
    act_ref[...] = activated
    gelu_ref[...] = gelu.astype(BF16)
    slope_ref[...] = (up * slope).astype(BF16)
    out_ref[...] = dot_tn(activated, wd_ref[...]).astype(BF16)


def glu_forward(live, hidden, wg, wu, wd, bg, bu):
    length, width = hidden.shape
    columns = wg.shape[0]
    whole = lambda *shape: pl.BlockSpec(shape, lambda i: (0,) * len(shape))
    tall = pl.BlockSpec((columns, ROW_TILE), lambda i: (0, i))
    wide = pl.BlockSpec((ROW_TILE, width), lambda i: (i, 0))
    return pl.pallas_call(
        glu_forward_kernel,
        grid=(length // ROW_TILE,),
        in_specs=[pl.BlockSpec(memory_space=pltpu.SMEM), wide]
        + [whole(columns, width)] * 3
        + [whole(columns, 1)] * 2,
        out_specs=[tall, tall, tall, wide],
        out_shape=[jax.ShapeDtypeStruct((columns, length), BF16)] * 3
        + [jax.ShapeDtypeStruct((length, width), BF16)],
        compiler_params=pltpu.CompilerParams(vmem_limit_bytes=VMEM_LIMIT),
        cost_estimate=LONG,
        name="glu_forward",
    )(live, hidden, wg, wu, wd, bg, bu)


def glu_backward_kernel(
    live_ref,
    g_ref,
    wg_ref,
    wu_ref,
    wd_ref,
    gelu_ref,
    slope_ref,
    gate_ref,
    up_ref,
    gate_bias_ref,
    up_bias_ref,
    out_ref,
    gate_sum,
    up_sum,
):
    @pl.when(pl.program_id(0) == 0)
    def _():
        gate_sum[...] = jnp.zeros_like(gate_sum)
        up_sum[...] = jnp.zeros_like(up_sum)

    grad = dot_nt(wd_ref[...], g_ref[...])
    column = lax.broadcasted_iota(jnp.int32, grad.shape, 0)
    grad = jnp.where(column < live_ref[0], grad, 0.0)
    gate_grad = grad * slope_ref[...].astype(F32)
    up_grad = grad * gelu_ref[...].astype(F32)
    for first in range(0, grad.shape[1], 128):
        gate_sum[...] += gate_grad[:, first : first + 128]
        up_sum[...] += up_grad[:, first : first + 128]

    @pl.when(pl.program_id(0) == pl.num_programs(0) - 1)
    def _():
        gate_bias_ref[...] = jnp.sum(gate_sum[...], axis=1, keepdims=True)
        up_bias_ref[...] = jnp.sum(up_sum[...], axis=1, keepdims=True)

    gate_low = gate_grad.astype(BF16)
    up_low = up_grad.astype(BF16)
    gate_ref[...] = gate_low
    up_ref[...] = up_low
    out_ref[...] = (dot_tn(gate_low, wg_ref[...]) + dot_tn(up_low, wu_ref[...])).astype(BF16)


def glu_backward(live, grad, wg, wu, wd, gelu, slope):
    length, width = grad.shape
    columns = wg.shape[0]
    whole = lambda *shape: pl.BlockSpec(shape, lambda i: (0,) * len(shape))
    tall = pl.BlockSpec((columns, ROW_TILE), lambda i: (0, i))
    wide = pl.BlockSpec((ROW_TILE, width), lambda i: (i, 0))
    return pl.pallas_call(
        glu_backward_kernel,
        grid=(length // ROW_TILE,),
        in_specs=[pl.BlockSpec(memory_space=pltpu.SMEM), wide]
        + [whole(columns, width)] * 3
        + [tall, tall],
        out_specs=[tall, tall, whole(columns, 1), whole(columns, 1), wide],
        out_shape=[jax.ShapeDtypeStruct((columns, length), BF16)] * 2
        + [jax.ShapeDtypeStruct((columns, 1), F32)] * 2
        + [jax.ShapeDtypeStruct((length, width), BF16)],
        scratch_shapes=[pltpu.VMEM((columns, 128), F32)] * 2,
        compiler_params=pltpu.CompilerParams(vmem_limit_bytes=VMEM_LIMIT),
        cost_estimate=LONG,
        name="glu_backward",
    )(live, grad, wg, wu, wd, gelu, slope)


def weight_grad_kernel(packs, outs, blocks_ref, *refs):
    lefts = refs[: packs * outs]
    rights = refs[packs * outs : packs * (outs + 1)]
    results = refs[packs * (outs + 1) :]
    for index, result in enumerate(results):

        @pl.when(pl.program_id(0) == index)
        def _():
            for out in range(outs):
                total = dot_nn(lefts[out][...], rights[0][...])
                for pack in range(1, packs):
                    total += dot_nn(lefts[pack * outs + out][...], rights[pack][...])
                result[out] = total.astype(BF16)


def weight_grad(lefts, rights, blocks):
    packs = len(rights)
    outs = len(lefts[0])
    length, width = rights[0].shape
    columns = lefts[0][0].shape[0]
    count = blocks.shape[0]
    tile = width // count
    return pl.pallas_call(
        functools.partial(weight_grad_kernel, packs, outs),
        grid_spec=pltpu.PrefetchScalarGridSpec(
            num_scalar_prefetch=1,
            grid=(count,),
            in_specs=[pl.BlockSpec((columns, length), lambda i, at: (0, 0))] * (packs * outs)
            + [pl.BlockSpec((length, tile), lambda i, at: (0, at[i]))] * packs,
            out_specs=[pl.BlockSpec((outs, columns, tile), lambda i, at: (0, 0, 0))] * count,
        ),
        out_shape=[jax.ShapeDtypeStruct((outs, columns, tile), BF16)] * count,
        compiler_params=pltpu.CompilerParams(vmem_limit_bytes=VMEM_LIMIT),
        cost_estimate=LONG,
        name="weight_grad",
    )(blocks, *[left for pack in lefts for left in pack], *rights)


def slab_grad_kernel(packs, blocks_ref, *refs):
    results = refs[2 * packs :]
    for index, result in enumerate(results):

        @pl.when(pl.program_id(0) == index)
        def _():
            for part in range(3):
                total = dot_tn(refs[0][...], refs[packs][part])
                for pack in range(1, packs):
                    total += dot_tn(refs[pack][...], refs[packs + pack][part])
                result[part] = total.astype(BF16)


def slab_grad(lefts, rights, blocks):
    packs = len(rights)
    length, width = lefts[0].shape
    columns = rights[0].shape[2]
    count = blocks.shape[0]
    tile = width // count
    return pl.pallas_call(
        functools.partial(slab_grad_kernel, packs),
        grid_spec=pltpu.PrefetchScalarGridSpec(
            num_scalar_prefetch=1,
            grid=(count,),
            in_specs=[pl.BlockSpec((length, tile), lambda i, at: (0, at[i]))] * packs
            + [pl.BlockSpec((3, length, columns), lambda i, at: (0, 0, 0))] * packs,
            out_specs=[pl.BlockSpec((3, tile, columns), lambda i, at: (0, 0, 0))] * count,
        ),
        out_shape=[jax.ShapeDtypeStruct((3, tile, columns), BF16)] * count,
        compiler_params=pltpu.CompilerParams(vmem_limit_bytes=VMEM_LIMIT),
        cost_estimate=SHORT,
        name="slab_grad",
    )(blocks, *lefts, *rights)


def row_grad_kernel(sides_ref, left_ref, right_ref, *results):
    columns = left_ref.shape[1]
    for index, result in enumerate(results):

        @pl.when(pl.program_id(0) == index)
        def _():
            rows = pl.ds(pl.multiple_of(pl.program_id(1) * columns, columns), columns)
            result[rows, :] = dot_tn(left_ref[...], right_ref[...]).astype(BF16)


def row_grad(left, right, sides, columns):
    rows, depth = left.shape
    width = right.shape[1]
    count = sides.shape[0]
    steps = depth // columns // count
    return pl.pallas_call(
        row_grad_kernel,
        grid_spec=pltpu.PrefetchScalarGridSpec(
            num_scalar_prefetch=1,
            grid=(count, steps),
            in_specs=[
                pl.BlockSpec((rows, columns), lambda i, j, at: (0, count * j + at[i])),
                pl.BlockSpec((rows, width), lambda i, j, at: (0, 0)),
            ],
            out_specs=[pl.BlockSpec((depth // count, width), lambda i, j, at: (0, 0))] * count,
        ),
        out_shape=[jax.ShapeDtypeStruct((depth // count, width), BF16)] * count,
        compiler_params=pltpu.CompilerParams(vmem_limit_bytes=VMEM_LIMIT),
        cost_estimate=SHORT,
        name="row_grad",
    )(sides, left, right)


def assemble_kernel(dim, sources_ref, *refs):
    pieces, result = refs[:-1], refs[-1]
    for index, piece in enumerate(pieces):

        @pl.when(sources_ref[pl.program_id(0)] == index)
        def _():
            result[...] = piece[...].astype(F32)


def assemble(pieces, sources, dim, cost):
    shape = pieces[0].shape
    count = len(pieces)
    whole = shape[:dim] + (shape[dim] * count,) + shape[dim + 1 :]
    zeros = (0,) * len(shape)
    place = lambda i, at: zeros[:dim] + (i,) + zeros[dim + 1 :]
    return pl.pallas_call(
        functools.partial(assemble_kernel, dim),
        grid_spec=pltpu.PrefetchScalarGridSpec(
            num_scalar_prefetch=1,
            grid=(count,),
            in_specs=[pl.BlockSpec(shape, lambda i, at: zeros)] * count,
            out_specs=pl.BlockSpec(shape, place),
        ),
        out_shape=jax.ShapeDtypeStruct(whole, F32),
        compiler_params=pltpu.CompilerParams(vmem_limit_bytes=VMEM_LIMIT),
        cost_estimate=cost,
        name="assemble",
    )(sources, *pieces)


def add_low(a, b):
    return (a.astype(F32) + b.astype(F32)).astype(BF16)


def after(x, *earlier):
    return lax.optimization_barrier((x, *jax.tree.leaves(earlier)))[0]


def all_after(xs, earlier):
    earlier = jax.tree.leaves(earlier)
    if not earlier:
        return list(xs)
    return list(lax.optimization_barrier((*xs, *earlier))[: len(xs)])


def swap_bit(x, axis_name, bit):
    size = lax.axis_size(axis_name)
    return lax.ppermute(x, axis_name, [(i, i ^ (1 << bit)) for i in range(size)])


class Flow:
    def __init__(self, chain):
        self.chain = chain
        self.result = None
        self.moving = None

    def step(self, *earlier):
        try:
            if self.moving is None:
                sends = next(self.chain)
                self.sent = all_after([x for x, _ in sends], earlier)
            else:
                sends = self.chain.send(all_after(self.moving, earlier))
                self.sent = [x for x, _ in sends]
            self.moving = [move(x) for x, (_, move) in zip(self.sent, sends)]
        except StopIteration as end:
            self.moving = None
            self.result = end.value
        return self

    def settle(self, *earlier):
        self.moving = all_after(self.moving, earlier)
        return self.moving

    def finish(self, *earlier):
        while self.result is None:
            self.step(*earlier)
            earlier = ()
        return self.result


def by_bit(bit, axis_name="batch"):
    return lambda x: swap_bit(x, axis_name, bit)


def halving_blocks(rank, orders):
    bits = [(rank >> order[0]) & 1 for order in orders]
    sends = [2 * index + 1 - bit for index, bit in enumerate(bits)]
    keeps = [2 * index + bit for index, bit in enumerate(bits)]
    return jnp.stack(sends + keeps).astype(jnp.int32)


def scatter_stages(parts, rank, orders, dim, blocks=None, axis_name="batch", first_bit=0):
    if blocks is not None:
        count = len(orders)
        got = yield [
            (block, by_bit(order[0])) for block, order in zip(blocks[:count], orders)
        ]
        parts = [add_low(keep, other) for keep, other in zip(blocks[count:], got)]
    for place in range(blocks is not None, len(orders[0])):
        keeps, sends = [], []
        for part, order in zip(parts, orders):
            half = part.shape[dim] // 2
            mine = (rank >> order[place]) & 1
            send = lax.dynamic_slice_in_dim(part, (1 - mine) * half, half, dim)
            keeps.append(lax.dynamic_slice_in_dim(part, mine * half, half, dim))
            sends.append((send, by_bit(order[place] + first_bit, axis_name)))
        parts = [add_low(keep, got) for keep, got in zip(keeps, (yield sends))]
    return parts


def gather_stages(parts, rank, orders, dim):
    for place in reversed(range(len(orders[0]))):
        sends = [(part, by_bit(order[place])) for part, order in zip(parts, orders)]
        others = yield sends
        joined = []
        for part, other, order in zip(parts, others, orders):
            mine = ((rank >> order[place]) & 1) == 1
            joined.append(
                jnp.concatenate(
                    [jnp.where(mine, other, part), jnp.where(mine, part, other)], axis=dim
                )
            )
        parts = joined
    return parts


def bit_orders(size):
    count = size.bit_length() - 1
    return [[(start + k) % count for k in range(count)] for start in range(min(count, 2))]


def cut(x, count, dim):
    size = x.shape[dim] // count
    return [lax.slice_in_dim(x, k * size, (k + 1) * size, axis=dim) for k in range(count)]


def sum_stages(blocks, rank, orders, dim, cost):
    parts = yield from scatter_stages(None, rank, orders, dim, blocks)
    parts = yield from gather_stages(parts, rank, [order[1:] for order in orders], dim)
    others = yield [(part, by_bit(order[0])) for part, order in zip(parts, orders)]
    sources = []
    for index, order in enumerate(orders):
        bit = (rank >> order[0]) & 1
        sources += [bit * len(orders) + index, (1 - bit) * len(orders) + index]
    return assemble(parts + others, jnp.stack(sources).astype(jnp.int32), dim, cost)


def to_peer(mask):
    def move(x):
        size = lax.axis_size("batch")
        return lax.ppermute(x, "batch", [(i, i ^ mask) for i in range(size)])

    return move


def peer_blocks(rank, size):
    return jnp.stack([rank ^ mask for mask in range(size)]).astype(jnp.int32)


def direct_gather_stages(piece, rank, size, dim):
    others = yield [(piece, to_peer(mask)) for mask in range(1, size)]
    return assemble([piece, *others], peer_blocks(rank, size), dim, LONG)


def direct_sum_stages(blocks, rank, size, dim):
    got = yield [(blocks[mask], to_peer(mask)) for mask in range(1, size)]
    total = blocks[0].astype(F32)
    for other in got:
        total = total + other.astype(F32)
    result = yield from direct_gather_stages(total.astype(BF16), rank, size, dim)
    return result


def small_stages(everywhere, over_batch, batch_bits, tensor_bits):
    for bit in range(tensor_bits):
        (other,) = yield [(everywhere, by_bit(bit, "tensor"))]
        everywhere = everywhere + other
    values = [everywhere, *over_batch]
    if callable(values[-1]):
        values = values[:-1] + [values[-1]()]
    for bit in range(batch_bits):
        others = yield [(value, by_bit(bit)) for value in values]
        values = [value + other for value, other in zip(values, others)]
    return values


def norm_forward(values, gain_vector, shift_vector):
    average = jnp.mean(values, axis=-1, keepdims=True)
    centred = values - average
    spread = jnp.mean(centred * centred, axis=-1, keepdims=True)
    inverse = lax.rsqrt(spread + EPSILON)
    normal = centred * inverse
    return (normal * gain_vector + shift_vector, normal, inverse)


def norm_backward(grad_rows, gain_vector, normal, inverse):
    scaled = grad_rows * gain_vector
    return inverse * (
        scaled
        - jnp.mean(scaled, axis=-1, keepdims=True)
        - normal * jnp.mean(scaled * normal, axis=-1, keepdims=True)
    )


def rotary_tables(positions):
    half_dim = HEAD_DIM // 2
    frequency = jnp.exp(
        jnp.arange(half_dim, dtype=F32) * (-2.0 * math.log(ROPE_BASE) / HEAD_DIM)
    )
    angles = positions.astype(F32)[..., None] * frequency
    cosine, sine = jnp.cos(angles), jnp.sin(angles)
    return (
        jnp.concatenate([cosine, cosine], axis=-1),
        jnp.concatenate([-sine, sine], axis=-1),
    )


def visible_range(segment, prefix):
    member = (segment[:, None] == jnp.arange(SEGS, dtype=jnp.int32)[None, :]).astype(jnp.int32)
    counts = jnp.sum(member, axis=0)
    starts = jnp.cumsum(counts) - counts
    ordinal = jnp.arange(segment.shape[0], dtype=jnp.int32)
    first = jnp.sum(member * starts[None, :], axis=1)
    seen = jnp.sum(member * jnp.minimum(prefix, counts)[None, :], axis=1)
    last = jnp.maximum(ordinal, first + seen - 1)
    tiled = (segment.shape[0] // QUERY_TILE, 1, QUERY_TILE)
    return first.reshape(tiled), last.reshape(tiled)


def per_device(
    batch_size,
    tensor_size,
    tokens,
    cotangent,
    segment_ids,
    prefix_lengths,
    rotary_positions,
    residual_scale,
    qkv_weight,
    qkv_bias,
    out_weight,
    out_bias,
    norm_gain,
    norm_shift,
    gate_weight,
    gate_bias,
    up_weight,
    up_bias,
    down_weight,
    down_bias,
    final_gain,
    final_shift,
):
    packs, local_rows, width = tokens.shape
    columns = down_weight.shape[0]
    batch_rank = lax.axis_index("batch")
    tensor_rank = lax.axis_index("tensor")
    chips = tensor_size // 2
    chip_rank = tensor_rank // 2
    core = lax.rem(tensor_rank, 2)
    first_core = core == 0
    orders = bit_orders(batch_size)
    scale_value = residual_scale[0]
    across = by_bit(0, "tensor")

    def by_core(mine, other, axis):
        return jnp.concatenate(
            [jnp.where(first_core, mine, other), jnp.where(first_core, other, mine)], axis=axis
        )

    def gather_rows(x):
        return lax.all_gather(x, "tensor", axis=0, tiled=True)

    def scatter_rows(x):
        return lax.psum_scatter(x, "tensor", scatter_dimension=0, tiled=True)

    gate_rows = gate_weight.T
    up_rows = up_weight.T
    qkv_slabs = jnp.transpose(qkv_weight, (1, 0, 2))
    qkv_bias_rows = qkv_bias[:, None, :]
    gate_bias_column = gate_bias[:, None]
    up_bias_column = up_bias[:, None]
    live = (FF_LIVE - tensor_rank * columns).astype(jnp.int32)[None]
    half = width // 2

    def own_piece(x, side):
        pieces = []
        for index, order in enumerate(orders):
            part = half // len(orders)
            piece = lax.dynamic_slice_in_dim(x, side * half + index * part, part, 1)
            for bit in order:
                size = piece.shape[1] // 2
                piece = lax.dynamic_slice_in_dim(piece, ((batch_rank >> bit) & 1) * size, size, 1)
            pieces.append(piece)
        return jnp.concatenate(pieces, axis=1)

    def out_gather_stages(piece):
        side = piece.shape[1] // 2
        piece = lax.dynamic_slice_in_dim(piece, core * side, side, 1)
        parts = yield from gather_stages(cut(piece, len(orders), 1), batch_rank, orders, 1)
        mine = jnp.concatenate(parts, axis=1)
        (other,) = yield [(mine, across)]
        return by_core(mine, other, 1)

    def out_scatter_stages(send, keep):
        (other,) = yield [(send, across)]
        total = add_low(keep, other)
        parts = yield from scatter_stages(
            cut(total, len(orders), 1), batch_rank, orders, 1
        )
        total = jnp.concatenate(parts, axis=1)
        chip_bits = list(reversed(range(chips.bit_length() - 1)))
        (total,) = yield from scatter_stages(
            [total], chip_rank, [chip_bits], 0, axis_name="tensor", first_bit=1
        )
        parts = yield from gather_stages(cut(total, len(orders), 1), batch_rank, orders, 1)
        return jnp.concatenate(parts, axis=1).astype(F32)

    tables = [rotary_tables(rotary_positions[p]) for p in range(packs)]
    ranges = [visible_range(segment_ids[p], prefix_lengths[p]) for p in range(packs)]

    out_piece = gather_rows(
        jnp.concatenate([own_piece(out_weight, 0), own_piece(out_weight, 1)], axis=1)
    )
    whole_tokens = []
    last = out_piece
    for p in range(packs):
        whole_tokens.append(gather_rows(tokens[p]))
    out_flow = Flow(out_gather_stages(out_piece))
    whole_out = out_flow.finish()
    last = whole_out

    qkvs, log_sums, context_rows = [], [], []
    normed, normal_one, inverse_one, hidden = [], [], [], []
    for p in range(packs):
        qkv, context, log_sum = attend_forward(
            after(whole_tokens[p], last), qkv_slabs, qkv_bias_rows, *tables[p], *ranges[p]
        )
        qkvs.append(qkv)
        log_sums.append(log_sum)
        context_rows.append(
            lax.all_to_all(context, "tensor", split_axis=0, concat_axis=1, tiled=True)
        )
        attended = dot_nn(context_rows[p], whole_out) + out_bias
        value, normal, inverse = norm_forward(
            scale_value * tokens[p].astype(F32) + attended, norm_gain, norm_shift
        )
        normed.append(value)
        normal_one.append(normal)
        inverse_one.append(inverse)
        last = value.astype(BF16)
        hidden.append(gather_rows(last))

    activated, gelus, slopes, branches = [], [], [], []
    for p in range(packs):
        act, gelu, slope, branch = glu_forward(
            live, after(hidden[p], last), gate_rows, up_rows, down_weight,
            gate_bias_column, up_bias_column,
        )
        activated.append(act)
        gelus.append(gelu)
        slopes.append(slope)
        branches.append(scatter_rows(branch))
        last = act

    outputs, grads_two = [], []
    final_gain_part = final_shift_part = down_bias_part = 0.0
    branch_grads = []
    for p in range(packs):
        rows, normal_two, inverse_two = norm_forward(
            scale_value * normed[p] + (after(branches[p], last).astype(F32) + down_bias),
            final_gain,
            final_shift,
        )
        outputs.append(rows.astype(BF16))
        grad_final = cotangent[p].astype(F32)
        final_gain_part += jnp.sum(grad_final * normal_two, axis=0)
        final_shift_part += jnp.sum(grad_final, axis=0)
        grad_two = norm_backward(grad_final, final_gain, normal_two, inverse_two)
        down_bias_part += jnp.sum(grad_two, axis=0)
        grads_two.append(grad_two)
        last = grad_two.astype(BF16)
        branch_grads.append(gather_rows(last))

    blocks = halving_blocks(batch_rank, orders)
    gate_lows, up_lows, normed_sums = [], [], []
    gate_bias_part = up_bias_part = 0.0
    for p in range(packs):
        if p == packs - 1:
            down_blocks = weight_grad(
                [[after(act, last)] for act in activated], branch_grads, blocks
            )
            down_flow = Flow(
                sum_stages([block[0] for block in down_blocks], batch_rank, orders, 1, LONG)
            ).step()
            last = down_flow.sent
        gate_low, up_low, gate_sum, up_sum, normed_part = glu_backward(
            live, after(branch_grads[p], last), gate_rows, up_rows, down_weight,
            gelus[p], slopes[p],
        )
        gate_lows.append(gate_low)
        up_lows.append(up_low)
        gate_bias_part += gate_sum
        up_bias_part += up_sum
        normed_sums.append(scatter_rows(normed_part))
        last = gate_low
    last = down_flow.step(last).sent
    glu_blocks = weight_grad(
        [[after(gate, last), up] for gate, up in zip(gate_lows, up_lows)], hidden, blocks
    )
    glu_flow = Flow(sum_stages(glu_blocks, batch_rank, orders, 2, SHORT)).step()
    down_flow.step(glu_flow.sent)
    last = down_flow.sent

    grads_one, attended_lows, lows, input_grads = [], [], [], []
    norm_gain_part = norm_shift_part = out_bias_part = 0.0
    qkv_bias_part = 0.0
    for p in range(packs):
        normed_grad = (
            after(normed_sums[p], last).astype(F32) + scale_value * grads_two[p]
        )
        norm_gain_part += jnp.sum(normed_grad * normal_one[p], axis=0)
        norm_shift_part += jnp.sum(normed_grad, axis=0)
        grad_one = norm_backward(normed_grad, norm_gain, normal_one[p], inverse_one[p])
        out_bias_part += jnp.sum(grad_one, axis=0)
        attended_low = grad_one.astype(BF16)
        grads_one.append(grad_one)
        attended_lows.append(attended_low)
        context_grad = dot_nt(attended_low, whole_out).astype(BF16)
        last = context_grad
        context_grad = lax.all_to_all(
            context_grad, "tensor", split_axis=1, concat_axis=0, tiled=True
        )
        if p == packs - 1:
            last = glu_flow.step(last).sent
            last = down_flow.step(last).result
            send, keep = row_grad(
                after(jnp.concatenate(context_rows, axis=0), last),
                jnp.concatenate(attended_lows, axis=0),
                jnp.stack([1 - core, core]).astype(jnp.int32),
                out_weight.shape[0],
            )
            out_flow = Flow(out_scatter_stages(send, keep)).step()
            last = send
            shared = jnp.stack(
                [
                    out_bias_part,
                    norm_gain_part,
                    norm_shift_part,
                    down_bias_part,
                    final_gain_part,
                    final_shift_part,
                ]
            )
            glu_bias = jnp.concatenate([gate_bias_part[:, 0], up_bias_part[:, 0]])
            small_flow = Flow(
                small_stages(
                    shared,
                    (glu_bias, lambda: qkv_bias_part[:, 0, :]),
                    batch_size.bit_length() - 1,
                    tensor_size.bit_length() - 1,
                )
            ).step(send)
        else:
            down_flow.step(last)
            last = glu_flow.step(down_flow.sent, context_grad).sent
        low, bias_sum, input_part = attend_backward(
            qkvs[p], after(context_grad, last), log_sums[p], *ranges[p], *tables[p], qkv_slabs,
            LONG if p < packs - 1 else SHORT,
        )
        last = low
        lows.append(low)
        qkv_bias_part += bias_sum
        input_grads.append(
            scatter_rows(input_part).astype(F32) + scale_value * grads_one[p]
        )
        if p == packs - 1:
            last = [out_flow.step(low).sent, small_flow.step(low).sent, glu_flow.settle(low)]
        else:
            last = glu_flow.step(last).sent
    qkv_blocks = slab_grad(
        whole_tokens, [after(low, last) for low in lows], peer_blocks(batch_rank, batch_size)
    )
    qkv_flow = Flow(direct_sum_stages(qkv_blocks, batch_rank, batch_size, 1)).step()
    last = qkv_flow.sent
    flows = [down_flow, glu_flow, small_flow, out_flow, qkv_flow]
    last = glu_flow.step(last).result
    while any(flow.result is None for flow in flows):
        for flow in (out_flow, small_flow, qkv_flow, small_flow, glu_flow, down_flow):
            if flow.result is None:
                flow.step(last)
                if flow.result is None:
                    last = flow.sent
    down_grad, glu_grad, (shared, glu_bias, qkv_bias_grad), out_grad, qkv_grad = [
        flow.result for flow in flows
    ]
    return (
        jnp.stack(outputs),
        jnp.stack(input_grads),
        jnp.transpose(qkv_grad, (1, 0, 2)),
        qkv_bias_grad,
        out_grad,
        shared[0],
        shared[1],
        shared[2],
        glu_grad[0].T,
        glu_bias[:columns],
        glu_grad[1].T,
        glu_bias[columns:],
        down_grad,
        shared[3],
        shared[4],
        shared[5],
    )


def solution(mesh):
    return jax.shard_map(
        functools.partial(per_device, mesh.shape["batch"], mesh.shape["tensor"]),
        mesh=mesh,
        in_specs=(
            P("batch", "tensor", None),
            P("batch", "tensor", None),
            P("batch", None),
            P("batch", None),
            P("batch", None),
            P(),
            P(None, None, "tensor"),
            P(None, "tensor"),
            P("tensor", None),
            P(),
            P(),
            P(),
            P(None, "tensor"),
            P("tensor"),
            P(None, "tensor"),
            P("tensor"),
            P("tensor", None),
            P(),
            P(),
            P(),
        ),
        out_specs=(
            P("batch", "tensor", None),
            P("batch", "tensor", None),
            P(None, None, "tensor"),
            P(None, "tensor"),
            P("tensor", None),
            P(),
            P(),
            P(),
            P(None, "tensor"),
            P("tensor"),
            P(None, "tensor"),
            P("tensor"),
            P("tensor", None),
            P(),
            P(),
            P(),
        ),
        check_vma=False,
    )
```

```python
import functools
import math

import jax
import jax.numpy as jnp
from jax import lax
from jax.experimental import pallas as pl
from jax.experimental.pallas import tpu as pltpu
from jax.sharding import PartitionSpec as P

FF_LIVE = 5461
SEGS = 4
HEAD_DIM = 128

EPSILON = 1e-05
NEG_FILL = -1e30
ROPE_BASE = 10000.0
GELU_ROOT = math.sqrt(2.0 / math.pi)
GELU_CUBIC = 0.044715
FACTOR = 1.0 / math.sqrt(HEAD_DIM)
QUERY_TILE = 512
ROW_TILE = 256
VMEM_LIMIT = 56 * 1024 * 1024
LONG = pl.CostEstimate(flops=200_000_000_000, bytes_accessed=1024, transcendentals=0)
SHORT = pl.CostEstimate(flops=1024, bytes_accessed=1024, transcendentals=0)
MIDDLE = pl.CostEstimate(flops=25_000_000_000, bytes_accessed=1024, transcendentals=0)
BF16 = jnp.bfloat16
F32 = jnp.float32


def dot_nn(a, b):
    return lax.dot_general(a, b, (((1,), (0,)), ((), ())), preferred_element_type=F32)


def dot_nt(a, b):
    return lax.dot_general(a, b, (((1,), (1,)), ((), ())), preferred_element_type=F32)


def dot_tn(a, b):
    return lax.dot_general(a, b, (((0,), (0,)), ((), ())), preferred_element_type=F32)


def attend_forward_kernel(
    x_ref, w_ref, b_ref, cos_ref, sin_ref, lo_ref, hi_ref, qkv_ref, ctx_ref, lse_ref
):
    step = pl.program_id(0)
    heads = ctx_ref.shape[1] // HEAD_DIM
    tile = x_ref.shape[0]
    rows = pl.ds(pl.multiple_of(step * tile, tile), tile)
    x = x_ref[...]
    cosine = cos_ref[rows, :]
    sine = sin_ref[rows, :]
    for part in range(3):
        projected = dot_nn(x, w_ref[part]) + b_ref[part]
        for head in range(heads):
            value = projected[:, head * HEAD_DIM : (head + 1) * HEAD_DIM]
            if part < 2:
                value = value * cosine + pltpu.roll(value, HEAD_DIM // 2, 1) * sine
            qkv_ref[part * heads + head, rows, :] = value.astype(BF16)

    @pl.when(step == pl.num_programs(0) - 1)
    def _():
        length = qkv_ref.shape[1]
        for head in range(heads):
            keys = qkv_ref[heads + head]
            values_t = qkv_ref[2 * heads + head].T

            def one_tile(index, carry):
                first = pl.multiple_of(index * QUERY_TILE, QUERY_TILE)
                queries = qkv_ref[head, pl.ds(first, QUERY_TILE), :]
                scores = dot_nt(keys, queries)
                place = lax.broadcasted_iota(jnp.int32, (length, QUERY_TILE), 0)
                seen = (place >= lo_ref[index]) & (place <= hi_ref[index])
                scores = jnp.where(seen, scores, NEG_FILL)
                top = jnp.max(scores, axis=0, keepdims=True)
                shifted = jnp.exp((scores - top) * FACTOR)
                total = jnp.sum(shifted, axis=0, keepdims=True)
                probs = (shifted * (1.0 / total)).astype(BF16)
                context_t = dot_nn(values_t, probs)
                ctx_ref[pl.ds(first, QUERY_TILE), head * HEAD_DIM : (head + 1) * HEAD_DIM] = (
                    context_t.T.astype(BF16)
                )
                lse_ref[head, index] = top * FACTOR + jnp.log(total)
                return carry

            lax.fori_loop(0, length // QUERY_TILE, one_tile, 0, unroll=True)


def attend_forward(x, w, b, cosine, sine, lo, hi):
    length, width = x.shape
    head_width = w.shape[2]
    heads = head_width // HEAD_DIM
    tiles = length // QUERY_TILE
    whole = lambda *shape: pl.BlockSpec(shape, lambda i: (0,) * len(shape))
    return pl.pallas_call(
        attend_forward_kernel,
        grid=(length // ROW_TILE,),
        in_specs=[
            pl.BlockSpec((ROW_TILE, width), lambda i: (i, 0)),
            whole(3, width, head_width),
            whole(3, 1, head_width),
            whole(length, HEAD_DIM),
            whole(length, HEAD_DIM),
            whole(tiles, 1, QUERY_TILE),
            whole(tiles, 1, QUERY_TILE),
        ],
        out_specs=[
            whole(3 * heads, length, HEAD_DIM),
            whole(length, head_width),
            whole(heads, tiles, 1, QUERY_TILE),
        ],
        out_shape=[
            jax.ShapeDtypeStruct((3 * heads, length, HEAD_DIM), BF16),
            jax.ShapeDtypeStruct((length, head_width), BF16),
            jax.ShapeDtypeStruct((heads, tiles, 1, QUERY_TILE), F32),
        ],
        compiler_params=pltpu.CompilerParams(vmem_limit_bytes=VMEM_LIMIT),
        cost_estimate=LONG,
        name="attend_forward",
    )(x, w, b, cosine, sine, lo, hi)


def attend_backward_kernel(
    qkv_ref,
    grad_ref,
    lse_ref,
    lo_ref,
    hi_ref,
    cos_ref,
    sin_ref,
    w_ref,
    low_ref,
    bias_ref,
    x_grad_ref,
    key_total,
    value_total,
):
    step = pl.program_id(0)
    length = qkv_ref.shape[1]
    heads = qkv_ref.shape[0] // 3
    tile = x_grad_ref.shape[0]

    def rope_back(grad, cosine, sine):
        return grad * cosine - pltpu.roll(grad, HEAD_DIM // 2, 1) * sine

    @pl.when(step == 0)
    def _():
        for head in range(heads):
            lanes = slice(head * HEAD_DIM, (head + 1) * HEAD_DIM)
            keys = qkv_ref[heads + head]
            keys_t = keys.T
            values = qkv_ref[2 * heads + head]
            key_total[...] = jnp.zeros_like(key_total)
            value_total[...] = jnp.zeros_like(value_total)

            def one_tile(index, query_bias):
                first = pl.multiple_of(index * QUERY_TILE, QUERY_TILE)
                rows = pl.ds(first, QUERY_TILE)
                queries = qkv_ref[head, rows, :]
                grads = grad_ref[rows, lanes]
                scores = dot_nt(keys, queries)
                place = lax.broadcasted_iota(jnp.int32, (length, QUERY_TILE), 0)
                seen = (place >= lo_ref[index]) & (place <= hi_ref[index])
                scores = jnp.where(seen, scores * FACTOR, NEG_FILL)
                probs = jnp.exp(scores - lse_ref[head, index])
                probs_grad = dot_nt(values, grads)
                delta = jnp.sum(probs * probs_grad, axis=0, keepdims=True)
                score_grad = (probs * (probs_grad - delta)).astype(BF16)
                query_grad = dot_nn(keys_t, score_grad).T * FACTOR
                key_total[...] += dot_nn(score_grad, queries)
                value_total[...] += dot_nn(probs.astype(BF16), grads)
                query_grad = rope_back(query_grad, cos_ref[rows, :], sin_ref[rows, :])
                low_ref[0, rows, lanes] = query_grad.astype(BF16)
                return query_bias + jnp.sum(query_grad, axis=0, keepdims=True)

            query_bias = lax.fori_loop(
                0, length // QUERY_TILE, one_tile, jnp.zeros((1, HEAD_DIM), F32), unroll=True
            )
            key_grad = rope_back(key_total[...] * FACTOR, cos_ref[...], sin_ref[...])
            value_grad = value_total[...]
            low_ref[1, :, lanes] = key_grad.astype(BF16)
            low_ref[2, :, lanes] = value_grad.astype(BF16)
            bias_ref[0, :, lanes] = query_bias
            bias_ref[1, :, lanes] = jnp.sum(key_grad, axis=0, keepdims=True)
            bias_ref[2, :, lanes] = jnp.sum(value_grad, axis=0, keepdims=True)

    rows = pl.ds(pl.multiple_of(step * tile, tile), tile)
    total = dot_nt(low_ref[0, rows, :], w_ref[0])
    total += dot_nt(low_ref[1, rows, :], w_ref[1])
    total += dot_nt(low_ref[2, rows, :], w_ref[2])
    x_grad_ref[...] = total.astype(BF16)


def attend_backward(qkv, grad, lse, lo, hi, cosine, sine, w, cost):
    width, head_width = w.shape[1:]
    length = grad.shape[0]
    heads = head_width // HEAD_DIM
    tiles = length // QUERY_TILE
    whole = lambda *shape: pl.BlockSpec(shape, lambda i: (0,) * len(shape))
    return pl.pallas_call(
        attend_backward_kernel,
        grid=(length // ROW_TILE,),
        in_specs=[
            whole(3 * heads, length, HEAD_DIM),
            whole(length, head_width),
            whole(heads, tiles, 1, QUERY_TILE),
            whole(tiles, 1, QUERY_TILE),
            whole(tiles, 1, QUERY_TILE),
            whole(length, HEAD_DIM),
            whole(length, HEAD_DIM),
            whole(3, width, head_width),
        ],
        out_specs=[
            whole(3, length, head_width),
            whole(3, 1, head_width),
            pl.BlockSpec((ROW_TILE, width), lambda i: (i, 0)),
        ],
        out_shape=[
            jax.ShapeDtypeStruct((3, length, head_width), BF16),
            jax.ShapeDtypeStruct((3, 1, head_width), F32),
            jax.ShapeDtypeStruct((length, width), BF16),
        ],
        scratch_shapes=[
            pltpu.VMEM((length, HEAD_DIM), F32),
            pltpu.VMEM((length, HEAD_DIM), F32),
        ],
        compiler_params=pltpu.CompilerParams(vmem_limit_bytes=VMEM_LIMIT),
        cost_estimate=cost,
        name="attend_backward",
    )(qkv, grad, lse, lo, hi, cosine, sine, w)


def glu_forward_kernel(
    live_ref, h_ref, wg_ref, wu_ref, wd_ref, bg_ref, bu_ref, act_ref, gelu_ref, slope_ref, out_ref
):
    hidden = h_ref[...]
    gate = dot_nt(wg_ref[...], hidden) + bg_ref[...]
    up = dot_nt(wu_ref[...], hidden) + bu_ref[...]
    squared = gate * gate
    tangent = jnp.tanh(GELU_ROOT * gate * (1.0 + GELU_CUBIC * squared))
    half = 0.5 * (1.0 + tangent)
    gelu = gate * half
    slope = half + 0.5 * gate * (1.0 - tangent * tangent) * GELU_ROOT * (
        1.0 + 3.0 * GELU_CUBIC * squared
    )
    column = lax.broadcasted_iota(jnp.int32, gate.shape, 0)
    activated = jnp.where(column < live_ref[0], gelu * up, 0.0).astype(BF16)
    act_ref[...] = activated
    gelu_ref[...] = gelu.astype(BF16)
    slope_ref[...] = (up * slope).astype(BF16)
    out_ref[...] = dot_tn(activated, wd_ref[...]).astype(BF16)


def glu_forward(live, hidden, wg, wu, wd, bg, bu):
    length, width = hidden.shape
    columns = wg.shape[0]
    whole = lambda *shape: pl.BlockSpec(shape, lambda i: (0,) * len(shape))
    tall = pl.BlockSpec((columns, ROW_TILE), lambda i: (0, i))
    wide = pl.BlockSpec((ROW_TILE, width), lambda i: (i, 0))
    return pl.pallas_call(
        glu_forward_kernel,
        grid=(length // ROW_TILE,),
        in_specs=[pl.BlockSpec(memory_space=pltpu.SMEM), wide]
        + [whole(columns, width)] * 3
        + [whole(columns, 1)] * 2,
        out_specs=[tall, tall, tall, wide],
        out_shape=[jax.ShapeDtypeStruct((columns, length), BF16)] * 3
        + [jax.ShapeDtypeStruct((length, width), BF16)],
        compiler_params=pltpu.CompilerParams(vmem_limit_bytes=VMEM_LIMIT),
        cost_estimate=LONG,
        name="glu_forward",
    )(live, hidden, wg, wu, wd, bg, bu)


def glu_backward_kernel(
    live_ref,
    g_ref,
    wg_ref,
    wu_ref,
    wd_ref,
    gelu_ref,
    slope_ref,
    gate_ref,
    up_ref,
    gate_bias_ref,
    up_bias_ref,
    out_ref,
    gate_sum,
    up_sum,
):
    @pl.when(pl.program_id(0) == 0)
    def _():
        gate_sum[...] = jnp.zeros_like(gate_sum)
        up_sum[...] = jnp.zeros_like(up_sum)

    grad = dot_nt(wd_ref[...], g_ref[...])
    column = lax.broadcasted_iota(jnp.int32, grad.shape, 0)
    grad = jnp.where(column < live_ref[0], grad, 0.0)
    gate_grad = grad * slope_ref[...].astype(F32)
    up_grad = grad * gelu_ref[...].astype(F32)
    for first in range(0, grad.shape[1], 128):
        gate_sum[...] += gate_grad[:, first : first + 128]
        up_sum[...] += up_grad[:, first : first + 128]

    @pl.when(pl.program_id(0) == pl.num_programs(0) - 1)
    def _():
        gate_bias_ref[...] = jnp.sum(gate_sum[...], axis=1, keepdims=True)
        up_bias_ref[...] = jnp.sum(up_sum[...], axis=1, keepdims=True)

    gate_low = gate_grad.astype(BF16)
    up_low = up_grad.astype(BF16)
    gate_ref[...] = gate_low
    up_ref[...] = up_low
    out_ref[...] = (dot_tn(gate_low, wg_ref[...]) + dot_tn(up_low, wu_ref[...])).astype(BF16)


def glu_backward(live, grad, wg, wu, wd, gelu, slope):
    length, width = grad.shape
    columns = wg.shape[0]
    whole = lambda *shape: pl.BlockSpec(shape, lambda i: (0,) * len(shape))
    tall = pl.BlockSpec((columns, ROW_TILE), lambda i: (0, i))
    wide = pl.BlockSpec((ROW_TILE, width), lambda i: (i, 0))
    return pl.pallas_call(
        glu_backward_kernel,
        grid=(length // ROW_TILE,),
        in_specs=[pl.BlockSpec(memory_space=pltpu.SMEM), wide]
        + [whole(columns, width)] * 3
        + [tall, tall],
        out_specs=[tall, tall, whole(columns, 1), whole(columns, 1), wide],
        out_shape=[jax.ShapeDtypeStruct((columns, length), BF16)] * 2
        + [jax.ShapeDtypeStruct((columns, 1), F32)] * 2
        + [jax.ShapeDtypeStruct((length, width), BF16)],
        scratch_shapes=[pltpu.VMEM((columns, 128), F32)] * 2,
        compiler_params=pltpu.CompilerParams(vmem_limit_bytes=VMEM_LIMIT),
        cost_estimate=LONG,
        name="glu_backward",
    )(live, grad, wg, wu, wd, gelu, slope)


def weight_grad_kernel(packs, outs, blocks_ref, *refs):
    lefts = refs[: packs * outs]
    rights = refs[packs * outs : packs * (outs + 1)]
    results = refs[packs * (outs + 1) :]
    for index, result in enumerate(results):

        @pl.when(pl.program_id(0) == index)
        def _():
            for out in range(outs):
                total = dot_nn(lefts[out][...], rights[0][...])
                for pack in range(1, packs):
                    total += dot_nn(lefts[pack * outs + out][...], rights[pack][...])
                result[out] = total.astype(BF16)


def weight_grad(lefts, rights, blocks):
    packs = len(rights)
    outs = len(lefts[0])
    length, width = rights[0].shape
    columns = lefts[0][0].shape[0]
    count = blocks.shape[0]
    tile = width // count
    return pl.pallas_call(
        functools.partial(weight_grad_kernel, packs, outs),
        grid_spec=pltpu.PrefetchScalarGridSpec(
            num_scalar_prefetch=1,
            grid=(count,),
            in_specs=[pl.BlockSpec((columns, length), lambda i, at: (0, 0))] * (packs * outs)
            + [pl.BlockSpec((length, tile), lambda i, at: (0, at[i]))] * packs,
            out_specs=[pl.BlockSpec((outs, columns, tile), lambda i, at: (0, 0, 0))] * count,
        ),
        out_shape=[jax.ShapeDtypeStruct((outs, columns, tile), BF16)] * count,
        compiler_params=pltpu.CompilerParams(vmem_limit_bytes=VMEM_LIMIT),
        cost_estimate=LONG,
        name="weight_grad",
    )(blocks, *[left for pack in lefts for left in pack], *rights)


def slab_grad_kernel(packs, blocks_ref, *refs):
    results = refs[2 * packs :]
    for index, result in enumerate(results):

        @pl.when(pl.program_id(0) == index)
        def _():
            for part in range(3):
                total = dot_tn(refs[0][...], refs[packs][part])
                for pack in range(1, packs):
                    total += dot_tn(refs[pack][...], refs[packs + pack][part])
                result[part] = total.astype(BF16)


def slab_grad(lefts, rights, blocks):
    packs = len(rights)
    length, width = lefts[0].shape
    columns = rights[0].shape[2]
    count = blocks.shape[0]
    tile = width // count
    return pl.pallas_call(
        functools.partial(slab_grad_kernel, packs),
        grid_spec=pltpu.PrefetchScalarGridSpec(
            num_scalar_prefetch=1,
            grid=(count,),
            in_specs=[pl.BlockSpec((length, tile), lambda i, at: (0, at[i]))] * packs
            + [pl.BlockSpec((3, length, columns), lambda i, at: (0, 0, 0))] * packs,
            out_specs=[pl.BlockSpec((3, tile, columns), lambda i, at: (0, 0, 0))] * count,
        ),
        out_shape=[jax.ShapeDtypeStruct((3, tile, columns), BF16)] * count,
        compiler_params=pltpu.CompilerParams(vmem_limit_bytes=VMEM_LIMIT),
        cost_estimate=LONG,
        name="slab_grad",
    )(blocks, *lefts, *rights)


def row_grad_kernel(sides_ref, left_ref, right_ref, *results):
    columns = left_ref.shape[1]
    for index, result in enumerate(results):

        @pl.when(pl.program_id(0) == index)
        def _():
            rows = pl.ds(pl.multiple_of(pl.program_id(1) * columns, columns), columns)
            result[rows, :] = dot_tn(left_ref[...], right_ref[...]).astype(BF16)


def row_grad(left, right, sides, columns):
    rows, depth = left.shape
    width = right.shape[1]
    count = sides.shape[0]
    steps = depth // columns // count
    return pl.pallas_call(
        row_grad_kernel,
        grid_spec=pltpu.PrefetchScalarGridSpec(
            num_scalar_prefetch=1,
            grid=(count, steps),
            in_specs=[
                pl.BlockSpec((rows, columns), lambda i, j, at: (0, count * j + at[i])),
                pl.BlockSpec((rows, width), lambda i, j, at: (0, 0)),
            ],
            out_specs=[pl.BlockSpec((depth // count, width), lambda i, j, at: (0, 0))] * count,
        ),
        out_shape=[jax.ShapeDtypeStruct((depth // count, width), BF16)] * count,
        compiler_params=pltpu.CompilerParams(vmem_limit_bytes=VMEM_LIMIT),
        cost_estimate=SHORT,
        name="row_grad",
    )(sides, left, right)


def assemble_kernel(dim, sources_ref, *refs):
    pieces, result = refs[:-1], refs[-1]
    for index, piece in enumerate(pieces):

        @pl.when(sources_ref[pl.program_id(0)] == index)
        def _():
            result[...] = piece[...].astype(F32)


def assemble(pieces, sources, dim, cost):
    shape = pieces[0].shape
    count = len(pieces)
    whole = shape[:dim] + (shape[dim] * count,) + shape[dim + 1 :]
    zeros = (0,) * len(shape)
    place = lambda i, at: zeros[:dim] + (i,) + zeros[dim + 1 :]
    return pl.pallas_call(
        functools.partial(assemble_kernel, dim),
        grid_spec=pltpu.PrefetchScalarGridSpec(
            num_scalar_prefetch=1,
            grid=(count,),
            in_specs=[pl.BlockSpec(shape, lambda i, at: zeros)] * count,
            out_specs=pl.BlockSpec(shape, place),
        ),
        out_shape=jax.ShapeDtypeStruct(whole, F32),
        compiler_params=pltpu.CompilerParams(vmem_limit_bytes=VMEM_LIMIT),
        cost_estimate=cost,
        name="assemble",
    )(sources, *pieces)


def add_low(a, b):
    return (a.astype(F32) + b.astype(F32)).astype(BF16)


def after(x, *earlier):
    return lax.optimization_barrier((x, *jax.tree.leaves(earlier)))[0]


def all_after(xs, earlier):
    earlier = jax.tree.leaves(earlier)
    if not earlier:
        return list(xs)
    return list(lax.optimization_barrier((*xs, *earlier))[: len(xs)])


def swap_bit(x, axis_name, bit):
    size = lax.axis_size(axis_name)
    return lax.ppermute(x, axis_name, [(i, i ^ (1 << bit)) for i in range(size)])


class Flow:
    def __init__(self, chain):
        self.chain = chain
        self.result = None
        self.moving = None

    def step(self, *earlier):
        try:
            if self.moving is None:
                sends = next(self.chain)
                self.sent = all_after([x for x, _ in sends], earlier)
            else:
                sends = self.chain.send(all_after(self.moving, earlier))
                self.sent = [x for x, _ in sends]
            self.moving = [move(x) for x, (_, move) in zip(self.sent, sends)]
        except StopIteration as end:
            self.moving = None
            self.result = end.value
        return self

    def settle(self, *earlier):
        self.moving = all_after(self.moving, earlier)
        return self.moving

    def finish(self, *earlier):
        while self.result is None:
            self.step(*earlier)
            earlier = ()
        return self.result


def by_bit(bit, axis_name="batch"):
    return lambda x: swap_bit(x, axis_name, bit)


def halving_blocks(rank, orders):
    bits = [(rank >> order[0]) & 1 for order in orders]
    sends = [2 * index + 1 - bit for index, bit in enumerate(bits)]
    keeps = [2 * index + bit for index, bit in enumerate(bits)]
    return jnp.stack(sends + keeps).astype(jnp.int32)


def scatter_stages(parts, rank, orders, dim, blocks=None, axis_name="batch", first_bit=0):
    if blocks is not None:
        count = len(orders)
        got = yield [
            (block, by_bit(order[0])) for block, order in zip(blocks[:count], orders)
        ]
        parts = [add_low(keep, other) for keep, other in zip(blocks[count:], got)]
    for place in range(blocks is not None, len(orders[0])):
        keeps, sends = [], []
        for part, order in zip(parts, orders):
            half = part.shape[dim] // 2
            mine = (rank >> order[place]) & 1
            send = lax.dynamic_slice_in_dim(part, (1 - mine) * half, half, dim)
            keeps.append(lax.dynamic_slice_in_dim(part, mine * half, half, dim))
            sends.append((send, by_bit(order[place] + first_bit, axis_name)))
        parts = [add_low(keep, got) for keep, got in zip(keeps, (yield sends))]
    return parts


def gather_stages(parts, rank, orders, dim):
    for place in reversed(range(len(orders[0]))):
        sends = [(part, by_bit(order[place])) for part, order in zip(parts, orders)]
        others = yield sends
        joined = []
        for part, other, order in zip(parts, others, orders):
            mine = ((rank >> order[place]) & 1) == 1
            joined.append(
                jnp.concatenate(
                    [jnp.where(mine, other, part), jnp.where(mine, part, other)], axis=dim
                )
            )
        parts = joined
    return parts


def bit_orders(size):
    count = size.bit_length() - 1
    return [[(start + k) % count for k in range(count)] for start in range(min(count, 2))]


def cut(x, count, dim):
    size = x.shape[dim] // count
    return [lax.slice_in_dim(x, k * size, (k + 1) * size, axis=dim) for k in range(count)]


def sum_stages(blocks, rank, orders, dim, cost):
    parts = yield from scatter_stages(None, rank, orders, dim, blocks)
    parts = yield from gather_stages(parts, rank, [order[1:] for order in orders], dim)
    others = yield [(part, by_bit(order[0])) for part, order in zip(parts, orders)]
    sources = []
    for index, order in enumerate(orders):
        bit = (rank >> order[0]) & 1
        sources += [bit * len(orders) + index, (1 - bit) * len(orders) + index]
    return assemble(parts + others, jnp.stack(sources).astype(jnp.int32), dim, cost)


def to_peer(mask):
    def move(x):
        size = lax.axis_size("batch")
        return lax.ppermute(x, "batch", [(i, i ^ mask) for i in range(size)])

    return move


def peer_blocks(rank, size):
    return jnp.stack([rank ^ mask for mask in range(size)]).astype(jnp.int32)


def direct_gather_stages(piece, rank, size, dim):
    others = yield [(piece, to_peer(mask)) for mask in range(1, size)]
    return assemble([piece, *others], peer_blocks(rank, size), dim, LONG)


def direct_sum_stages(blocks, rank, size, dim):
    got = yield [(blocks[mask], to_peer(mask)) for mask in range(1, size)]
    total = blocks[0].astype(F32)
    for other in got:
        total = total + other.astype(F32)
    result = yield from direct_gather_stages(total.astype(BF16), rank, size, dim)
    return result


def small_stages(everywhere, over_batch, batch_bits, tensor_bits):
    for bit in range(tensor_bits):
        (other,) = yield [(everywhere, by_bit(bit, "tensor"))]
        everywhere = everywhere + other
    values = [everywhere, *over_batch]
    if callable(values[-1]):
        values = values[:-1] + [values[-1]()]
    for bit in range(batch_bits):
        others = yield [(value, by_bit(bit)) for value in values]
        values = [value + other for value, other in zip(values, others)]
    return values


def norm_forward(values, gain_vector, shift_vector):
    average = jnp.mean(values, axis=-1, keepdims=True)
    centred = values - average
    spread = jnp.mean(centred * centred, axis=-1, keepdims=True)
    inverse = lax.rsqrt(spread + EPSILON)
    normal = centred * inverse
    return (normal * gain_vector + shift_vector, normal, inverse)


def norm_backward(grad_rows, gain_vector, normal, inverse):
    scaled = grad_rows * gain_vector
    return inverse * (
        scaled
        - jnp.mean(scaled, axis=-1, keepdims=True)
        - normal * jnp.mean(scaled * normal, axis=-1, keepdims=True)
    )


def rotary_tables(positions):
    half_dim = HEAD_DIM // 2
    frequency = jnp.exp(
        jnp.arange(half_dim, dtype=F32) * (-2.0 * math.log(ROPE_BASE) / HEAD_DIM)
    )
    angles = positions.astype(F32)[..., None] * frequency
    cosine, sine = jnp.cos(angles), jnp.sin(angles)
    return (
        jnp.concatenate([cosine, cosine], axis=-1),
        jnp.concatenate([-sine, sine], axis=-1),
    )


def visible_range(segment, prefix):
    member = (segment[:, None] == jnp.arange(SEGS, dtype=jnp.int32)[None, :]).astype(jnp.int32)
    counts = jnp.sum(member, axis=0)
    starts = jnp.cumsum(counts) - counts
    ordinal = jnp.arange(segment.shape[0], dtype=jnp.int32)
    first = jnp.sum(member * starts[None, :], axis=1)
    seen = jnp.sum(member * jnp.minimum(prefix, counts)[None, :], axis=1)
    last = jnp.maximum(ordinal, first + seen - 1)
    tiled = (segment.shape[0] // QUERY_TILE, 1, QUERY_TILE)
    return first.reshape(tiled), last.reshape(tiled)


def per_device(
    batch_size,
    tensor_size,
    tokens,
    cotangent,
    segment_ids,
    prefix_lengths,
    rotary_positions,
    residual_scale,
    qkv_weight,
    qkv_bias,
    out_weight,
    out_bias,
    norm_gain,
    norm_shift,
    gate_weight,
    gate_bias,
    up_weight,
    up_bias,
    down_weight,
    down_bias,
    final_gain,
    final_shift,
):
    packs, local_rows, width = tokens.shape
    columns = down_weight.shape[0]
    batch_rank = lax.axis_index("batch")
    tensor_rank = lax.axis_index("tensor")
    chips = tensor_size // 2
    chip_rank = tensor_rank // 2
    core = lax.rem(tensor_rank, 2)
    first_core = core == 0
    orders = bit_orders(batch_size)
    scale_value = residual_scale[0]
    across = by_bit(0, "tensor")

    def by_core(mine, other, axis):
        return jnp.concatenate(
            [jnp.where(first_core, mine, other), jnp.where(first_core, other, mine)], axis=axis
        )

    def gather_rows(x):
        return lax.all_gather(x, "tensor", axis=0, tiled=True)

    def scatter_rows(x):
        return lax.psum_scatter(x, "tensor", scatter_dimension=0, tiled=True)

    gate_rows = gate_weight.T
    up_rows = up_weight.T
    qkv_slabs = jnp.transpose(qkv_weight, (1, 0, 2))
    qkv_bias_rows = qkv_bias[:, None, :]
    gate_bias_column = gate_bias[:, None]
    up_bias_column = up_bias[:, None]
    live = (FF_LIVE - tensor_rank * columns).astype(jnp.int32)[None]
    half = width // 2

    def own_piece(x, side):
        pieces = []
        for index, order in enumerate(orders):
            part = half // len(orders)
            piece = lax.dynamic_slice_in_dim(x, side * half + index * part, part, 1)
            for bit in order:
                size = piece.shape[1] // 2
                piece = lax.dynamic_slice_in_dim(piece, ((batch_rank >> bit) & 1) * size, size, 1)
            pieces.append(piece)
        return jnp.concatenate(pieces, axis=1)

    def out_gather_stages(piece):
        side = piece.shape[1] // 2
        piece = lax.dynamic_slice_in_dim(piece, core * side, side, 1)
        parts = yield from gather_stages(cut(piece, len(orders), 1), batch_rank, orders, 1)
        mine = jnp.concatenate(parts, axis=1)
        (other,) = yield [(mine, across)]
        return by_core(mine, other, 1)

    def out_scatter_stages(send, keep):
        (other,) = yield [(send, across)]
        total = add_low(keep, other)
        parts = yield from scatter_stages(
            cut(total, len(orders), 1), batch_rank, orders, 1
        )
        total = jnp.concatenate(parts, axis=1)
        chip_bits = list(reversed(range(chips.bit_length() - 1)))
        (total,) = yield from scatter_stages(
            [total], chip_rank, [chip_bits], 0, axis_name="tensor", first_bit=1
        )
        parts = yield from gather_stages(cut(total, len(orders), 1), batch_rank, orders, 1)
        return jnp.concatenate(parts, axis=1).astype(F32)

    tables = [rotary_tables(rotary_positions[p]) for p in range(packs)]
    ranges = [visible_range(segment_ids[p], prefix_lengths[p]) for p in range(packs)]

    out_piece = gather_rows(
        jnp.concatenate([own_piece(out_weight, 0), own_piece(out_weight, 1)], axis=1)
    )
    whole_tokens = []
    last = out_piece
    for p in range(packs):
        whole_tokens.append(gather_rows(tokens[p]))
    out_flow = Flow(out_gather_stages(out_piece))
    whole_out = out_flow.finish()
    last = whole_out

    qkvs, log_sums, context_rows = [], [], []
    normed, normal_one, inverse_one, hidden = [], [], [], []
    for p in range(packs):
        qkv, context, log_sum = attend_forward(
            after(whole_tokens[p], last), qkv_slabs, qkv_bias_rows, *tables[p], *ranges[p]
        )
        qkvs.append(qkv)
        log_sums.append(log_sum)
        context_rows.append(
            lax.all_to_all(context, "tensor", split_axis=0, concat_axis=1, tiled=True)
        )
        attended = dot_nn(context_rows[p], whole_out) + out_bias
        value, normal, inverse = norm_forward(
            scale_value * tokens[p].astype(F32) + attended, norm_gain, norm_shift
        )
        normed.append(value)
        normal_one.append(normal)
        inverse_one.append(inverse)
        last = value.astype(BF16)
        hidden.append(gather_rows(last))

    activated, gelus, slopes, branches = [], [], [], []
    for p in range(packs):
        act, gelu, slope, branch = glu_forward(
            live, after(hidden[p], last), gate_rows, up_rows, down_weight,
            gate_bias_column, up_bias_column,
        )
        activated.append(act)
        gelus.append(gelu)
        slopes.append(slope)
        branches.append(scatter_rows(branch))
        last = act

    outputs, grads_two = [], []
    final_gain_part = final_shift_part = down_bias_part = 0.0
    branch_grads = []
    for p in range(packs):
        rows, normal_two, inverse_two = norm_forward(
            scale_value * normed[p] + (after(branches[p], last).astype(F32) + down_bias),
            final_gain,
            final_shift,
        )
        outputs.append(rows.astype(BF16))
        grad_final = cotangent[p].astype(F32)
        final_gain_part += jnp.sum(grad_final * normal_two, axis=0)
        final_shift_part += jnp.sum(grad_final, axis=0)
        grad_two = norm_backward(grad_final, final_gain, normal_two, inverse_two)
        down_bias_part += jnp.sum(grad_two, axis=0)
        grads_two.append(grad_two)
        last = grad_two.astype(BF16)
        branch_grads.append(gather_rows(last))

    blocks = halving_blocks(batch_rank, orders)
    gate_lows, up_lows, normed_sums = [], [], []
    gate_bias_part = up_bias_part = 0.0
    for p in range(packs):
        if p == packs - 1:
            down_blocks = weight_grad(
                [[after(act, last)] for act in activated], branch_grads, blocks
            )
            down_flow = Flow(
                sum_stages([block[0] for block in down_blocks], batch_rank, orders, 1, LONG)
            ).step()
            last = down_flow.sent
        gate_low, up_low, gate_sum, up_sum, normed_part = glu_backward(
            live, after(branch_grads[p], last), gate_rows, up_rows, down_weight,
            gelus[p], slopes[p],
        )
        gate_lows.append(gate_low)
        up_lows.append(up_low)
        gate_bias_part += gate_sum
        up_bias_part += up_sum
        normed_sums.append(scatter_rows(normed_part))
        last = gate_low
    last = down_flow.step(last).sent
    glu_blocks = weight_grad(
        [[after(gate, last), up] for gate, up in zip(gate_lows, up_lows)], hidden, blocks
    )
    glu_flow = Flow(sum_stages(glu_blocks, batch_rank, orders, 2, LONG)).step()
    down_flow.step(glu_flow.sent)
    last = down_flow.sent

    grads_one, attended_lows, context_grads = [], [], []
    norm_gain_part = norm_shift_part = out_bias_part = 0.0
    for p in range(packs):
        normed_grad = (
            after(normed_sums[p], last).astype(F32) + scale_value * grads_two[p]
        )
        norm_gain_part += jnp.sum(normed_grad * normal_one[p], axis=0)
        norm_shift_part += jnp.sum(normed_grad, axis=0)
        grad_one = norm_backward(normed_grad, norm_gain, normal_one[p], inverse_one[p])
        out_bias_part += jnp.sum(grad_one, axis=0)
        attended_low = grad_one.astype(BF16)
        grads_one.append(grad_one)
        attended_lows.append(attended_low)
        context_grad = dot_nt(attended_low, whole_out).astype(BF16)
        context_grads.append(
            lax.all_to_all(context_grad, "tensor", split_axis=1, concat_axis=0, tiled=True)
        )
        last = context_grad
        if p == 0:
            last = [down_flow.step(last).sent, glu_flow.step(last).sent]
    shared = jnp.stack(
        [
            out_bias_part,
            norm_gain_part,
            norm_shift_part,
            down_bias_part,
            final_gain_part,
            final_shift_part,
        ]
    )
    glu_bias = jnp.concatenate([gate_bias_part[:, 0], up_bias_part[:, 0]])

    lows, input_grads = [], []
    qkv_bias_part = 0.0
    for p in range(packs):
        low, bias_sum, input_part = attend_backward(
            qkvs[p], after(context_grads[p], last), log_sums[p], *ranges[p], *tables[p], qkv_slabs,
            MIDDLE,
        )
        lows.append(low)
        qkv_bias_part += bias_sum
        input_grads.append(
            scatter_rows(input_part).astype(F32) + scale_value * grads_one[p]
        )
        last = glu_flow.step(low).sent
        if p == 0:
            last = [last, down_flow.settle(low)]
    send, keep = row_grad(
        after(jnp.concatenate(context_rows, axis=0), last),
        jnp.concatenate(attended_lows, axis=0),
        jnp.stack([1 - core, core]).astype(jnp.int32),
        out_weight.shape[0],
    )
    out_flow = Flow(out_scatter_stages(send, keep)).step()
    small_flow = Flow(
        small_stages(
            shared,
            (glu_bias, lambda: qkv_bias_part[:, 0, :]),
            batch_size.bit_length() - 1,
            tensor_size.bit_length() - 1,
        )
    ).step(send)
    last = out_flow.sent
    qkv_blocks = slab_grad(
        whole_tokens, [after(low, last) for low in lows], peer_blocks(batch_rank, batch_size)
    )
    qkv_flow = Flow(direct_sum_stages(qkv_blocks, batch_rank, batch_size, 1)).step()
    last = qkv_flow.sent
    flows = [down_flow, glu_flow, small_flow, out_flow, qkv_flow]
    last = out_flow.step(last).sent
    last = [last, glu_flow.step(last).result]
    for flow in (qkv_flow, out_flow, small_flow):
        last = flow.step(last).sent
    last = [last, down_flow.step(last).result]
    while any(flow.result is None for flow in flows):
        for flow in (out_flow, small_flow, qkv_flow, small_flow, glu_flow, down_flow):
            if flow.result is None:
                flow.step(last)
                if flow.result is None:
                    last = flow.sent
    down_grad, glu_grad, (shared, glu_bias, qkv_bias_grad), out_grad, qkv_grad = [
        flow.result for flow in flows
    ]
    return (
        jnp.stack(outputs),
        jnp.stack(input_grads),
        jnp.transpose(qkv_grad, (1, 0, 2)),
        qkv_bias_grad,
        out_grad,
        shared[0],
        shared[1],
        shared[2],
        glu_grad[0].T,
        glu_bias[:columns],
        glu_grad[1].T,
        glu_bias[columns:],
        down_grad,
        shared[3],
        shared[4],
        shared[5],
    )


def solution(mesh):
    return jax.shard_map(
        functools.partial(per_device, mesh.shape["batch"], mesh.shape["tensor"]),
        mesh=mesh,
        in_specs=(
            P("batch", "tensor", None),
            P("batch", "tensor", None),
            P("batch", None),
            P("batch", None),
            P("batch", None),
            P(),
            P(None, None, "tensor"),
            P(None, "tensor"),
            P("tensor", None),
            P(),
            P(),
            P(),
            P(None, "tensor"),
            P("tensor"),
            P(None, "tensor"),
            P("tensor"),
            P("tensor", None),
            P(),
            P(),
            P(),
        ),
        out_specs=(
            P("batch", "tensor", None),
            P("batch", "tensor", None),
            P(None, None, "tensor"),
            P(None, "tensor"),
            P("tensor", None),
            P(),
            P(),
            P(),
            P(None, "tensor"),
            P("tensor"),
            P(None, "tensor"),
            P("tensor"),
            P("tensor", None),
            P(),
            P(),
            P(),
        ),
        check_vma=False,
    )
```
